32 devices in a mesh: img: 8 (over z, y), band: 4 (over x, core).
Axes of the slice: x: 2, y: 2, z: 4, core: 2. Of those that a mesh axis runs over, the one named last changes fastest.
Arguments:
- image_tokens: bfloat16 [16, 64, 64, 768], P('img', 'band'), may hold values from -6 to 6
- pad_offsets: int32 [16, 2], P('img'), may hold values from 0 to 6
- ln1_gain: bfloat16 [768], P('img'), may hold values from 0.099609375 to 1.8984375
- ln1_bias: bfloat16 [768], P('img'), may hold values from -1.5 to 1.5
- w_qkv: bfloat16 [768, 2304], P('band', 'img'), may hold values from -0.21875 to 0.21875
- q_bias: bfloat16 [768], P('img'), may hold values from -2.5 to 2.5
- v_bias: bfloat16 [768], P('img'), may hold values from -1.5 to 1.5
- rel_rows: bfloat16 [27, 64], P(None, 'band'), may hold values from -0.5 to 0.5
- rel_cols: bfloat16 [27, 64], P(None, 'band'), may hold values from -0.5 to 0.5
- w_proj: bfloat16 [768, 768], P('band', 'img'), may hold values from -1.25 to 1.25
- proj_bias: bfloat16 [768], P('img'), may hold values from -1.5 to 1.5
- ln2_gain: bfloat16 [768], P('img'), may hold values from 0.099609375 to 1.8984375
- ln2_bias: bfloat16 [768], P('img'), may hold values from -1.5 to 1.5
- w_fc1: bfloat16 [768, 3072], P('band', 'img'), may hold values from -0.21875 to 0.21875
- fc1_bias: bfloat16 [3072], P('img'), may hold values from -1.5 to 1.5
- w_fc2: bfloat16 [3072, 768], P('img', 'band'), may hold values from -0.21875 to 0.21875
- fc2_bias: bfloat16 [768], P('img'), may hold values from -1.5 to 1.5
- out_grad: bfloat16 [16, 64, 64, 768], P('img', 'band'), may hold values from -6 to 6
Outputs:
- output: bfloat16 [16, 64, 64, 768], P('img', 'band')
- input_grad: float32 [16, 64, 64, 768], P('img', 'band')
- d_ln1_gain: float32 [768], P('img')
- d_ln1_bias: float32 [768], P('img')
- d_w_qkv: float32 [768, 2304], P('band', 'img')
- d_q_bias: float32 [768], P('img')
- d_v_bias: float32 [768], P('img')
- d_rel_rows: float32 [27, 64], P(None, 'band')
- d_rel_cols: float32 [27, 64], P(None, 'band')
- d_w_proj: float32 [768, 768], P('band', 'img')
- d_proj_bias: float32 [768], P('img')
- d_ln2_gain: float32 [768], P('img')
- d_ln2_bias: float32 [768], P('img')
- d_w_fc1: float32 [768, 3072], P('band', 'img')
- d_fc1_bias: float32 [3072], P('img')
- d_w_fc2: float32 [3072, 768], P('img', 'band')
- d_fc2_bias: float32 [768], P('img')
The draws below stay inside these ranges and needn't reach their ends.
Inputs may be any that keep to these rules, and one draw needn't show every extreme that they name: pad_offsets[b, 0] zero rows lie above image b and pad_offsets[b, 1] zero columns to its left in its 70 x 70 grid.
All inputs are finite; a program needn't handle non-finite values.
Results may differ from the reference program's by a relative error of at most 0.018.
Values may be sent and summed in bfloat16 or wider, within the bound.
A program may use at most 384 MiB of HBM per device.

```python
import jax
import jax.numpy as jnp
from jax import lax

D = 768
HEADS = 12
HEAD = 64
FF = 3072
WIN = 14
SIDE = 64
GRID = 5
PADDED = 70
PAD = 6
WINDOWS = 25
RELS = 27
IMAGES = 16


def set_ends(values, rng, smallest, top_value):
    index_at = [jax.random.randint(jax.random.fold_in(rng, axis), (), 0, length) for axis, length in enumerate(values.shape)]
    longest = values.shape.index(max(values.shape))
    next_to = index_at[:longest] + [(index_at[longest] + 1) % values.shape[longest]] + index_at[longest + 1:]
    return values.at[tuple(index_at)].set(smallest).at[tuple(next_to)].set(top_value)


def block_levels(own_key, shape, cuts, least, largest):
    def one(dim, parts):
        steps = jax.random.uniform(jax.random.fold_in(jax.random.fold_in(own_key, 6), dim), (parts,), jnp.float32, least / len(cuts), largest / len(cuts))
        return jnp.repeat(jnp.exp(steps), shape[dim] // parts).reshape((-1,) + (1,) * (len(shape) - dim - 1))

    level = one(*cuts[0])
    for cut in cuts[1:]:
        level = level * one(*cut)
    return level


def bell_draw(own_key, shape, scale, bound, split=(), held_as=jnp.bfloat16):
    values = scale * jax.random.normal(own_key, shape, jnp.float32)
    if split:
        values = values * block_levels(own_key, shape, split, -0.22, 0.18)
    return jnp.clip(values, -bound, bound).astype(held_as)


def setup_inputs(seed: int = 0) -> dict:
    keys = jax.random.split(jax.random.key(seed), 19)
    return {
        "image_tokens": bell_draw(keys[0], (IMAGES, SIDE, SIDE, D), 1.0, 6.0, ((0, 8), (1, 4))),
        "pad_offsets": set_ends(jax.random.randint(keys[1], (IMAGES, 2), 0, PAD + 1), jax.random.fold_in(keys[1], 1), 0, PAD).astype(jnp.int32),
        "ln1_gain": jnp.clip(1.0 + 0.18 * jax.random.normal(keys[2], (D,), jnp.float32), 0.099609375, 1.8984375).astype(jnp.bfloat16),
        "ln1_bias": bell_draw(keys[3], (D,), 0.3, 1.5, ((0, 8),)),
        "w_qkv": bell_draw(keys[4], (D, 3 * D), D ** -0.5, 0.21875, ((0, 4), (1, 8))),
        "q_bias": bell_draw(keys[5], (D,), 0.5, 2.5, ((0, 8),)),
        "v_bias": bell_draw(keys[6], (D,), 0.3, 1.5, ((0, 8),)),
        "rel_rows": bell_draw(keys[7], (RELS, HEAD), 0.1, 0.5, ((1, 4),)),
        "rel_cols": bell_draw(keys[8], (RELS, HEAD), 0.1, 0.5, ((1, 4),)),
        "w_proj": bell_draw(keys[9], (D, D), (D // 32) ** -0.5, 1.25, ((0, 4), (1, 8))),
        "proj_bias": bell_draw(keys[10], (D,), 0.3, 1.5, ((0, 8),)),
        "ln2_gain": jnp.clip(1.0 + 0.18 * jax.random.normal(keys[11], (D,), jnp.float32), 0.099609375, 1.8984375).astype(jnp.bfloat16),
        "ln2_bias": bell_draw(keys[12], (D,), 0.3, 1.5, ((0, 8),)),
        "w_fc1": bell_draw(keys[13], (D, FF), D ** -0.5, 0.21875, ((0, 4), (1, 8))),
        "fc1_bias": bell_draw(keys[14], (FF,), 0.3, 1.5, ((0, 8),)),
        "w_fc2": bell_draw(keys[15], (FF, D), (FF // 4) ** -0.5, 0.21875, ((0, 8), (1, 4))),
        "fc2_bias": bell_draw(keys[16], (D,), 0.3, 1.5, ((0, 8),)),
        "out_grad": bell_draw(keys[17], (IMAGES, SIDE, SIDE, D), 1.0, 6.0, ((0, 8), (1, 4))),
    }


EPSILON = 1e-06
HIGHEST_PRECISION = lax.Precision.HIGHEST

@jax.custom_vjp
def low(v):
    return lax.optimization_barrier(v.astype(jnp.bfloat16)).astype(jnp.float32)

@jax.custom_vjp
def low_back(v):
    return v

def low_keep(v):
    return (low(v), None)

def low_pass(kept, grad):
    return (grad,)

def back_keep(v):
    return (v, None)

def back_low(kept, grad):
    return (low(grad),)
low.defvjp(low_keep, low_pass)
low_back.defvjp(back_keep, back_low)

def layer_norm(values, gain_row, shift_row):
    average = lax.optimization_barrier(jnp.mean(values, axis=-1, keepdims=True))
    centred = values - average
    variance = lax.optimization_barrier(jnp.mean(centred * centred, axis=-1, keepdims=True))
    return centred * lax.rsqrt(variance + EPSILON) * gain_row + shift_row

def offset_table(table):
    positions = jnp.arange(WIN, dtype=jnp.int32)
    offset_index = positions[:, None] - positions[None, :] + (WIN - 1)
    return table[offset_index]

def window_attention(normed, top_row, left_col, w_qkv, q_bias, v_bias, rel_rows, rel_cols):
    canvas = jnp.zeros((PADDED, PADDED, D), normed.dtype)
    anchor = jnp.zeros((), jnp.int32)
    canvas = lax.dynamic_update_slice(canvas, normed, (top_row, left_col, anchor))
    windows = canvas.reshape(GRID, WIN, GRID, WIN, D).transpose(0, 2, 1, 3, 4).reshape(WINDOWS, WIN * WIN, D)
    bias_row = jnp.concatenate([q_bias, jnp.zeros_like(q_bias), v_bias])
    projected = jnp.einsum('wtd,de->wte', windows, w_qkv, precision=HIGHEST_PRECISION) + bias_row
    queries = low_back(low(projected[..., :D])).reshape(WINDOWS, WIN, WIN, HEADS, HEAD)
    key_rows = low_back(low(projected[..., D:2 * D])).reshape(WINDOWS, WIN * WIN, HEADS, HEAD)
    values = low_back(low(projected[..., 2 * D:])).reshape(WINDOWS, WIN * WIN, HEADS, HEAD)
    flat_queries = queries.reshape(WINDOWS, WIN * WIN, HEADS, HEAD)
    scores = jnp.einsum('wqhc,wkhc->whqk', flat_queries, key_rows, precision=HIGHEST_PRECISION) * HEAD ** (-0.5)
    along_rows = jnp.einsum('wabhc,akc->whabk', queries, offset_table(rel_rows), precision=HIGHEST_PRECISION)
    along_cols = jnp.einsum('wabhc,bkc->whabk', queries, offset_table(rel_cols), precision=HIGHEST_PRECISION)
    scores = scores.reshape(WINDOWS, HEADS, WIN, WIN, WIN, WIN) + along_rows[..., :, None] + along_cols[..., None, :]
    scores = low_back(scores.reshape(WINDOWS, HEADS, WIN * WIN, WIN * WIN))
    attention = low(jax.nn.softmax(scores, axis=-1))
    attended = jnp.einsum('whqk,wkhc->wqhc', attention, values, precision=HIGHEST_PRECISION)
    attended = attended.reshape(GRID, GRID, WIN, WIN, D).transpose(0, 2, 1, 3, 4).reshape(PADDED, PADDED, D)
    cropped = lax.dynamic_slice(attended, (top_row, left_col, anchor), (SIDE, SIDE, D))
    return low_back(low(cropped))

def block(tokens, top_row, left_col, weights):
    gain_one, shift_one, w_qkv, q_bias, v_bias, rel_rows, rel_cols, w_proj, proj_bias, gain_two, shift_two, w_fc1, fc1_bias, w_fc2, fc2_bias = weights
    normed = low_back(low(layer_norm(tokens, gain_one, shift_one)))
    attended = window_attention(normed, top_row, left_col, w_qkv, q_bias, v_bias, rel_rows, rel_cols)
    mixed_rows = low_back(jnp.einsum('ijd,de->ije', attended, w_proj, precision=HIGHEST_PRECISION) + proj_bias)
    hidden = tokens + mixed_rows
    normed_two = low(layer_norm(hidden, gain_two, shift_two))
    pre_act = low_back(jnp.einsum('ijd,df->ijf', normed_two, w_fc1, precision=HIGHEST_PRECISION) + fc1_bias)
    activated = low(jax.nn.gelu(pre_act, approximate=False))
    return hidden + jnp.einsum('ijf,fd->ijd', activated, w_fc2, precision=HIGHEST_PRECISION) + fc2_bias

def reference(image_tokens, pad_offsets, ln1_gain, ln1_bias, w_qkv, q_bias, v_bias, rel_rows, rel_cols, w_proj, proj_bias, ln2_gain, ln2_bias, w_fc1, fc1_bias, w_fc2, fc2_bias, out_grad):
    weights = tuple((item.astype(jnp.float32) for item in (ln1_gain, ln1_bias, w_qkv, q_bias, v_bias, rel_rows, rel_cols, w_proj, proj_bias, ln2_gain, ln2_bias, w_fc1, fc1_bias, w_fc2, fc2_bias)))

    def per_image(totals, item):
        tokens, offsets, cotangent = item

        def run(token_rows, weight_set):
            return block(token_rows, offsets[0], offsets[1], weight_set)
        result, pull_back = jax.vjp(run, tokens.astype(jnp.float32), weights)
        grad_tokens, grad_weights = pull_back(cotangent.astype(jnp.float32))
        totals = jax.tree.map(jnp.add, totals, grad_weights)
        return (totals, (result.astype(jnp.bfloat16), grad_tokens))
    start = jax.tree.map(jnp.zeros_like, weights)
    totals, (output, input_grad) = lax.scan(per_image, start, (image_tokens, pad_offsets, out_grad))
    return (output, input_grad, totals[0], totals[1], totals[2], totals[3], totals[4], totals[5], totals[6], totals[7], totals[8], totals[9], totals[10], totals[11], totals[12], totals[13], totals[14])
```

```python
import functools
import numpy as np
import jax
import jax.numpy as jnp
from jax import lax
from jax.sharding import PartitionSpec as P
from jax.experimental import pallas as pl
from jax.experimental.pallas import tpu as pltpu

D = 768
HEADS = 12
HEAD = 64
FF = 3072
WIN = 14
SIDE = 64
GRID = 5
WINDOWS = 25
RELS = 27
STRIDE = 16
TW = WIN * STRIDE
PAIRS = HEADS // 2
LANES = 128
EPSILON = 1e-06
F32 = jnp.float32
BF16 = jnp.bfloat16
VMEM_LIMIT = 60 * 1024 * 1024
NT = (((1,), (1,)), ((), ()))


def mm(a, b):
    return jnp.dot(a, b, preferred_element_type=F32)


def mm_nt(a, b):
    return lax.dot_general(a, b, NT, preferred_element_type=F32)


def iota(shape, dim):
    return lax.broadcasted_iota(jnp.int32, shape, dim)


def token_target(meta_ref, w):
    t = iota((TW, 1), 0)
    a, b = t >> 4, t & 15
    col = meta_ref[w, 1] + b
    row = meta_ref[w, 2] + a
    ok = (b < WIN) & (col >= 0) & (col < SIDE) & (row >= 0) & (row < SIDE) & (meta_ref[w, 3] > 0)
    return jnp.where(ok, ((a & 3) << 6) + col, -1)


def take_window(target, rows_ref):
    picks = jnp.where(iota((TW, 256), 1) == target, 1.0, 0.0).astype(BF16)
    parts = []
    for q in range(3):
        src = rows_ref[4 * q : 4 * q + 4].reshape(256, D)
        parts.append(mm(picks[64 * q : 64 * q + 64], src))
    src = rows_ref[12:14].reshape(128, D)
    parts.append(mm(picks[192:224, :128], src))
    return jnp.concatenate(parts, axis=0)


def norm(values):
    mean = jnp.sum(values, axis=-1, keepdims=True) * (1.0 / D)
    centred = values - mean
    inverse = lax.rsqrt(jnp.sum(centred * centred, axis=-1, keepdims=True) * (1.0 / D) + EPSILON)
    return centred * inverse, inverse


def norm_back(grad, unit, inverse, gain):
    s = grad * gain
    m1 = jnp.sum(s, axis=-1, keepdims=True) * (1.0 / D)
    m2 = jnp.sum(s * unit, axis=-1, keepdims=True) * (1.0 / D)
    return inverse * (s - m1 - unit * m2)


def fold8(x):
    return jnp.sum(x.reshape(x.shape[0] // 8, 8, x.shape[1]), axis=0)


def roll_rows(x, sign):
    out = []
    for a in range(WIN):
        piece = x[STRIDE * a : STRIDE * a + STRIDE]
        by = (sign * (13 - a)) % LANES
        out.append(pltpu.roll(piece, by, 1) if by else piece)
    return jnp.concatenate(out, axis=0)


def roll_cols(x, first):
    out = []
    for a in range(WIN):
        piece = x[STRIDE * a : STRIDE * a + STRIDE]
        out.append(pltpu.roll(piece, first, 1, stride=1, stride_axis=0))
    return jnp.concatenate(out, axis=0)


def attn_fwd_pair(q, k8, v, table, keys_a, keys_b, p_ref, p):
    lane = iota((TW, LANES), 1)
    low_half = lane < 64
    rc = mm(q, table)
    both = jnp.where((lane & 31) < 16, roll_rows(rc[:, :LANES], -1), roll_cols(rc[:, LANES:], 3))
    high = both.astype(BF16)
    rest = (both - high.astype(F32)).astype(BF16)
    extra = jnp.where((lane & 63) < 32, high, rest)
    extra = jnp.where((lane & 63) == 14, jnp.ones_like(extra), extra)
    left = jnp.concatenate([q, extra], axis=1)
    zero = jnp.zeros_like(k8)
    wide_v = jnp.concatenate([v, jnp.ones_like(v)], axis=1)
    outs, invs = [], []
    for h in range(2):
        keys = jnp.concatenate(
            [jnp.where(low_half if h == 0 else ~low_half, k8, zero), (keys_a, keys_b)[h]], axis=1
        )
        s = mm_nt(left, keys)
        e = jnp.exp(s - jnp.max(s, axis=-1, keepdims=True)).astype(BF16)
        p_ref[2 * p + h] = e
        o = mm(e, wide_v)
        inv = 1.0 / o[:, LANES:]
        outs.append(o[:, :LANES] * inv)
        invs.append(inv)
    att = jnp.where(low_half, outs[0], outs[1]).astype(BF16)
    inv = jnp.where(low_half, invs[0], invs[1])
    return att, inv


def fwd_kernel(
    meta_ref, rows_ref, gain_ref, shift_ref, wqkv_ref, bias_ref, table_ref, ka_ref, kb_ref,
    x_ref, n_ref, qkv_ref, p_ref, inv_ref, att_ref,
):
    w = pl.program_id(0)
    target = token_target(meta_ref, w)
    x = take_window(target, rows_ref)
    x_ref[...] = x.astype(BF16)
    unit, _ = norm(x)
    normed = jnp.where(target >= 0, unit * gain_ref[...] + shift_ref[...], 0.0).astype(BF16)
    n_ref[...] = normed
    for c in range(9):
        cols = slice(256 * c, 256 * c + 256)
        y = mm(normed, wqkv_ref[:, cols]) + bias_ref[:, cols]
        if 3 <= c < 6:
            y = y.astype(BF16).astype(F32) * 0.125
        qkv_ref[:, cols] = y.astype(BF16)

    for p in range(PAIRS):
        a = slice(LANES * p, LANES * p + LANES)
        q = qkv_ref[:, LANES * p : LANES * p + LANES]
        k8 = qkv_ref[:, D + LANES * p : D + LANES * p + LANES]
        v = qkv_ref[:, 2 * D + LANES * p : 2 * D + LANES * p + LANES]
        att, inv = attn_fwd_pair(q, k8, v, table_ref[...], ka_ref[...], kb_ref[...], p_ref, p)
        att_ref[:, a] = att
        inv_ref[:, a] = inv


def rows_spec(rows):
    return pl.BlockSpec(
        (pl.Element(rows), pl.Element(SIDE), pl.Element(D)), lambda w, meta: (meta[w, 0], 0, 0)
    )


def whole(shape, buffers=1):
    zeros = (0,) * len(shape)
    return pl.BlockSpec(shape, lambda w, meta: zeros, pipeline_mode=pl.Buffered(buffers))


def per_window(*tail):
    zeros = (0,) * len(tail)
    return pl.BlockSpec((None,) + tail, lambda w, meta: (w,) + zeros)


def key_constants():
    t = np.arange(TW)
    kr, kc = t >> 4, t & 15
    real = kc < WIN
    base = np.zeros((TW, 64), np.float32)
    for off in (0, 32):
        base[t[real], off + kr[real]] = 1.0
        base[t[real], off + 16 + kc[real]] = 1.0
    back = np.zeros_like(base)
    back[t[real], kr[real]] = 1.0
    back[t[real], 16 + 13 - kc[real]] = 1.0
    base[~real, 14] = -1e30
    none = np.zeros_like(base)
    ka = np.concatenate([base, none], 1)
    kb = np.concatenate([none, base], 1)
    back = np.concatenate([back, back], 1)
    return jnp.asarray(ka, BF16), jnp.asarray(kb, BF16), jnp.asarray(back, BF16)


def rel_table(rel_rows, rel_cols, forward):
    def wide(rel):
        turned = jnp.pad(rel.T, ((0, 0), (0, 32 - RELS)))
        twice = jnp.concatenate([turned, turned], axis=1)
        none = jnp.zeros_like(twice)
        return jnp.concatenate(
            [jnp.concatenate([twice, none], 1), jnp.concatenate([none, twice], 1)], 0
        )

    return jnp.concatenate([wide(rel_rows[::-1]), wide(rel_cols[::-1] if forward else rel_cols)], axis=1)


def attention_forward(meta, ext, gain, shift, wqkv, bias, table, ka, kb):
    cap = meta.shape[0]
    sds = jax.ShapeDtypeStruct
    return pl.pallas_call(
        fwd_kernel,
        grid_spec=pltpu.PrefetchScalarGridSpec(
            num_scalar_prefetch=1,
            grid=(cap,),
            in_specs=[
                rows_spec(WIN), whole((1, D)), whole((1, D)), whole((D, 3 * D)), whole((1, 3 * D)),
                whole((LANES, 256)), whole((TW, LANES)), whole((TW, LANES)),
            ],
            out_specs=[
                per_window(TW, D), per_window(TW, D), per_window(TW, 3 * D),
                per_window(HEADS, TW, TW), per_window(TW, D), per_window(TW, D),
            ],
        ),
        out_shape=[
            sds((cap, TW, D), BF16), sds((cap, TW, D), BF16), sds((cap, TW, 3 * D), BF16),
            sds((cap, HEADS, TW, TW), BF16), sds((cap, TW, D), F32), sds((cap, TW, D), BF16),
        ],
        compiler_params=pltpu.CompilerParams(vmem_limit_bytes=VMEM_LIMIT),
        cost_estimate=pl.CostEstimate(flops=40_000_000_000, bytes_accessed=80_000_000, transcendentals=8_000_000),
    )(meta, ext, gain, shift, wqkv, bias, table, ka, kb)


def phi_parts(u):
    e = jnp.exp(u * u * -0.5)
    t = 1.0 / (1.0 + (0.3275911 * 0.7071067811865476) * jnp.abs(u))
    poly = t * (0.254829592 + t * (-0.284496736 + t * (1.421413741 + t * (-1.453152027 + t * 1.061405429))))
    tail = 0.5 * poly * e
    return jnp.where(u >= 0, 1.0 - tail, tail), e * 0.3989422804014327


def mlp_kernel(
    meta_ref, grows_ref, x_ref, att_ref, wproj_ref, pbias_ref, gain_ref, shift_ref, ff_ref, b1_ref, b2_ref,
    out_ref, g_ref, n2_ref, act_ref, dpre_ref, dmix_ref, datt_ref, sums_ref, sum1_ref,
    acc_ref, dn_ref,
):
    w = pl.program_id(0)

    @pl.when(w == 0)
    def _():
        sums_ref[...] = jnp.zeros_like(sums_ref)
        sum1_ref[...] = jnp.zeros_like(sum1_ref)

    target = token_target(meta_ref, w)
    g = take_window(target, grows_ref)
    gb = g.astype(BF16)
    g_ref[...] = gb
    sums_ref[0] += fold8(g)
    hidden = x_ref[...].astype(F32) + mm(att_ref[...], wproj_ref[...]) + pbias_ref[...]
    unit, inverse = norm(hidden)
    n2 = (unit * gain_ref[...] + shift_ref[...]).astype(BF16)
    n2_ref[...] = n2
    acc_ref[...] = hidden + b2_ref[...]
    parts, chunk = ff_ref.shape[0], ff_ref.shape[2] // 2
    for c in range(parts):
        cols = slice(chunk * c, chunk * c + chunk)
        w1, w2t = ff_ref[c, :, :chunk], ff_ref[c, :, chunk:]
        u = mm(n2, w1) + b1_ref[:, cols]
        dact = mm(gb, w2t)
        cdf, pdf = phi_parts(u)
        act = (u * cdf).astype(BF16)
        act_ref[:, cols] = act
        acc_ref[...] += mm_nt(act, w2t)
        dpre32 = dact * (cdf + u * pdf)
        dpre = dpre32.astype(BF16)
        dpre_ref[:, cols] = dpre
        sum1_ref[:, cols] += fold8(dpre32)
        step = mm_nt(dpre, w1)
        if c == 0:
            dn_ref[...] = step
        else:
            dn_ref[...] += step
    out_ref[...] = acc_ref[...].astype(BF16)
    dn = dn_ref[...]
    sums_ref[1] += fold8(dn * unit)
    sums_ref[2] += fold8(dn)
    dh = g + norm_back(dn, unit, inverse, gain_ref[...])
    dmix = dh.astype(BF16)
    dmix_ref[...] = dmix
    sums_ref[3] += fold8(dh)
    datt_ref[...] = mm_nt(dmix, wproj_ref[...]).astype(BF16)


def feed_forward(meta, gext, x, att, wproj, pbias, gain, shift, ff, b1, b2):
    cap = meta.shape[0]
    sds = jax.ShapeDtypeStruct
    return pl.pallas_call(
        mlp_kernel,
        grid_spec=pltpu.PrefetchScalarGridSpec(
            num_scalar_prefetch=1,
            grid=(cap,),
            in_specs=[
                rows_spec(WIN), per_window(TW, D), per_window(TW, D), whole((D, D)), whole((1, D)), whole((1, D)),
                whole((1, D)), whole(ff.shape), whole((1, FF)), whole((1, D)),
            ],
            out_specs=[
                per_window(TW, D), per_window(TW, D), per_window(TW, D), per_window(TW, FF), per_window(TW, FF),
                per_window(TW, D), per_window(TW, D), whole((4, 8, D)), whole((8, FF)),
            ],
            scratch_shapes=[pltpu.VMEM((TW, D), F32), pltpu.VMEM((TW, D), F32)],
        ),
        out_shape=[
            sds((cap, TW, D), BF16), sds((cap, TW, D), BF16), sds((cap, TW, D), BF16), sds((cap, TW, FF), BF16),
            sds((cap, TW, FF), BF16), sds((cap, TW, D), BF16), sds((cap, TW, D), BF16), sds((4, 8, D), F32),
            sds((8, FF), F32),
        ],
        compiler_params=pltpu.CompilerParams(vmem_limit_bytes=VMEM_LIMIT),
        cost_estimate=pl.CostEstimate(flops=60_000_000_000, bytes_accessed=80_000_000, transcendentals=8_000_000),
    )(meta, gext, x, att, wproj, pbias, gain, shift, ff, b1, b2)


def attn_bwd_kernel(
    meta_ref, qkv_ref, p_ref, inv_ref, att_ref, datt_ref, table_ref, kback_ref,
    dqkv_ref, rel_ref, bias_ref,
):
    w = pl.program_id(0)

    @pl.when(w == 0)
    def _():
        rel_ref[...] = jnp.zeros_like(rel_ref)
        bias_ref[...] = jnp.zeros_like(bias_ref)

    lane = iota((TW, LANES), 1)
    low_half = lane < 64
    onehot = kback_ref[...]
    for p in range(PAIRS):
        q = qkv_ref[:, LANES * p : LANES * p + LANES]
        k8 = qkv_ref[:, D + LANES * p : D + LANES * p + LANES]
        v = qkv_ref[:, 2 * D + LANES * p : 2 * D + LANES * p + LANES]
        cols = slice(LANES * p, LANES * p + LANES)
        da = datt_ref[:, cols].astype(F32) * inv_ref[:, cols]
        da_low = da.astype(BF16)
        prod = da_low.astype(F32) * att_ref[:, cols].astype(F32)
        keys = jnp.concatenate([k8, onehot], axis=1)
        da_t = da.T.astype(BF16)
        q_t = q.astype(F32).T.astype(BF16)
        zero = jnp.zeros_like(v)
        dqx, dv_t, dk_t = [], [], []
        for h in range(2):
            mine = low_half if h == 0 else ~low_half
            centre = jnp.sum(jnp.where(mine, prod, 0.0), axis=-1, keepdims=True)
            dp = mm_nt(da_low, jnp.where(mine, v, zero))
            e = p_ref[2 * p + h]
            ds = (e.astype(F32) * (dp - centre)).astype(BF16)
            dqx.append(mm(ds, keys))
            dv_t.append(mm(da_t[64 * h : 64 * h + 64], e))
            dk_t.append(mm(q_t[64 * h : 64 * h + 64], ds))
        dq = jnp.where(low_half, dqx[0][:, :LANES], dqx[1][:, :LANES])
        drc = jnp.where(low_half, dqx[0][:, LANES:], dqx[1][:, LANES:])
        part = lane & 63
        rows = roll_rows(jnp.where(part < 16, drc, 0.0), 1)
        cols_part = roll_cols(jnp.where((part >= 16) & (part < 32), drc, 0.0), LANES - 16)
        skew = jnp.concatenate([rows, cols_part], axis=1).astype(BF16)
        dq = dq + mm_nt(skew, table_ref[...])
        rel_ref[...] += mm(q_t, skew)
        dv = jnp.concatenate(dv_t, axis=0).T
        dk = (jnp.concatenate(dk_t, axis=0) * 0.125).T
        dqkv_ref[:, cols] = dq.astype(BF16)
        dqkv_ref[:, D + LANES * p : D + LANES * p + LANES] = dk.astype(BF16)
        dqkv_ref[:, 2 * D + LANES * p : 2 * D + LANES * p + LANES] = dv.astype(BF16)
        bias_ref[0, :, cols] += fold8(dq)
        bias_ref[1, :, cols] += fold8(dv)


def attention_backward(meta, qkv, p, inv, att, datt, table, kback):
    cap = meta.shape[0]
    sds = jax.ShapeDtypeStruct
    return pl.pallas_call(
        attn_bwd_kernel,
        grid_spec=pltpu.PrefetchScalarGridSpec(
            num_scalar_prefetch=1,
            grid=(cap,),
            in_specs=[
                per_window(TW, 3 * D), per_window(HEADS, TW, TW), per_window(TW, D), per_window(TW, D),
                per_window(TW, D), whole((LANES, 256)), whole((TW, LANES)),
            ],
            out_specs=[per_window(TW, 3 * D), whole((LANES, 256)), whole((2, 8, D))],
        ),
        out_shape=[sds((cap, TW, 3 * D), BF16), sds((LANES, 256), F32), sds((2, 8, D), F32)],
        compiler_params=pltpu.CompilerParams(vmem_limit_bytes=VMEM_LIMIT),
        cost_estimate=pl.CostEstimate(flops=60_000_000_000, bytes_accessed=80_000_000, transcendentals=0),
    )(meta, qkv, p, inv, att, datt, table, kback)


def rel_from(acc):
    def one(block):
        own = block[:64, :32] + block[64:, 64:96]
        return own[:, :RELS].T

    return one(acc[:, :LANES])[::-1], one(acc[:, LANES:])


def put_window(target, y, acc_ref, row0):
    picks = jnp.where(iota((TW, 256), 1) == target, 1.0, 0.0).astype(BF16)
    for q in range(4):
        n = 4 if q < 3 else 2
        t = slice(64 * q, 64 * q + STRIDE * n)
        part = lax.dot_general(
            picks[t, : 64 * n], y[t], (((0,), (0,)), ((), ())), preferred_element_type=F32
        )
        acc_ref[pl.ds(row0 + 4 * q, n)] += part.reshape(n, SIDE, D)


def scatter_kernel(meta_ref, y_ref, ext_ref, acc_ref):
    w = pl.program_id(0)

    @pl.when(w == 0)
    def _():
        acc_ref[...] = jnp.zeros_like(acc_ref)

    put_window(token_target(meta_ref, w), y_ref[...], acc_ref, meta_ref[w, 0])

    @pl.when(w == pl.num_programs(0) - 1)
    def _():
        def copy(i, _):
            ext_ref[i] = acc_ref[i].astype(BF16)
            return 0
        lax.fori_loop(0, ext_ref.shape[0], copy, 0)


def scatter(meta, y, ext_rows):
    cap = meta.shape[0]
    return pl.pallas_call(
        scatter_kernel,
        grid_spec=pltpu.PrefetchScalarGridSpec(
            num_scalar_prefetch=1,
            grid=(cap,),
            in_specs=[per_window(TW, D)],
            out_specs=whole((ext_rows, SIDE, D)),
            scratch_shapes=[pltpu.VMEM((ext_rows, SIDE, D), F32)],
        ),
        out_shape=jax.ShapeDtypeStruct((ext_rows, SIDE, D), BF16),
        compiler_params=pltpu.CompilerParams(vmem_limit_bytes=VMEM_LIMIT),
        cost_estimate=pl.CostEstimate(flops=5_000_000_000, bytes_accessed=20_000_000, transcendentals=0),
    )(meta, y)


def last_kernel(
    meta_ref, dqkv_ref, wqkv_ref, x_ref, dmix_ref, gain_ref, ext_ref, sums_ref, acc_ref,
):
    w = pl.program_id(0)

    @pl.when(w == 0)
    def _():
        acc_ref[...] = jnp.zeros_like(acc_ref)
        sums_ref[...] = jnp.zeros_like(sums_ref)

    target = token_target(meta_ref, w)
    dn = jnp.zeros((TW, D), F32)
    for c in range(3):
        cols = slice(D * c, D * c + D)
        dn = dn + mm_nt(dqkv_ref[:, cols], wqkv_ref[:, cols])
    dn = jnp.where(target >= 0, dn, 0.0)
    unit, inverse = norm(x_ref[...].astype(F32))
    sums_ref[0] += fold8(dn * unit)
    sums_ref[1] += fold8(dn)
    grad = dmix_ref[...].astype(F32) + norm_back(dn, unit, inverse, gain_ref[...])
    put_window(target, grad.astype(BF16), acc_ref, meta_ref[w, 0])

    @pl.when(w == pl.num_programs(0) - 1)
    def _():
        def copy(i, _):
            ext_ref[i] = acc_ref[i].astype(BF16)
            return 0
        lax.fori_loop(0, ext_ref.shape[0], copy, 0)


def last_norm(meta, dqkv, wqkv, x, dmix, gain, ext_rows):
    cap = meta.shape[0]
    sds = jax.ShapeDtypeStruct
    return pl.pallas_call(
        last_kernel,
        grid_spec=pltpu.PrefetchScalarGridSpec(
            num_scalar_prefetch=1,
            grid=(cap,),
            in_specs=[
                per_window(TW, 3 * D), whole((D, 3 * D)), per_window(TW, D), per_window(TW, D), whole((1, D)),
            ],
            out_specs=[whole((ext_rows, SIDE, D)), whole((2, 8, D))],
            scratch_shapes=[pltpu.VMEM((ext_rows, SIDE, D), F32)],
        ),
        out_shape=[sds((ext_rows, SIDE, D), BF16), sds((2, 8, D), F32)],
        compiler_params=pltpu.CompilerParams(vmem_limit_bytes=VMEM_LIMIT),
        cost_estimate=pl.CostEstimate(flops=15_000_000_000, bytes_accessed=30_000_000, transcendentals=0),
    )(meta, dqkv, wqkv, x, dmix, gain)


def window_plan(images, bands):
    lists = [[] for _ in range(bands)]
    if images == 2 and bands == 4:
        cuts = ((0, 8, 15, 20, 25), (0, 5, 10, 17, 25))
    else:
        cuts = [
            [(WINDOWS * b + (bands - 1 if m % 2 else 0)) // bands for b in range(bands + 1)] for m in range(images)
        ]
    for m in range(images):
        for b in range(bands):
            lists[b] += [(m, w) for w in range(cuts[m][b], min(cuts[m][b + 1], WINDOWS))]
    cap = max(len(item) for item in lists)
    return np.array([item + [(0, -1)] * (cap - len(item)) for item in lists], np.int32)


HALO = 12


def near(images, bands, band_rows):
    return images == 2 and bands == 4 and band_rows == 16


CORE = [(0, 1), (1, 0), (2, 3), (3, 2)]
CROSS = [(1, 2), (2, 1)]


def extend(rows, band):
    images, band_rows = rows.shape[:2]
    if not near(images, lax.axis_size("band"), band_rows):
        full = lax.all_gather(rows, "band", axis=1, tiled=True)
        return jnp.pad(full, ((0, 0), (6, 6), (0, 0), (0, 0)))
    odd = band % 2 == 1
    top, bottom = rows[:, :HALO], rows[:, -HALO:]
    from_core = lax.ppermute(jnp.where(odd, top, bottom), "band", CORE)
    from_cross = lax.ppermute(jnp.where(odd, bottom[1], top[0]), "band", CROSS)
    zero = jnp.zeros_like(from_cross)
    above = jnp.where(odd, from_core, jnp.stack([zero, from_cross]))
    below = jnp.where(odd, jnp.stack([from_cross, zero]), from_core)
    return jnp.concatenate([above, rows, below], axis=1)


def collect(ext, band, images, band_rows):
    if not near(images, lax.axis_size("band"), band_rows):
        return lax.psum_scatter(ext[:, 6:-6], "band", scatter_dimension=1, tiled=True).astype(F32)
    odd = band % 2 == 1
    above, below = ext[:, :HALO], ext[:, -HALO:]
    from_core = lax.ppermute(jnp.where(odd, above, below), "band", CORE).astype(F32)
    from_cross = lax.ppermute(jnp.where(odd, below[0], above[1]), "band", CROSS).astype(F32)
    zero = jnp.zeros_like(from_cross)
    top = jnp.where(odd, from_core, jnp.stack([from_cross, zero]))
    bottom = jnp.where(odd, jnp.stack([zero, from_cross]), from_core)
    own = ext[:, HALO:-HALO].astype(F32)
    rest = band_rows - HALO
    return own + jnp.pad(top, ((0, 0), (0, rest), (0, 0), (0, 0))) + jnp.pad(bottom, ((0, 0), (rest, 0), (0, 0), (0, 0)))


def shards(
    image_tokens, pad_offsets, ln1_gain, ln1_bias, w_qkv, q_bias, v_bias, rel_rows, rel_cols, w_proj, proj_bias,
    ln2_gain, ln2_bias, w_fc1, fc1_bias, w_fc2, fc2_bias, out_grad,
):
    images, band_rows = image_tokens.shape[:2]
    bands, groups = lax.axis_size("band"), lax.axis_size("img")
    band, group = lax.axis_index("band"), lax.axis_index("img")
    axes = ("img", "band")

    part, wide = w_qkv.shape
    small = jnp.concatenate(
        [
            ln1_gain, ln1_bias, q_bias, v_bias, proj_bias, ln2_gain, ln2_bias, fc2_bias, fc1_bias,
            rel_rows.reshape(-1), rel_cols.reshape(-1),
        ]
    )
    small_rows = -(-small.shape[0] // (wide * 8)) * 8
    small = jnp.pad(small, (0, small_rows * wide - small.shape[0])).reshape(small_rows, wide)
    first = lax.all_gather(jnp.concatenate([w_qkv, small], axis=0), axes, axis=0, tiled=False)
    first = first.reshape(groups, bands, part + small_rows, wide)
    second = lax.all_gather(
        jnp.concatenate([w_fc1, w_fc2.T, w_proj], axis=1), axes, axis=0, tiled=False
    ).reshape(groups, bands * part, -1)
    wqkv = first[:, :, :part].transpose(1, 2, 0, 3).reshape(D, 3 * D)
    tail = first[:, :, part:].reshape(groups, bands, small_rows * wide)
    share = D // groups
    vectors = tail[:, 0, : 8 * share].reshape(groups, 8, share).transpose(1, 0, 2).reshape(8, 1, D).astype(F32)
    fc1_shift = tail[:, 0, 8 * share : 8 * share + FF // groups].reshape(1, FF).astype(F32)
    at = 8 * share + FF // groups
    rels = tail[0, :, at : at + 2 * RELS * (HEAD // bands)].reshape(bands, 2, RELS, HEAD // bands)
    rels = rels.transpose(1, 2, 0, 3).reshape(2, RELS, HEAD)
    gain1, shift1, qb, vb, pb, gain2, shift2, b2 = [vectors[i] for i in range(8)]
    bias = jnp.concatenate([qb, jnp.zeros_like(qb), vb], axis=1)
    inner = FF // groups
    ff = second[:, :, : 2 * inner]
    wproj = second[:, :, 2 * inner :].transpose(1, 0, 2).reshape(D, D)

    plan = jnp.asarray(window_plan(images, bands))[band]
    image, window = plan[:, 0], plan[:, 1]
    close = near(images, bands, band_rows)
    ext_per = band_rows + 2 * HALO if close else bands * band_rows + 12
    base = band_rows * band - HALO if close else -6
    live = window >= 0
    spot = jnp.maximum(window, 0)
    offsets = pad_offsets[image]
    row = spot // GRID * WIN - offsets[:, 0]
    col = spot % GRID * WIN - offsets[:, 1]
    meta = jnp.stack(
        [jnp.where(live, image * ext_per + row - base, 0), col, row, live.astype(jnp.int32)], axis=1
    ).astype(jnp.int32)
    cap = meta.shape[0]
    ext_rows = images * ext_per

    ka, kb, kback = key_constants()
    ext = extend(image_tokens, band).reshape(ext_rows, SIDE, D)
    x, normed1, qkv, probs, inv, att = attention_forward(
        meta, ext, gain1, shift1, wqkv, bias, rel_table(rels[0], rels[1], True), ka, kb
    )
    gext = extend(out_grad, band).reshape(ext_rows, SIDE, D)
    out_win, g, normed2, act, d_pre, d_mixed, d_att, sums, sum_fc1 = feed_forward(
        meta, gext, x, att, wproj, pb, gain2, shift2, ff, fc1_shift, b2
    )
    out_ext = scatter(meta, out_win, ext_rows).reshape(images, ext_per, SIDE, D)
    output = collect(out_ext, band, images, band_rows).astype(BF16)

    def flat(a):
        return a.reshape(cap * TW, a.shape[-1])

    def weight_grad(left, right):
        return jnp.einsum("td,te->de", flat(left), flat(right), preferred_element_type=F32).astype(BF16)

    d_fc1 = weight_grad(normed2, d_pre)
    d_fc2 = weight_grad(act, g)
    d_proj = weight_grad(att, d_mixed)
    d_qkv, rel_acc, bias_sums = attention_backward(
        meta, qkv, probs, inv, att, d_att, rel_table(rels[0], rels[1], False), kback
    )
    d_wqkv = weight_grad(normed1, d_qkv)
    in_ext, sums1 = last_norm(meta, d_qkv, wqkv, x, d_mixed, gain1, ext_rows)
    input_grad = collect(in_ext.reshape(images, ext_per, SIDE, D), band, images, band_rows)

    def reduce(grad, rows_axis, cols_axis):
        grad = lax.psum_scatter(grad, cols_axis, scatter_dimension=1, tiled=True)
        return lax.psum_scatter(grad, rows_axis, scatter_dimension=0, tiled=True).astype(F32)

    d_rel_rows, d_rel_cols = rel_from(rel_acc)
    total = lax.psum(
        (jnp.sum(sums1, 1), jnp.sum(bias_sums, 1), jnp.sum(sums, 1), jnp.sum(sum_fc1, 0), d_rel_rows, d_rel_cols), axes
    )

    def img_share(vector):
        n = vector.shape[0] // groups
        return lax.dynamic_slice_in_dim(vector, group * n, n, 0)

    def band_share(table):
        n = table.shape[1] // bands
        return lax.dynamic_slice_in_dim(table, band * n, n, 1)

    return (
        output,
        input_grad,
        img_share(total[0][0]),
        img_share(total[0][1]),
        reduce(d_wqkv, "band", "img"),
        img_share(total[1][0]),
        img_share(total[1][1]),
        band_share(total[4]),
        band_share(total[5]),
        reduce(d_proj, "band", "img"),
        img_share(total[2][3]),
        img_share(total[2][1]),
        img_share(total[2][2]),
        reduce(d_fc1, "band", "img"),
        img_share(total[3]),
        reduce(d_fc2, "img", "band"),
        img_share(total[2][0]),
    )


def solution(mesh):
    tokens, vector, matrix = P("img", "band", None, None), P("img"), P("band", "img")
    table, wide = P(None, "band"), P("img", "band")
    return jax.shard_map(
        shards,
        mesh=mesh,
        in_specs=(
            tokens, P("img", None), vector, vector, matrix, vector, vector, table, table, matrix, vector, vector,
            vector, matrix, vector, wide, vector, tokens,
        ),
        out_specs=(
            tokens, tokens, vector, vector, matrix, vector, vector, table, table, matrix, vector, vector, vector,
            matrix, vector, wide, vector,
        ),
        check_vma=False,
    )
```

```python
import functools
import numpy as np
import jax
import jax.numpy as jnp
from jax import lax
from jax.sharding import PartitionSpec as P
from jax.experimental import pallas as pl
from jax.experimental.pallas import tpu as pltpu

D = 768
HEADS = 12
HEAD = 64
FF = 3072
WIN = 14
SIDE = 64
GRID = 5
WINDOWS = 25
RELS = 27
STRIDE = 16
TW = WIN * STRIDE
PAIRS = HEADS // 2
LANES = 128
EPSILON = 1e-06
F32 = jnp.float32
BF16 = jnp.bfloat16
VMEM_LIMIT = 60 * 1024 * 1024
NT = (((1,), (1,)), ((), ()))


def mm(a, b):
    return jnp.dot(a, b, preferred_element_type=F32)


def mm_nt(a, b):
    return lax.dot_general(a, b, NT, preferred_element_type=F32)


def iota(shape, dim):
    return lax.broadcasted_iota(jnp.int32, shape, dim)


def token_target(meta_ref, w):
    t = iota((TW, 1), 0)
    a, b = t >> 4, t & 15
    col = meta_ref[w, 1] + b
    row = meta_ref[w, 2] + a
    ok = (b < WIN) & (col >= 0) & (col < SIDE) & (row >= 0) & (row < SIDE) & (meta_ref[w, 3] > 0)
    return jnp.where(ok, ((a & 3) << 6) + col, -1)


def take_window(target, rows_ref):
    picks = jnp.where(iota((TW, 256), 1) == target, 1.0, 0.0).astype(BF16)
    parts = []
    for q in range(3):
        src = rows_ref[4 * q : 4 * q + 4].reshape(256, D)
        parts.append(mm(picks[64 * q : 64 * q + 64], src))
    src = rows_ref[12:14].reshape(128, D)
    parts.append(mm(picks[192:224, :128], src))
    return jnp.concatenate(parts, axis=0)


def norm(values):
    mean = jnp.sum(values, axis=-1, keepdims=True) * (1.0 / D)
    centred = values - mean
    inverse = lax.rsqrt(jnp.sum(centred * centred, axis=-1, keepdims=True) * (1.0 / D) + EPSILON)
    return centred * inverse, inverse


def norm_back(grad, unit, inverse, gain):
    s = grad * gain
    m1 = jnp.sum(s, axis=-1, keepdims=True) * (1.0 / D)
    m2 = jnp.sum(s * unit, axis=-1, keepdims=True) * (1.0 / D)
    return inverse * (s - m1 - unit * m2)


def fold8(x):
    return jnp.sum(x.reshape(x.shape[0] // 8, 8, x.shape[1]), axis=0)


def roll_rows(x, sign):
    out = []
    for a in range(WIN):
        piece = x[STRIDE * a : STRIDE * a + STRIDE]
        by = (sign * (13 - a)) % LANES
        out.append(pltpu.roll(piece, by, 1) if by else piece)
    return jnp.concatenate(out, axis=0)


def roll_cols(x, first):
    out = []
    for a in range(WIN):
        piece = x[STRIDE * a : STRIDE * a + STRIDE]
        out.append(pltpu.roll(piece, first, 1, stride=1, stride_axis=0))
    return jnp.concatenate(out, axis=0)


def attn_fwd_pair(q, k8, v, table, keys_a, keys_b, p_ref, p):
    lane = iota((TW, LANES), 1)
    low_half = lane < 64
    rc = mm(q, table)
    both = jnp.where((lane & 31) < 16, roll_rows(rc[:, :LANES], -1), roll_cols(rc[:, LANES:], 3))
    high = both.astype(BF16)
    rest = (both - high.astype(F32)).astype(BF16)
    extra = jnp.where((lane & 63) < 32, high, rest)
    extra = jnp.where((lane & 63) == 14, jnp.ones_like(extra), extra)
    left = jnp.concatenate([q, extra], axis=1)
    zero = jnp.zeros_like(k8)
    wide_v = jnp.concatenate([v, jnp.ones_like(v)], axis=1)
    outs, invs = [], []
    for h in range(2):
        keys = jnp.concatenate(
            [jnp.where(low_half if h == 0 else ~low_half, k8, zero), (keys_a, keys_b)[h]], axis=1
        )
        s = mm_nt(left, keys)
        e = jnp.exp(s - jnp.max(s, axis=-1, keepdims=True)).astype(BF16)
        p_ref[2 * p + h] = e
        o = mm(e, wide_v)
        inv = 1.0 / o[:, LANES:]
        outs.append(o[:, :LANES] * inv)
        invs.append(inv)
    att = jnp.where(low_half, outs[0], outs[1]).astype(BF16)
    inv = jnp.where(low_half, invs[0], invs[1])
    return att, inv


def fwd_kernel(
    meta_ref, rows_ref, gain_ref, shift_ref, wqkv_ref, bias_ref, table_ref, ka_ref, kb_ref,
    x_ref, n_ref, qkv_ref, p_ref, inv_ref, att_ref,
):
    w = pl.program_id(0)
    target = token_target(meta_ref, w)
    x = take_window(target, rows_ref)
    x_ref[...] = x.astype(BF16)
    unit, _ = norm(x)
    normed = jnp.where(target >= 0, unit * gain_ref[...] + shift_ref[...], 0.0).astype(BF16)
    n_ref[...] = normed
    for c in range(9):
        cols = slice(256 * c, 256 * c + 256)
        y = mm(normed, wqkv_ref[:, cols]) + bias_ref[:, cols]
        if 3 <= c < 6:
            y = y.astype(BF16).astype(F32) * 0.125
        qkv_ref[:, cols] = y.astype(BF16)

    for p in range(PAIRS):
        a = slice(LANES * p, LANES * p + LANES)
        q = qkv_ref[:, LANES * p : LANES * p + LANES]
        k8 = qkv_ref[:, D + LANES * p : D + LANES * p + LANES]
        v = qkv_ref[:, 2 * D + LANES * p : 2 * D + LANES * p + LANES]
        att, inv = attn_fwd_pair(q, k8, v, table_ref[...], ka_ref[...], kb_ref[...], p_ref, p)
        att_ref[:, a] = att
        inv_ref[:, a] = inv


def rows_spec(rows):
    return pl.BlockSpec(
        (pl.Element(rows), pl.Element(SIDE), pl.Element(D)), lambda w, meta: (meta[w, 0], 0, 0)
    )


def whole(shape, buffers=1):
    zeros = (0,) * len(shape)
    return pl.BlockSpec(shape, lambda w, meta: zeros, pipeline_mode=pl.Buffered(buffers))


def per_window(*tail):
    zeros = (0,) * len(tail)
    return pl.BlockSpec((None,) + tail, lambda w, meta: (w,) + zeros)


def key_constants():
    t = np.arange(TW)
    kr, kc = t >> 4, t & 15
    real = kc < WIN
    base = np.zeros((TW, 64), np.float32)
    for off in (0, 32):
        base[t[real], off + kr[real]] = 1.0
        base[t[real], off + 16 + kc[real]] = 1.0
    back = np.zeros_like(base)
    back[t[real], kr[real]] = 1.0
    back[t[real], 16 + 13 - kc[real]] = 1.0
    base[~real, 14] = -1e30
    none = np.zeros_like(base)
    ka = np.concatenate([base, none], 1)
    kb = np.concatenate([none, base], 1)
    back = np.concatenate([back, back], 1)
    return jnp.asarray(ka, BF16), jnp.asarray(kb, BF16), jnp.asarray(back, BF16)


def rel_table(rel_rows, rel_cols, forward):
    def wide(rel):
        turned = jnp.pad(rel.T, ((0, 0), (0, 32 - RELS)))
        twice = jnp.concatenate([turned, turned], axis=1)
        none = jnp.zeros_like(twice)
        return jnp.concatenate(
            [jnp.concatenate([twice, none], 1), jnp.concatenate([none, twice], 1)], 0
        )

    return jnp.concatenate([wide(rel_rows[::-1]), wide(rel_cols[::-1] if forward else rel_cols)], axis=1)


def attention_forward(meta, ext, gain, shift, wqkv, bias, table, ka, kb):
    cap = meta.shape[0]
    sds = jax.ShapeDtypeStruct
    return pl.pallas_call(
        fwd_kernel,
        grid_spec=pltpu.PrefetchScalarGridSpec(
            num_scalar_prefetch=1,
            grid=(cap,),
            in_specs=[
                rows_spec(WIN), whole((1, D)), whole((1, D)), whole((D, 3 * D)), whole((1, 3 * D)),
                whole((LANES, 256)), whole((TW, LANES)), whole((TW, LANES)),
            ],
            out_specs=[
                per_window(TW, D), per_window(TW, D), per_window(TW, 3 * D),
                per_window(HEADS, TW, TW), per_window(TW, D), per_window(TW, D),
            ],
        ),
        out_shape=[
            sds((cap, TW, D), BF16), sds((cap, TW, D), BF16), sds((cap, TW, 3 * D), BF16),
            sds((cap, HEADS, TW, TW), BF16), sds((cap, TW, D), F32), sds((cap, TW, D), BF16),
        ],
        compiler_params=pltpu.CompilerParams(vmem_limit_bytes=VMEM_LIMIT),
        cost_estimate=pl.CostEstimate(flops=40_000_000_000, bytes_accessed=80_000_000, transcendentals=8_000_000),
    )(meta, ext, gain, shift, wqkv, bias, table, ka, kb)


def phi_parts(u):
    e = jnp.exp(u * u * -0.5)
    t = 1.0 / (1.0 + (0.3275911 * 0.7071067811865476) * jnp.abs(u))
    poly = t * (0.254829592 + t * (-0.284496736 + t * (1.421413741 + t * (-1.453152027 + t * 1.061405429))))
    tail = 0.5 * poly * e
    return jnp.where(u >= 0, 1.0 - tail, tail), e * 0.3989422804014327


def mlp_kernel(
    meta_ref, grows_ref, x_ref, att_ref, wproj_ref, pbias_ref, gain_ref, shift_ref, ff_ref, b1_ref, b2_ref,
    out_ref, g_ref, n2_ref, act_ref, dpre_ref, dmix_ref, datt_ref, sums_ref, sum1_ref,
    acc_ref, dn_ref,
):
    w = pl.program_id(0)

    @pl.when(w == 0)
    def _():
        sums_ref[...] = jnp.zeros_like(sums_ref)
        sum1_ref[...] = jnp.zeros_like(sum1_ref)

    target = token_target(meta_ref, w)
    g = take_window(target, grows_ref)
    gb = g.astype(BF16)
    g_ref[...] = gb
    sums_ref[0] += fold8(g)
    hidden = x_ref[...].astype(F32) + mm(att_ref[...], wproj_ref[...]) + pbias_ref[...]
    unit, inverse = norm(hidden)
    n2 = (unit * gain_ref[...] + shift_ref[...]).astype(BF16)
    n2_ref[...] = n2
    acc_ref[...] = hidden + b2_ref[...]
    parts, chunk = ff_ref.shape[0], ff_ref.shape[2] // 2
    for c in range(parts):
        cols = slice(chunk * c, chunk * c + chunk)
        w1, w2t = ff_ref[c, :, :chunk], ff_ref[c, :, chunk:]
        u = mm(n2, w1) + b1_ref[:, cols]
        dact = mm(gb, w2t)
        cdf, pdf = phi_parts(u)
        act = (u * cdf).astype(BF16)
        act_ref[:, cols] = act
        acc_ref[...] += mm_nt(act, w2t)
        dpre32 = dact * (cdf + u * pdf)
        dpre = dpre32.astype(BF16)
        dpre_ref[:, cols] = dpre
        sum1_ref[:, cols] += fold8(dpre32)
        step = mm_nt(dpre, w1)
        if c == 0:
            dn_ref[...] = step
        else:
            dn_ref[...] += step
    out_ref[...] = acc_ref[...].astype(BF16)
    dn = dn_ref[...]
    sums_ref[1] += fold8(dn * unit)
    sums_ref[2] += fold8(dn)
    dh = g + norm_back(dn, unit, inverse, gain_ref[...])
    dmix = dh.astype(BF16)
    dmix_ref[...] = dmix
    sums_ref[3] += fold8(dh)
    datt_ref[...] = mm_nt(dmix, wproj_ref[...]).astype(BF16)


def feed_forward(meta, gext, x, att, wproj, pbias, gain, shift, ff, b1, b2):
    cap = meta.shape[0]
    sds = jax.ShapeDtypeStruct
    return pl.pallas_call(
        mlp_kernel,
        grid_spec=pltpu.PrefetchScalarGridSpec(
            num_scalar_prefetch=1,
            grid=(cap,),
            in_specs=[
                rows_spec(WIN), per_window(TW, D), per_window(TW, D), whole((D, D)), whole((1, D)), whole((1, D)),
                whole((1, D)), whole(ff.shape), whole((1, FF)), whole((1, D)),
            ],
            out_specs=[
                per_window(TW, D), per_window(TW, D), per_window(TW, D), per_window(TW, FF), per_window(TW, FF),
                per_window(TW, D), per_window(TW, D), whole((4, 8, D)), whole((8, FF)),
            ],
            scratch_shapes=[pltpu.VMEM((TW, D), F32), pltpu.VMEM((TW, D), F32)],
        ),
        out_shape=[
            sds((cap, TW, D), BF16), sds((cap, TW, D), BF16), sds((cap, TW, D), BF16), sds((cap, TW, FF), BF16),
            sds((cap, TW, FF), BF16), sds((cap, TW, D), BF16), sds((cap, TW, D), BF16), sds((4, 8, D), F32),
            sds((8, FF), F32),
        ],
        compiler_params=pltpu.CompilerParams(vmem_limit_bytes=VMEM_LIMIT),
        cost_estimate=pl.CostEstimate(flops=60_000_000_000, bytes_accessed=80_000_000, transcendentals=8_000_000),
    )(meta, gext, x, att, wproj, pbias, gain, shift, ff, b1, b2)


MESH = pl.DeviceIdType.MESH
SHARD_ROWS = 192
SHARD_COLS = 384


def place():
    img, band = lax.axis_index("img"), lax.axis_index("band")
    return {"zh": img // 4, "zl": img // 2 % 2, "y": img % 2, "x": band // 2, "c": band % 2}


def partner(dim):
    img, band = lax.axis_index("img"), lax.axis_index("band")
    at = place()[dim]
    step = {"zh": 4, "zl": 2, "y": 1, "x": 2, "c": 1}[dim]
    move = step - 2 * step * at
    return (img, band + move) if dim in ("x", "c") else (img + move, band)


def greet():
    barrier = pltpu.get_barrier_semaphore()
    for dim in ("c", "x", "y", "zh", "zl"):
        pl.semaphore_signal(barrier, inc=1, device_id=partner(dim), device_id_type=MESH)
    pl.semaphore_wait(barrier, 5)


class Halving:
    AXES = ("x", "zh", "zl", "y")

    def __init__(self, source, own, got, sems, order, rows):
        self.source, self.own, self.got, self.sems, self.order, self.rows = source, own, got, sems, order, rows
        self.at = place()

    @staticmethod
    def scratch(rows):
        shapes = [(2, 2, 2, 2), (2, 2, 2, 2), (2, 2, 2), (2, 2), (2,), (1,)]
        return [pltpu.VMEM(s + (rows, SHARD_COLS), BF16) for s in shapes] + [pltpu.SemaphoreType.DMA((11,))]

    def first(self):
        c = self.at["c"]
        send, recv, local = self.sems.at[0], self.sems.at[1], self.sems.at[10]
        for x in range(2):
            for img in range(8):
                spot = (x, img // 4, img // 2 % 2, img % 2)
                pltpu.make_async_remote_copy(
                    src_ref=self.source(x, img, 1 - c), dst_ref=self.got[0].at[spot], send_sem=send, recv_sem=recv,
                    device_id=partner("c"), device_id_type=MESH,
                ).start()
                pltpu.make_async_copy(self.source(x, img, c), self.own.at[spot], local).start()

    def first_done(self):
        send, recv, local = self.sems.at[0], self.sems.at[1], self.sems.at[10]
        whole = pltpu.make_async_remote_copy(
            src_ref=self.got[0], dst_ref=self.got[0], send_sem=send, recv_sem=recv,
            device_id=partner("c"), device_id_type=MESH,
        )
        whole.wait_send()
        whole.wait_recv()
        pltpu.make_async_copy(self.got[0], self.own, local).wait()

        def add(i, _):
            spot = (i // 8, i // 4 % 2, i // 2 % 2, i % 2)
            self.own[spot] = (self.own[spot].astype(F32) + self.got[0][spot].astype(F32)).astype(BF16)
            return 0

        lax.fori_loop(0, 16, add, 0)

    def index(self, k, dim=None):
        spot = []
        for axis in self.AXES:
            if axis == dim:
                spot.append(1 - self.at[axis])
            elif axis in self.order[:k]:
                spot.append(self.at[axis])
            else:
                spot.append(slice(None))
        return tuple(spot)

    def copy(self, k):
        dim = self.order[k]
        src = self.own.at[self.index(k, dim)]
        dst = self.got[k + 1].at[0] if k == 3 else self.got[k + 1]
        return pltpu.make_async_remote_copy(
            src_ref=src, dst_ref=dst, send_sem=self.sems.at[2 + 2 * k], recv_sem=self.sems.at[3 + 2 * k],
            device_id=partner(dim), device_id_type=MESH,
        )

    def step(self, k):
        self.copy(k).start()

    def step_done(self, k):
        self.copy(k).wait()
        done = self.order[: k + 1]
        free = [axis for axis in self.AXES if axis not in done]
        count = 2 ** len(free)

        def add(i, _):
            bits = {axis: (i // 2 ** (len(free) - 1 - j)) % 2 for j, axis in enumerate(free)}
            spot = tuple(bits[axis] if axis in bits else self.at[axis] for axis in self.AXES)
            self.own[spot] = (self.own[spot].astype(F32) + self.got[k + 1][tuple(bits[axis] for axis in free)].astype(F32)).astype(BF16)
            return 0

        if k < 3:
            lax.fori_loop(0, count, add, 0)

    def result(self):
        spot = tuple(self.at[axis] for axis in self.AXES)
        return self.own[spot].astype(F32) + self.got[4][0].astype(F32)


def timeline(w, moments):
    for when, bodies in moments.items():
        @pl.when(w == when)
        def _(bodies=bodies):
            for body in bodies:
                body()


def attn_bwd_kernel(
    meta_ref, qkv_ref, p_ref, inv_ref, att_ref, datt_ref, table_ref, kback_ref, *rest,
):
    w = pl.program_id(0)
    if len(rest) == 3:
        dqkv_ref, rel_ref, bias_ref = rest
        streams = None
    else:
        fc1_ref, fc2_ref, dqkv_ref, rel_ref, bias_ref, sum1_ref, sum2_ref = rest[:7]
        streams = []
        for n, (ref, order) in enumerate(((fc1_ref, ("x", "y", "zh", "zl")), (fc2_ref, ("y", "zh", "zl", "x")))):
            own, *got, sems = rest[7 + 7 * n : 14 + 7 * n]

            def source(x, img, c, ref=ref):
                row = pl.multiple_of((2 * x + c) * SHARD_ROWS, SHARD_ROWS)
                return ref.at[pl.ds(row, SHARD_ROWS), pl.ds(img * SHARD_COLS, SHARD_COLS)]

            streams.append(Halving(source, own, got, sems, order, SHARD_ROWS))
        one, two = streams
        timeline(
            w,
            {
                0: [greet, one.first, two.first],
                3: [one.first_done, lambda: one.step(0), two.first_done, lambda: two.step(0)],
                9: [
                    lambda: one.step_done(0), lambda: one.step(1), lambda: two.step_done(0), lambda: two.step(1),
                ],
                12: [lambda: one.step_done(1), lambda: one.step(2)],
            },
        )

    @pl.when(w == 0)
    def _():
        rel_ref[...] = jnp.zeros_like(rel_ref)
        bias_ref[...] = jnp.zeros_like(bias_ref)

    lane = iota((TW, LANES), 1)
    low_half = lane < 64
    onehot = kback_ref[...]
    for p in range(PAIRS):
        q = qkv_ref[:, LANES * p : LANES * p + LANES]
        k8 = qkv_ref[:, D + LANES * p : D + LANES * p + LANES]
        v = qkv_ref[:, 2 * D + LANES * p : 2 * D + LANES * p + LANES]
        cols = slice(LANES * p, LANES * p + LANES)
        da = datt_ref[:, cols].astype(F32) * inv_ref[:, cols]
        da_low = da.astype(BF16)
        prod = da_low.astype(F32) * att_ref[:, cols].astype(F32)
        keys = jnp.concatenate([k8, onehot], axis=1)
        da_t = da.T.astype(BF16)
        q_t = q.astype(F32).T.astype(BF16)
        zero = jnp.zeros_like(v)
        dqx, dv_t, dk_t = [], [], []
        for h in range(2):
            mine = low_half if h == 0 else ~low_half
            centre = jnp.sum(jnp.where(mine, prod, 0.0), axis=-1, keepdims=True)
            dp = mm_nt(da_low, jnp.where(mine, v, zero))
            e = p_ref[2 * p + h]
            ds = (e.astype(F32) * (dp - centre)).astype(BF16)
            dqx.append(mm(ds, keys))
            dv_t.append(mm(da_t[64 * h : 64 * h + 64], e))
            dk_t.append(mm(q_t[64 * h : 64 * h + 64], ds))
        dq = jnp.where(low_half, dqx[0][:, :LANES], dqx[1][:, :LANES])
        drc = jnp.where(low_half, dqx[0][:, LANES:], dqx[1][:, LANES:])
        part = lane & 63
        rows = roll_rows(jnp.where(part < 16, drc, 0.0), 1)
        cols_part = roll_cols(jnp.where((part >= 16) & (part < 32), drc, 0.0), LANES - 16)
        skew = jnp.concatenate([rows, cols_part], axis=1).astype(BF16)
        dq = dq + mm_nt(skew, table_ref[...])
        rel_ref[...] += mm(q_t, skew)
        dv = jnp.concatenate(dv_t, axis=0).T
        dk = (jnp.concatenate(dk_t, axis=0) * 0.125).T
        dqkv_ref[:, cols] = dq.astype(BF16)
        dqkv_ref[:, D + LANES * p : D + LANES * p + LANES] = dk.astype(BF16)
        dqkv_ref[:, 2 * D + LANES * p : 2 * D + LANES * p + LANES] = dv.astype(BF16)
        bias_ref[0, :, cols] += fold8(dq)
        bias_ref[1, :, cols] += fold8(dv)

    if streams:
        @pl.when(w == pl.num_programs(0) - 1)
        def _():
            one.step_done(2)
            one.step(3)
            two.step_done(1)
            two.step(2)
            one.step_done(3)
            sum1_ref[...] = one.result()
            two.step_done(2)
            two.step(3)
            two.step_done(3)
            sum2_ref[...] = two.result()


def attention_backward(meta, qkv, p, inv, att, datt, table, kback, grads=()):
    cap = meta.shape[0]
    sds = jax.ShapeDtypeStruct
    anywhere = pl.BlockSpec(memory_space=pl.ANY)
    shard = (SHARD_ROWS, SHARD_COLS)
    extra = dict(collective_id=1, has_side_effects=True) if grads else {}
    return pl.pallas_call(
        attn_bwd_kernel,
        grid_spec=pltpu.PrefetchScalarGridSpec(
            num_scalar_prefetch=1,
            grid=(cap,),
            in_specs=[
                per_window(TW, 3 * D), per_window(HEADS, TW, TW), per_window(TW, D), per_window(TW, D),
                per_window(TW, D), whole((LANES, 256)), whole((TW, LANES)),
            ] + [anywhere] * len(grads),
            out_specs=[per_window(TW, 3 * D), whole((LANES, 256)), whole((2, 8, D))] + [whole(shard)] * len(grads),
            scratch_shapes=Halving.scratch(SHARD_ROWS) * len(grads),
        ),
        out_shape=[sds((cap, TW, 3 * D), BF16), sds((LANES, 256), F32), sds((2, 8, D), F32)]
        + [sds(shard, F32)] * len(grads),
        compiler_params=pltpu.CompilerParams(vmem_limit_bytes=VMEM_LIMIT, **extra),
        cost_estimate=pl.CostEstimate(flops=60_000_000_000, bytes_accessed=80_000_000, transcendentals=0),
    )(meta, qkv, p, inv, att, datt, table, kback, *grads)


def rel_from(acc):
    def one(block):
        own = block[:64, :32] + block[64:, 64:96]
        return own[:, :RELS].T

    return one(acc[:, :LANES])[::-1], one(acc[:, LANES:])


def put_window(target, y, acc_ref, row0):
    picks = jnp.where(iota((TW, 256), 1) == target, 1.0, 0.0).astype(BF16)
    for q in range(4):
        n = 4 if q < 3 else 2
        t = slice(64 * q, 64 * q + STRIDE * n)
        part = lax.dot_general(
            picks[t, : 64 * n], y[t], (((0,), (0,)), ((), ())), preferred_element_type=F32
        )
        acc_ref[pl.ds(row0 + 4 * q, n)] += part.reshape(n, SIDE, D)


def scatter_kernel(meta_ref, y_ref, ext_ref, acc_ref):
    w = pl.program_id(0)

    @pl.when(w == 0)
    def _():
        acc_ref[...] = jnp.zeros_like(acc_ref)

    put_window(token_target(meta_ref, w), y_ref[...], acc_ref, meta_ref[w, 0])

    @pl.when(w == pl.num_programs(0) - 1)
    def _():
        def copy(i, _):
            ext_ref[i] = acc_ref[i].astype(BF16)
            return 0
        lax.fori_loop(0, ext_ref.shape[0], copy, 0)


def scatter(meta, y, ext_rows):
    cap = meta.shape[0]
    return pl.pallas_call(
        scatter_kernel,
        grid_spec=pltpu.PrefetchScalarGridSpec(
            num_scalar_prefetch=1,
            grid=(cap,),
            in_specs=[per_window(TW, D)],
            out_specs=whole((ext_rows, SIDE, D)),
            scratch_shapes=[pltpu.VMEM((ext_rows, SIDE, D), F32)],
        ),
        out_shape=jax.ShapeDtypeStruct((ext_rows, SIDE, D), BF16),
        compiler_params=pltpu.CompilerParams(vmem_limit_bytes=VMEM_LIMIT),
        cost_estimate=pl.CostEstimate(flops=5_000_000_000, bytes_accessed=20_000_000, transcendentals=0),
    )(meta, y)


def last_kernel(
    meta_ref, dqkv_ref, wqkv_ref, x_ref, dmix_ref, gain_ref, ext_ref, sums_ref, acc_ref,
):
    w = pl.program_id(0)

    @pl.when(w == 0)
    def _():
        acc_ref[...] = jnp.zeros_like(acc_ref)
        sums_ref[...] = jnp.zeros_like(sums_ref)

    target = token_target(meta_ref, w)
    dn = jnp.zeros((TW, D), F32)
    for c in range(3):
        cols = slice(D * c, D * c + D)
        dn = dn + mm_nt(dqkv_ref[:, cols], wqkv_ref[:, cols])
    dn = jnp.where(target >= 0, dn, 0.0)
    unit, inverse = norm(x_ref[...].astype(F32))
    sums_ref[0] += fold8(dn * unit)
    sums_ref[1] += fold8(dn)
    grad = dmix_ref[...].astype(F32) + norm_back(dn, unit, inverse, gain_ref[...])
    put_window(target, grad.astype(BF16), acc_ref, meta_ref[w, 0])

    @pl.when(w == pl.num_programs(0) - 1)
    def _():
        def copy(i, _):
            ext_ref[i] = acc_ref[i].astype(BF16)
            return 0
        lax.fori_loop(0, ext_ref.shape[0], copy, 0)


def last_norm(meta, dqkv, wqkv, x, dmix, gain, ext_rows):
    cap = meta.shape[0]
    sds = jax.ShapeDtypeStruct
    return pl.pallas_call(
        last_kernel,
        grid_spec=pltpu.PrefetchScalarGridSpec(
            num_scalar_prefetch=1,
            grid=(cap,),
            in_specs=[
                per_window(TW, 3 * D), whole((D, 3 * D)), per_window(TW, D), per_window(TW, D), whole((1, D)),
            ],
            out_specs=[whole((ext_rows, SIDE, D)), whole((2, 8, D))],
            scratch_shapes=[pltpu.VMEM((ext_rows, SIDE, D), F32)],
        ),
        out_shape=[sds((ext_rows, SIDE, D), BF16), sds((2, 8, D), F32)],
        compiler_params=pltpu.CompilerParams(vmem_limit_bytes=VMEM_LIMIT),
        cost_estimate=pl.CostEstimate(flops=15_000_000_000, bytes_accessed=30_000_000, transcendentals=0),
    )(meta, dqkv, wqkv, x, dmix, gain)


def window_plan(images, bands):
    lists = [[] for _ in range(bands)]
    if images == 2 and bands == 4:
        cuts = ((0, 8, 15, 20, 25), (0, 5, 10, 17, 25))
    else:
        cuts = [
            [(WINDOWS * b + (bands - 1 if m % 2 else 0)) // bands for b in range(bands + 1)] for m in range(images)
        ]
    for m in range(images):
        for b in range(bands):
            lists[b] += [(m, w) for w in range(cuts[m][b], min(cuts[m][b + 1], WINDOWS))]
    cap = max(len(item) for item in lists)
    return np.array([item + [(0, -1)] * (cap - len(item)) for item in lists], np.int32)


HALO = 12


def near(images, bands, band_rows):
    return images == 2 and bands == 4 and band_rows == 16


CORE = [(0, 1), (1, 0), (2, 3), (3, 2)]
CROSS = [(1, 2), (2, 1)]


def extend(rows, band):
    images, band_rows = rows.shape[:2]
    if not near(images, lax.axis_size("band"), band_rows):
        full = lax.all_gather(rows, "band", axis=1, tiled=True)
        return jnp.pad(full, ((0, 0), (6, 6), (0, 0), (0, 0)))
    odd = band % 2 == 1
    top, bottom = rows[:, :HALO], rows[:, -HALO:]
    from_core = lax.ppermute(jnp.where(odd, top, bottom), "band", CORE)
    from_cross = lax.ppermute(jnp.where(odd, bottom[1], top[0]), "band", CROSS)
    zero = jnp.zeros_like(from_cross)
    above = jnp.where(odd, from_core, jnp.stack([zero, from_cross]))
    below = jnp.where(odd, jnp.stack([from_cross, zero]), from_core)
    return jnp.concatenate([above, rows, below], axis=1)


def collect(ext, band, images, band_rows):
    if not near(images, lax.axis_size("band"), band_rows):
        return lax.psum_scatter(ext[:, 6:-6], "band", scatter_dimension=1, tiled=True).astype(F32)
    odd = band % 2 == 1
    above, below = ext[:, :HALO], ext[:, -HALO:]
    from_core = lax.ppermute(jnp.where(odd, above, below), "band", CORE).astype(F32)
    from_cross = lax.ppermute(jnp.where(odd, below[0], above[1]), "band", CROSS).astype(F32)
    zero = jnp.zeros_like(from_cross)
    top = jnp.where(odd, from_core, jnp.stack([from_cross, zero]))
    bottom = jnp.where(odd, jnp.stack([zero, from_cross]), from_core)
    own = ext[:, HALO:-HALO].astype(F32)
    rest = band_rows - HALO
    return own + jnp.pad(top, ((0, 0), (0, rest), (0, 0), (0, 0))) + jnp.pad(bottom, ((0, 0), (rest, 0), (0, 0), (0, 0)))


def shards(
    image_tokens, pad_offsets, ln1_gain, ln1_bias, w_qkv, q_bias, v_bias, rel_rows, rel_cols, w_proj, proj_bias,
    ln2_gain, ln2_bias, w_fc1, fc1_bias, w_fc2, fc2_bias, out_grad,
):
    images, band_rows = image_tokens.shape[:2]
    bands, groups = lax.axis_size("band"), lax.axis_size("img")
    band, group = lax.axis_index("band"), lax.axis_index("img")
    axes = ("img", "band")

    part, wide = w_qkv.shape
    small = jnp.concatenate(
        [
            ln1_gain, ln1_bias, q_bias, v_bias, proj_bias, ln2_gain, ln2_bias, fc2_bias, fc1_bias,
            rel_rows.reshape(-1), rel_cols.reshape(-1),
        ]
    )
    small_rows = -(-small.shape[0] // (wide * 8)) * 8
    small = jnp.pad(small, (0, small_rows * wide - small.shape[0])).reshape(small_rows, wide)
    first = lax.all_gather(jnp.concatenate([w_qkv, small], axis=0), axes, axis=0, tiled=False)
    first = first.reshape(groups, bands, part + small_rows, wide)
    second = lax.all_gather(
        jnp.concatenate([w_fc1, w_fc2.T, w_proj], axis=1), axes, axis=0, tiled=False
    ).reshape(groups, bands * part, -1)
    wqkv = first[:, :, :part].transpose(1, 2, 0, 3).reshape(D, 3 * D)
    tail = first[:, :, part:].reshape(groups, bands, small_rows * wide)
    share = D // groups
    vectors = tail[:, 0, : 8 * share].reshape(groups, 8, share).transpose(1, 0, 2).reshape(8, 1, D).astype(F32)
    fc1_shift = tail[:, 0, 8 * share : 8 * share + FF // groups].reshape(1, FF).astype(F32)
    at = 8 * share + FF // groups
    rels = tail[0, :, at : at + 2 * RELS * (HEAD // bands)].reshape(bands, 2, RELS, HEAD // bands)
    rels = rels.transpose(1, 2, 0, 3).reshape(2, RELS, HEAD)
    gain1, shift1, qb, vb, pb, gain2, shift2, b2 = [vectors[i] for i in range(8)]
    bias = jnp.concatenate([qb, jnp.zeros_like(qb), vb], axis=1)
    inner = FF // groups
    ff = second[:, :, : 2 * inner]
    wproj = second[:, :, 2 * inner :].transpose(1, 0, 2).reshape(D, D)

    plan = jnp.asarray(window_plan(images, bands))[band]
    image, window = plan[:, 0], plan[:, 1]
    close = near(images, bands, band_rows)
    ext_per = band_rows + 2 * HALO if close else bands * band_rows + 12
    base = band_rows * band - HALO if close else -6
    live = window >= 0
    spot = jnp.maximum(window, 0)
    offsets = pad_offsets[image]
    row = spot // GRID * WIN - offsets[:, 0]
    col = spot % GRID * WIN - offsets[:, 1]
    meta = jnp.stack(
        [jnp.where(live, image * ext_per + row - base, 0), col, row, live.astype(jnp.int32)], axis=1
    ).astype(jnp.int32)
    cap = meta.shape[0]
    ext_rows = images * ext_per

    ka, kb, kback = key_constants()
    ext = extend(image_tokens, band).reshape(ext_rows, SIDE, D)
    x, normed1, qkv, probs, inv, att = attention_forward(
        meta, ext, gain1, shift1, wqkv, bias, rel_table(rels[0], rels[1], True), ka, kb
    )
    gext = extend(out_grad, band).reshape(ext_rows, SIDE, D)
    out_win, g, normed2, act, d_pre, d_mixed, d_att, sums, sum_fc1 = feed_forward(
        meta, gext, x, att, wproj, pb, gain2, shift2, ff, fc1_shift, b2
    )
    out_ext = scatter(meta, out_win, ext_rows).reshape(images, ext_per, SIDE, D)
    output = collect(out_ext, band, images, band_rows).astype(BF16)

    def flat(a):
        return a.reshape(cap * TW, a.shape[-1])

    def weight_grad(left, right):
        return jnp.einsum("td,te->de", flat(left), flat(right), preferred_element_type=F32).astype(BF16)

    fused = close and groups == 8
    d_fc2 = weight_grad(g, act)
    d_fc1 = weight_grad(normed2, d_pre)
    d_proj = weight_grad(att, d_mixed)
    d_qkv, rel_acc, bias_sums, *done = attention_backward(
        meta, qkv, probs, inv, att, d_att, rel_table(rels[0], rels[1], False), kback, (d_fc1, d_fc2) if fused else ()
    )
    d_wqkv = weight_grad(normed1, d_qkv)
    in_ext, sums1 = last_norm(meta, d_qkv, wqkv, x, d_mixed, gain1, ext_rows)
    input_grad = collect(in_ext.reshape(images, ext_per, SIDE, D), band, images, band_rows)

    def reduce(grad, rows_axis, cols_axis):
        grad = lax.psum_scatter(grad, cols_axis, scatter_dimension=1, tiled=True)
        return lax.psum_scatter(grad, rows_axis, scatter_dimension=0, tiled=True).astype(F32)

    g_fc1, g_fc2 = done if fused else (reduce(d_fc1, "band", "img"), reduce(d_fc2, "band", "img"))
    d_rel_rows, d_rel_cols = rel_from(rel_acc)
    total = lax.psum(
        (jnp.sum(sums1, 1), jnp.sum(bias_sums, 1), jnp.sum(sums, 1), jnp.sum(sum_fc1, 0), d_rel_rows, d_rel_cols), axes
    )

    def img_share(vector):
        n = vector.shape[0] // groups
        return lax.dynamic_slice_in_dim(vector, group * n, n, 0)

    def band_share(table):
        n = table.shape[1] // bands
        return lax.dynamic_slice_in_dim(table, band * n, n, 1)

    return (
        output,
        input_grad,
        img_share(total[0][0]),
        img_share(total[0][1]),
        reduce(d_wqkv, "band", "img"),
        img_share(total[1][0]),
        img_share(total[1][1]),
        band_share(total[4]),
        band_share(total[5]),
        reduce(d_proj, "band", "img"),
        img_share(total[2][3]),
        img_share(total[2][1]),
        img_share(total[2][2]),
        g_fc1,
        img_share(total[3]),
        g_fc2.T,
        img_share(total[2][0]),
    )


def solution(mesh):
    tokens, vector, matrix = P("img", "band", None, None), P("img"), P("band", "img")
    table, wide = P(None, "band"), P("img", "band")
    return jax.shard_map(
        shards,
        mesh=mesh,
        in_specs=(
            tokens, P("img", None), vector, vector, matrix, vector, vector, table, table, matrix, vector, vector,
            vector, matrix, vector, wide, vector, tokens,
        ),
        out_specs=(
            tokens, tokens, vector, vector, matrix, vector, vector, table, table, matrix, vector, vector, vector,
            matrix, vector, wide, vector,
        ),
        check_vma=False,
    )
```

```python
import functools
import numpy as np
import jax
import jax.numpy as jnp
from jax import lax
from jax.sharding import PartitionSpec as P
from jax.experimental import pallas as pl
from jax.experimental.pallas import tpu as pltpu

D = 768
HEADS = 12
HEAD = 64
FF = 3072
WIN = 14
SIDE = 64
GRID = 5
WINDOWS = 25
RELS = 27
STRIDE = 16
TW = WIN * STRIDE
PAIRS = HEADS // 2
LANES = 128
EPSILON = 1e-06
F32 = jnp.float32
BF16 = jnp.bfloat16
VMEM_LIMIT = 60 * 1024 * 1024
NT = (((1,), (1,)), ((), ()))


def mm(a, b):
    return jnp.dot(a, b, preferred_element_type=F32)


def mm_nt(a, b):
    return lax.dot_general(a, b, NT, preferred_element_type=F32)


def iota(shape, dim):
    return lax.broadcasted_iota(jnp.int32, shape, dim)


def token_target(meta_ref, w):
    t = iota((TW, 1), 0)
    a, b = t >> 4, t & 15
    col = meta_ref[w, 1] + b
    row = meta_ref[w, 2] + a
    ok = (b < WIN) & (col >= 0) & (col < SIDE) & (row >= 0) & (row < SIDE) & (meta_ref[w, 3] > 0)
    return jnp.where(ok, ((a & 3) << 6) + col, -1)


def take_window(target, rows_ref):
    picks = jnp.where(iota((TW, 256), 1) == target, 1.0, 0.0).astype(BF16)
    parts = []
    for q in range(3):
        src = rows_ref[4 * q : 4 * q + 4].reshape(256, D)
        parts.append(mm(picks[64 * q : 64 * q + 64], src))
    src = rows_ref[12:14].reshape(128, D)
    parts.append(mm(picks[192:224, :128], src))
    return jnp.concatenate(parts, axis=0)


def norm(values):
    mean = jnp.sum(values, axis=-1, keepdims=True) * (1.0 / D)
    centred = values - mean
    inverse = lax.rsqrt(jnp.sum(centred * centred, axis=-1, keepdims=True) * (1.0 / D) + EPSILON)
    return centred * inverse, inverse


def norm_back(grad, unit, inverse, gain):
    s = grad * gain
    m1 = jnp.sum(s, axis=-1, keepdims=True) * (1.0 / D)
    m2 = jnp.sum(s * unit, axis=-1, keepdims=True) * (1.0 / D)
    return inverse * (s - m1 - unit * m2)


def fold8(x):
    return jnp.sum(x.reshape(x.shape[0] // 8, 8, x.shape[1]), axis=0)


def roll_rows(x, sign):
    out = []
    for a in range(WIN):
        piece = x[STRIDE * a : STRIDE * a + STRIDE]
        by = (sign * (13 - a)) % LANES
        out.append(pltpu.roll(piece, by, 1) if by else piece)
    return jnp.concatenate(out, axis=0)


def roll_cols(x, first):
    out = []
    for a in range(WIN):
        piece = x[STRIDE * a : STRIDE * a + STRIDE]
        out.append(pltpu.roll(piece, first, 1, stride=1, stride_axis=0))
    return jnp.concatenate(out, axis=0)


def attn_fwd_pair(q, k8, v, table, keys_a, keys_b, p_ref, p):
    lane = iota((TW, LANES), 1)
    low_half = lane < 64
    rc = mm(q, table)
    both = jnp.where((lane & 31) < 16, roll_rows(rc[:, :LANES], -1), roll_cols(rc[:, LANES:], 3))
    high = both.astype(BF16)
    rest = (both - high.astype(F32)).astype(BF16)
    extra = jnp.where((lane & 63) < 32, high, rest)
    extra = jnp.where((lane & 63) == 14, jnp.ones_like(extra), extra)
    left = jnp.concatenate([q, extra], axis=1)
    zero = jnp.zeros_like(k8)
    wide_v = jnp.concatenate([v, jnp.ones_like(v)], axis=1)
    outs, invs = [], []
    for h in range(2):
        keys = jnp.concatenate(
            [jnp.where(low_half if h == 0 else ~low_half, k8, zero), (keys_a, keys_b)[h]], axis=1
        )
        s = mm_nt(left, keys)
        e = jnp.exp(s - jnp.max(s, axis=-1, keepdims=True)).astype(BF16)
        p_ref[2 * p + h] = e
        o = mm(e, wide_v)
        inv = 1.0 / o[:, LANES:]
        outs.append(o[:, :LANES] * inv)
        invs.append(inv)
    att = jnp.where(low_half, outs[0], outs[1]).astype(BF16)
    inv = jnp.where(low_half, invs[0], invs[1])
    return att, inv


def fwd_kernel(
    meta_ref, rows_ref, gain_ref, shift_ref, wqkv_ref, bias_ref, table_ref, ka_ref, kb_ref,
    x_ref, n_ref, qkv_ref, p_ref, inv_ref, att_ref,
):
    w = pl.program_id(0)
    target = token_target(meta_ref, w)
    x = take_window(target, rows_ref)
    x_ref[...] = x.astype(BF16)
    unit, _ = norm(x)
    normed = jnp.where(target >= 0, unit * gain_ref[...] + shift_ref[...], 0.0).astype(BF16)
    n_ref[...] = normed
    for c in range(9):
        cols = slice(256 * c, 256 * c + 256)
        y = mm(normed, wqkv_ref[:, cols]) + bias_ref[:, cols]
        if 3 <= c < 6:
            y = y.astype(BF16).astype(F32) * 0.125
        qkv_ref[:, cols] = y.astype(BF16)

    for p in range(PAIRS):
        a = slice(LANES * p, LANES * p + LANES)
        q = qkv_ref[:, LANES * p : LANES * p + LANES]
        k8 = qkv_ref[:, D + LANES * p : D + LANES * p + LANES]
        v = qkv_ref[:, 2 * D + LANES * p : 2 * D + LANES * p + LANES]
        att, inv = attn_fwd_pair(q, k8, v, table_ref[...], ka_ref[...], kb_ref[...], p_ref, p)
        att_ref[:, a] = att
        inv_ref[:, a] = inv


def rows_spec(rows):
    return pl.BlockSpec(
        (pl.Element(rows), pl.Element(SIDE), pl.Element(D)), lambda w, meta: (meta[w, 0], 0, 0)
    )


def whole(shape, buffers=1):
    zeros = (0,) * len(shape)
    return pl.BlockSpec(shape, lambda w, meta: zeros, pipeline_mode=pl.Buffered(buffers))


def per_window(*tail):
    zeros = (0,) * len(tail)
    return pl.BlockSpec((None,) + tail, lambda w, meta: (w,) + zeros)


def key_constants():
    t = np.arange(TW)
    kr, kc = t >> 4, t & 15
    real = kc < WIN
    base = np.zeros((TW, 64), np.float32)
    for off in (0, 32):
        base[t[real], off + kr[real]] = 1.0
        base[t[real], off + 16 + kc[real]] = 1.0
    back = np.zeros_like(base)
    back[t[real], kr[real]] = 1.0
    back[t[real], 16 + 13 - kc[real]] = 1.0
    base[~real, 14] = -1e30
    none = np.zeros_like(base)
    ka = np.concatenate([base, none], 1)
    kb = np.concatenate([none, base], 1)
    back = np.concatenate([back, back], 1)
    return jnp.asarray(ka, BF16), jnp.asarray(kb, BF16), jnp.asarray(back, BF16)


def rel_table(rel_rows, rel_cols, forward):
    def wide(rel):
        turned = jnp.pad(rel.T, ((0, 0), (0, 32 - RELS)))
        twice = jnp.concatenate([turned, turned], axis=1)
        none = jnp.zeros_like(twice)
        return jnp.concatenate(
            [jnp.concatenate([twice, none], 1), jnp.concatenate([none, twice], 1)], 0
        )

    return jnp.concatenate([wide(rel_rows[::-1]), wide(rel_cols[::-1] if forward else rel_cols)], axis=1)


def attention_forward(meta, ext, gain, shift, wqkv, bias, table, ka, kb):
    cap = meta.shape[0]
    sds = jax.ShapeDtypeStruct
    return pl.pallas_call(
        fwd_kernel,
        grid_spec=pltpu.PrefetchScalarGridSpec(
            num_scalar_prefetch=1,
            grid=(cap,),
            in_specs=[
                rows_spec(WIN), whole((1, D)), whole((1, D)), whole((D, 3 * D)), whole((1, 3 * D)),
                whole((LANES, 256)), whole((TW, LANES)), whole((TW, LANES)),
            ],
            out_specs=[
                per_window(TW, D), per_window(TW, D), per_window(TW, 3 * D),
                per_window(HEADS, TW, TW), per_window(TW, D), per_window(TW, D),
            ],
        ),
        out_shape=[
            sds((cap, TW, D), BF16), sds((cap, TW, D), BF16), sds((cap, TW, 3 * D), BF16),
            sds((cap, HEADS, TW, TW), BF16), sds((cap, TW, D), F32), sds((cap, TW, D), BF16),
        ],
        compiler_params=pltpu.CompilerParams(vmem_limit_bytes=VMEM_LIMIT),
        cost_estimate=pl.CostEstimate(flops=40_000_000_000, bytes_accessed=80_000_000, transcendentals=8_000_000),
    )(meta, ext, gain, shift, wqkv, bias, table, ka, kb)


def phi_parts(u):
    e = jnp.exp(u * u * -0.5)
    t = 1.0 / (1.0 + (0.3275911 * 0.7071067811865476) * jnp.abs(u))
    poly = t * (0.254829592 + t * (-0.284496736 + t * (1.421413741 + t * (-1.453152027 + t * 1.061405429))))
    tail = 0.5 * poly * e
    return jnp.where(u >= 0, 1.0 - tail, tail), e * 0.3989422804014327


def mlp_kernel(
    meta_ref, grows_ref, x_ref, att_ref, wproj_ref, pbias_ref, gain_ref, shift_ref, ff_ref, b1_ref, b2_ref,
    out_ref, g_ref, n2_ref, act_ref, dpre_ref, dmix_ref, datt_ref, sums_ref, sum1_ref,
    acc_ref, dn_ref,
):
    w = pl.program_id(0)

    @pl.when(w == 0)
    def _():
        sums_ref[...] = jnp.zeros_like(sums_ref)
        sum1_ref[...] = jnp.zeros_like(sum1_ref)

    target = token_target(meta_ref, w)
    g = take_window(target, grows_ref)
    gb = g.astype(BF16)
    g_ref[...] = gb
    sums_ref[0] += fold8(g)
    hidden = x_ref[...].astype(F32) + mm(att_ref[...], wproj_ref[...]) + pbias_ref[...]
    unit, inverse = norm(hidden)
    n2 = (unit * gain_ref[...] + shift_ref[...]).astype(BF16)
    n2_ref[...] = n2
    acc_ref[...] = hidden + b2_ref[...]
    parts, chunk = ff_ref.shape[0], ff_ref.shape[2] // 2
    for c in range(parts):
        cols = slice(chunk * c, chunk * c + chunk)
        w1, w2t = ff_ref[c, :, :chunk], ff_ref[c, :, chunk:]
        u = mm(n2, w1) + b1_ref[:, cols]
        dact = mm(gb, w2t)
        cdf, pdf = phi_parts(u)
        act = (u * cdf).astype(BF16)
        act_ref[:, cols] = act
        acc_ref[...] += mm_nt(act, w2t)
        dpre32 = dact * (cdf + u * pdf)
        dpre = dpre32.astype(BF16)
        dpre_ref[:, cols] = dpre
        sum1_ref[:, cols] += fold8(dpre32)
        step = mm_nt(dpre, w1)
        if c == 0:
            dn_ref[...] = step
        else:
            dn_ref[...] += step
    out_ref[...] = acc_ref[...].astype(BF16)
    dn = dn_ref[...]
    sums_ref[1] += fold8(dn * unit)
    sums_ref[2] += fold8(dn)
    dh = g + norm_back(dn, unit, inverse, gain_ref[...])
    dmix = dh.astype(BF16)
    dmix_ref[...] = dmix
    sums_ref[3] += fold8(dh)
    datt_ref[...] = mm_nt(dmix, wproj_ref[...]).astype(BF16)


def feed_forward(meta, gext, x, att, wproj, pbias, gain, shift, ff, b1, b2, spare):
    cap = meta.shape[0]
    sds = jax.ShapeDtypeStruct
    return pl.pallas_call(
        mlp_kernel,
        grid_spec=pltpu.PrefetchScalarGridSpec(
            num_scalar_prefetch=1,
            grid=(cap,),
            in_specs=[
                rows_spec(WIN), per_window(TW, D), per_window(TW, D), whole((D, D)), whole((1, D)), whole((1, D)),
                whole((1, D)), whole(ff.shape), whole((1, FF)), whole((1, D)),
            ],
            out_specs=[
                per_window(TW, D), per_window(TW, D), per_window(TW, D), per_window(TW, FF), per_window(TW, FF),
                per_window(TW, D), per_window(TW, D), whole((4, 8, D)), whole((8, FF)),
            ],
            scratch_shapes=[pltpu.VMEM((TW, D), F32), pltpu.VMEM((TW, D), F32)],
        ),
        out_shape=[
            sds((cap + spare, TW, D), BF16), sds((cap, TW, D), BF16), sds((cap, TW, D), BF16), sds((cap, TW, FF), BF16),
            sds((cap, TW, FF), BF16), sds((cap, TW, D), BF16), sds((cap, TW, D), BF16), sds((4, 8, D), F32),
            sds((8, FF), F32),
        ],
        compiler_params=pltpu.CompilerParams(vmem_limit_bytes=VMEM_LIMIT),
        cost_estimate=pl.CostEstimate(flops=60_000_000_000, bytes_accessed=80_000_000, transcendentals=8_000_000),
    )(meta, gext, x, att, wproj, pbias, gain, shift, ff, b1, b2)


MESH = pl.DeviceIdType.MESH
SHARD_ROWS = 192
SHARD_COLS = 384


def place():
    img, band = lax.axis_index("img"), lax.axis_index("band")
    return {"zh": img // 4, "zl": img // 2 % 2, "y": img % 2, "x": band // 2, "c": band % 2}


def partner(dim):
    img, band = lax.axis_index("img"), lax.axis_index("band")
    at = place()[dim]
    step = {"zh": 4, "zl": 2, "y": 1, "x": 2, "c": 1}[dim]
    move = step - 2 * step * at
    return (img, band + move) if dim in ("x", "c") else (img + move, band)


def peers():
    img, band = lax.axis_index("img"), lax.axis_index("band")
    return [(img, (band + d) % 4) for d in range(1, 4)], [((img + d) % 8, band) for d in range(1, 8)]


def greet():
    barrier = pltpu.get_barrier_semaphore()
    near_by, far = peers()
    for device in near_by + far:
        pl.semaphore_signal(barrier, inc=1, device_id=device, device_id_type=MESH)
    pl.semaphore_wait(barrier, 10)


class Halving:
    AXES = ("x", "zh", "zl", "y")

    def __init__(self, source, own, got, sems, order, rows):
        self.source, self.own, self.got, self.sems, self.order, self.rows = source, own, got, sems, order, rows
        self.at = place()

    @staticmethod
    def scratch(rows):
        shapes = [(2, 2, 2, 2), (2, 2, 2, 2), (2, 2, 2), (2, 2), (2,), (1,)]
        return [pltpu.VMEM(s + (rows, SHARD_COLS), BF16) for s in shapes] + [pltpu.SemaphoreType.DMA((11,))]

    def first(self):
        c = self.at["c"]
        send, recv, local = self.sems.at[0], self.sems.at[1], self.sems.at[10]
        for x in range(2):
            for img in range(8):
                spot = (x, img // 4, img // 2 % 2, img % 2)
                pltpu.make_async_remote_copy(
                    src_ref=self.source(x, img, 1 - c), dst_ref=self.got[0].at[spot], send_sem=send, recv_sem=recv,
                    device_id=partner("c"), device_id_type=MESH,
                ).start()
                pltpu.make_async_copy(self.source(x, img, c), self.own.at[spot], local).start()

    def first_done(self):
        send, recv, local = self.sems.at[0], self.sems.at[1], self.sems.at[10]
        whole = pltpu.make_async_remote_copy(
            src_ref=self.got[0], dst_ref=self.got[0], send_sem=send, recv_sem=recv,
            device_id=partner("c"), device_id_type=MESH,
        )
        whole.wait_send()
        whole.wait_recv()
        pltpu.make_async_copy(self.got[0], self.own, local).wait()

        def add(i, _):
            spot = (i // 8, i // 4 % 2, i // 2 % 2, i % 2)
            self.own[spot] = (self.own[spot].astype(F32) + self.got[0][spot].astype(F32)).astype(BF16)
            return 0

        lax.fori_loop(0, 16, add, 0)

    def index(self, k, dim=None):
        spot = []
        for axis in self.AXES:
            if axis == dim:
                spot.append(1 - self.at[axis])
            elif axis in self.order[:k]:
                spot.append(self.at[axis])
            else:
                spot.append(slice(None))
        return tuple(spot)

    def copy(self, k):
        dim = self.order[k]
        src = self.own.at[self.index(k, dim)]
        dst = self.got[k + 1].at[0] if k == 3 else self.got[k + 1]
        return pltpu.make_async_remote_copy(
            src_ref=src, dst_ref=dst, send_sem=self.sems.at[2 + 2 * k], recv_sem=self.sems.at[3 + 2 * k],
            device_id=partner(dim), device_id_type=MESH,
        )

    def step(self, k):
        self.copy(k).start()

    def step_done(self, k):
        self.copy(k).wait()
        done = self.order[: k + 1]
        free = [axis for axis in self.AXES if axis not in done]
        count = 2 ** len(free)

        def add(i, _):
            bits = {axis: (i // 2 ** (len(free) - 1 - j)) % 2 for j, axis in enumerate(free)}
            spot = tuple(bits[axis] if axis in bits else self.at[axis] for axis in self.AXES)
            self.own[spot] = (self.own[spot].astype(F32) + self.got[k + 1][tuple(bits[axis] for axis in free)].astype(F32)).astype(BF16)
            return 0

        if k < 3:
            lax.fori_loop(0, count, add, 0)

    def result(self):
        spot = tuple(self.at[axis] for axis in self.AXES)
        return self.own[spot].astype(F32) + self.got[4][0].astype(F32)


ORDERS = (("x", "y", "zh", "zl"), ("y", "x", "zh", "zl"))


def timeline(w, moments):
    for when, bodies in moments.items():
        @pl.when(w == when)
        def _(bodies=bodies):
            for body in bodies:
                body()


NEAR_CORE = 7
NEAR_CROSS = 5
CROSS_ROWS = 160


class Homeward:
    def __init__(self, windows, everything, sems):
        self.windows, self.all, self.sems = windows, everything, sems
        self.cap = everything.shape[0] - NEAR_CORE - NEAR_CROSS
        self.band = lax.axis_index("band")

    def inner(self):
        return (self.band == 1) | (self.band == 2)

    def outer(self):
        return (self.band == 0) | (self.band == 3)

    def keep(self):
        return pltpu.make_async_copy(self.windows, self.all.at[pl.ds(0, self.cap)], self.sems.at[4])

    def to_core(self, first, count):
        return pltpu.make_async_remote_copy(
            src_ref=self.windows.at[pl.ds(first, count)], dst_ref=self.all.at[pl.ds(self.cap, count)],
            send_sem=self.sems.at[0], recv_sem=self.sems.at[1], device_id=partner("c"), device_id_type=MESH,
        )

    def to_cross(self, sending):
        img = lax.axis_index("img")
        skip = (2 - self.band) if sending else (self.band - 1)
        rows = pl.ds(pl.multiple_of(skip * (TW - CROSS_ROWS), TW - CROSS_ROWS), CROSS_ROWS)
        return pltpu.make_async_remote_copy(
            src_ref=self.windows.at[pl.ds(0, NEAR_CROSS), rows],
            dst_ref=self.all.at[pl.ds(self.cap + NEAR_CORE, NEAR_CROSS), rows],
            send_sem=self.sems.at[2], recv_sem=self.sems.at[3], device_id=(img, 3 - self.band), device_id_type=MESH,
        )

    def send_cross(self):
        pl.when(self.inner())(lambda: self.to_cross(True).start())

    def send_core_inner(self):
        pl.when(self.inner())(lambda: self.to_core(NEAR_CROSS, NEAR_CORE).start())

    def send_core_outer(self):
        pl.when(self.outer())(lambda: self.to_core(0, 3).start())

    def finish(self):
        @pl.when(self.inner())
        def _():
            self.to_core(NEAR_CROSS, NEAR_CORE).wait_send()
            self.to_core(0, 3).wait_recv()
            self.to_cross(True).wait_send()
            self.to_cross(False).wait_recv()

        @pl.when(self.outer())
        def _():
            self.to_core(0, 3).wait_send()
            self.to_core(NEAR_CROSS, NEAR_CORE).wait_recv()


def attn_bwd_kernel(
    meta_ref, qkv_ref, p_ref, inv_ref, att_ref, datt_ref, table_ref, kback_ref, *rest,
):
    w = pl.program_id(0)
    if len(rest) == 3:
        dqkv_ref, rel_ref, bias_ref = rest
        streams = None
    else:
        fc1_ref, fc2_ref, _, dqkv_ref, rel_ref, bias_ref, sum1_ref, sum2_ref, all_ref = rest[:9]
        half = SHARD_ROWS // 2
        streams = []
        for n in range(4):
            own, *got, sems = rest[9 + 7 * n : 16 + 7 * n]

            def source(x, img, c, ref=(fc1_ref, fc2_ref)[n // 2], n=n):
                row = pl.multiple_of((2 * x + c) * SHARD_ROWS + n % 2 * half, half)
                return ref.at[pl.ds(row, half), pl.ds(img * SHARD_COLS, SHARD_COLS)]

            streams.append(Halving(source, own, got, sems, ORDERS[n % 2], half))
        ones, twos = streams[:2], streams[2:]
        back = Homeward(all_ref, all_ref, rest[37])

        def each(group, name, *args):
            def body():
                for stream in group:
                    getattr(stream, name)(*args)
            return body

        timeline(
            w,
            {
                0: [greet, each(streams, "first")],
                2: [
                    each(ones, "first_done"), each(ones, "step", 0), each(twos, "first_done"),
                    back.send_core_inner, back.send_core_outer,
                ],
                5: [each(ones, "step_done", 0), each(ones, "step", 1)],
                7: [each(ones, "step_done", 1), each(ones, "step", 2), each(twos, "step", 0)],
                10: [
                    each(ones, "step_done", 2), each(ones, "step", 3), each(twos, "step_done", 0), each(twos, "step", 1),
                    back.send_cross,
                ],
                12: [each(ones, "step_done", 3), each(twos, "step_done", 1), each(twos, "step", 2)],
            },
        )

    @pl.when(w == 0)
    def _():
        rel_ref[...] = jnp.zeros_like(rel_ref)
        bias_ref[...] = jnp.zeros_like(bias_ref)

    lane = iota((TW, LANES), 1)
    low_half = lane < 64
    onehot = kback_ref[...]
    for p in range(PAIRS):
        q = qkv_ref[:, LANES * p : LANES * p + LANES]
        k8 = qkv_ref[:, D + LANES * p : D + LANES * p + LANES]
        v = qkv_ref[:, 2 * D + LANES * p : 2 * D + LANES * p + LANES]
        cols = slice(LANES * p, LANES * p + LANES)
        da = datt_ref[:, cols].astype(F32) * inv_ref[:, cols]
        da_low = da.astype(BF16)
        prod = da_low.astype(F32) * att_ref[:, cols].astype(F32)
        keys = jnp.concatenate([k8, onehot], axis=1)
        da_t = da.T.astype(BF16)
        q_t = q.astype(F32).T.astype(BF16)
        zero = jnp.zeros_like(v)
        dqx, dv_t, dk_t = [], [], []
        for h in range(2):
            mine = low_half if h == 0 else ~low_half
            centre = jnp.sum(jnp.where(mine, prod, 0.0), axis=-1, keepdims=True)
            dp = mm_nt(da_low, jnp.where(mine, v, zero))
            e = p_ref[2 * p + h]
            ds = (e.astype(F32) * (dp - centre)).astype(BF16)
            dqx.append(mm(ds, keys))
            dv_t.append(mm(da_t[64 * h : 64 * h + 64], e))
            dk_t.append(mm(q_t[64 * h : 64 * h + 64], ds))
        dq = jnp.where(low_half, dqx[0][:, :LANES], dqx[1][:, :LANES])
        drc = jnp.where(low_half, dqx[0][:, LANES:], dqx[1][:, LANES:])
        part = lane & 63
        rows = roll_rows(jnp.where(part < 16, drc, 0.0), 1)
        cols_part = roll_cols(jnp.where((part >= 16) & (part < 32), drc, 0.0), LANES - 16)
        skew = jnp.concatenate([rows, cols_part], axis=1).astype(BF16)
        dq = dq + mm_nt(skew, table_ref[...])
        rel_ref[...] += mm(q_t, skew)
        dv = jnp.concatenate(dv_t, axis=0).T
        dk = (jnp.concatenate(dk_t, axis=0) * 0.125).T
        dqkv_ref[:, cols] = dq.astype(BF16)
        dqkv_ref[:, D + LANES * p : D + LANES * p + LANES] = dk.astype(BF16)
        dqkv_ref[:, 2 * D + LANES * p : 2 * D + LANES * p + LANES] = dv.astype(BF16)
        bias_ref[0, :, cols] += fold8(dq)
        bias_ref[1, :, cols] += fold8(dv)

    if streams:
        @pl.when(w == pl.num_programs(0) - 1)
        def _():
            sum1_ref[:half] = ones[0].result()
            sum1_ref[half:] = ones[1].result()
            each(twos, "step_done", 2)()
            each(twos, "step", 3)()
            back.finish()
            each(twos, "step_done", 3)()
            sum2_ref[:half] = twos[0].result()
            sum2_ref[half:] = twos[1].result()


def attention_backward(meta, qkv, p, inv, att, datt, table, kback, beside=()):
    cap = meta.shape[0]
    sds = jax.ShapeDtypeStruct
    anywhere = pl.BlockSpec(memory_space=pl.ANY)
    shard = (SHARD_ROWS, SHARD_COLS)
    more_specs, more_outs, scratch, extra = [], [], [], {}
    if beside:
        more_specs = [whole(shard), whole(shard), anywhere]
        more_outs = [sds(shard, F32), sds(shard, F32), sds((cap + NEAR_CORE + NEAR_CROSS, TW, D), BF16)]
        scratch = Halving.scratch(SHARD_ROWS // 2) * 4 + [pltpu.SemaphoreType.DMA((5,))]
        extra = dict(collective_id=1, has_side_effects=True)
    return pl.pallas_call(
        attn_bwd_kernel,
        input_output_aliases={10: 5} if beside else {},
        grid_spec=pltpu.PrefetchScalarGridSpec(
            num_scalar_prefetch=1,
            grid=(cap,),
            in_specs=[
                per_window(TW, 3 * D), per_window(HEADS, TW, TW), per_window(TW, D), per_window(TW, D),
                per_window(TW, D), whole((LANES, 256)), whole((TW, LANES)),
            ] + [anywhere] * len(beside),
            out_specs=[per_window(TW, 3 * D), whole((LANES, 256)), whole((2, 8, D))] + more_specs,
            scratch_shapes=scratch,
        ),
        out_shape=[sds((cap, TW, 3 * D), BF16), sds((LANES, 256), F32), sds((2, 8, D), F32)] + more_outs,
        compiler_params=pltpu.CompilerParams(vmem_limit_bytes=VMEM_LIMIT, **extra),
        cost_estimate=pl.CostEstimate(flops=60_000_000_000, bytes_accessed=80_000_000, transcendentals=0),
    )(meta, qkv, p, inv, att, datt, table, kback, *beside)


def rel_from(acc):
    def one(block):
        own = block[:64, :32] + block[64:, 64:96]
        return own[:, :RELS].T

    return one(acc[:, :LANES])[::-1], one(acc[:, LANES:])


def put_window(target, y, acc_ref, row0):
    picks = jnp.where(iota((TW, 256), 1) == target, 1.0, 0.0).astype(BF16)
    for q in range(4):
        n = 4 if q < 3 else 2
        t = slice(64 * q, 64 * q + STRIDE * n)
        part = lax.dot_general(
            picks[t, : 64 * n], y[t], (((0,), (0,)), ((), ())), preferred_element_type=F32
        )
        acc_ref[pl.ds(row0 + 4 * q, n)] += part.reshape(n, SIDE, D).astype(acc_ref.dtype)


def scatter_kernel(meta_ref, y_ref, ext_ref, acc_ref):
    w = pl.program_id(0)

    @pl.when(w == 0)
    def _():
        acc_ref[...] = jnp.zeros_like(acc_ref)

    put_window(token_target(meta_ref, w), y_ref[...], acc_ref, meta_ref[w, 0])

    @pl.when(w == pl.num_programs(0) - 1)
    def _():
        def copy(i, _):
            ext_ref[i] = acc_ref[i].astype(BF16)
            return 0
        lax.fori_loop(0, ext_ref.shape[0], copy, 0)


def scatter(meta, y, ext_rows):
    cap = meta.shape[0]
    return pl.pallas_call(
        scatter_kernel,
        grid_spec=pltpu.PrefetchScalarGridSpec(
            num_scalar_prefetch=1,
            grid=(cap,),
            in_specs=[per_window(TW, D)],
            out_specs=whole((ext_rows, SIDE, D)),
            scratch_shapes=[pltpu.VMEM((ext_rows, SIDE, D), F32)],
        ),
        out_shape=jax.ShapeDtypeStruct((ext_rows, SIDE, D), BF16),
        compiler_params=pltpu.CompilerParams(vmem_limit_bytes=VMEM_LIMIT),
        cost_estimate=pl.CostEstimate(flops=5_000_000_000, bytes_accessed=20_000_000, transcendentals=0),
    )(meta, y)


def last_kernel(
    meta_ref, dqkv_ref, wqkv_ref, x_ref, dmix_ref, gain_ref, ext_ref, sums_ref, acc_ref,
):
    w = pl.program_id(0)

    @pl.when(w == 0)
    def _():
        acc_ref[...] = jnp.zeros_like(acc_ref)
        sums_ref[...] = jnp.zeros_like(sums_ref)

    target = token_target(meta_ref, w)
    dn = jnp.zeros((TW, D), F32)
    for c in range(3):
        cols = slice(D * c, D * c + D)
        dn = dn + mm_nt(dqkv_ref[:, cols], wqkv_ref[:, cols])
    dn = jnp.where(target >= 0, dn, 0.0)
    unit, inverse = norm(x_ref[...].astype(F32))
    sums_ref[0] += fold8(dn * unit)
    sums_ref[1] += fold8(dn)
    grad = dmix_ref[...].astype(F32) + norm_back(dn, unit, inverse, gain_ref[...])
    put_window(target, grad.astype(BF16), acc_ref, meta_ref[w, 0])

    @pl.when(w == pl.num_programs(0) - 1)
    def _():
        def copy(i, _):
            ext_ref[i] = acc_ref[i].astype(BF16)
            return 0
        lax.fori_loop(0, ext_ref.shape[0], copy, 0)


def last_norm(meta, dqkv, wqkv, x, dmix, gain, ext_rows):
    cap = meta.shape[0]
    sds = jax.ShapeDtypeStruct
    return pl.pallas_call(
        last_kernel,
        grid_spec=pltpu.PrefetchScalarGridSpec(
            num_scalar_prefetch=1,
            grid=(cap,),
            in_specs=[
                per_window(TW, 3 * D), whole((D, 3 * D)), per_window(TW, D), per_window(TW, D), whole((1, D)),
            ],
            out_specs=[whole((ext_rows, SIDE, D)), whole((2, 8, D))],
            scratch_shapes=[pltpu.VMEM((ext_rows, SIDE, D), F32)],
        ),
        out_shape=[sds((ext_rows, SIDE, D), BF16), sds((2, 8, D), F32)],
        compiler_params=pltpu.CompilerParams(vmem_limit_bytes=VMEM_LIMIT),
        cost_estimate=pl.CostEstimate(flops=15_000_000_000, bytes_accessed=30_000_000, transcendentals=0),
    )(meta, dqkv, wqkv, x, dmix, gain)


class SmallSum:
    def __init__(self, mine, got_band, got_img, sems):
        self.mine, self.got, self.sems = mine, (got_band, got_img), sems

    @staticmethod
    def scratch(shape):
        return [
            pltpu.VMEM(shape, F32), pltpu.VMEM((3,) + shape, F32), pltpu.VMEM((7,) + shape, F32),
            pltpu.SemaphoreType.DMA((2, 2, 7)),
        ]

    def copies(self, k):
        return [
            pltpu.make_async_remote_copy(
                src_ref=self.mine, dst_ref=self.got[k].at[d], send_sem=self.sems.at[k, 0, d],
                recv_sem=self.sems.at[k, 1, d], device_id=device, device_id_type=MESH,
            )
            for d, device in enumerate(peers()[k])
        ]

    def send(self, k):
        for copy in self.copies(k):
            copy.start()

    def add(self, k):
        copies = self.copies(k)
        for copy in copies:
            copy.wait()
        total = self.mine[...]
        for d in range(len(copies)):
            total = total + self.got[k][d]
        self.mine[...] = total


HOME_ROWS = 8


def home_kernel(table_ref, *refs):
    arrays = len(refs) // 2
    step = pl.program_id(0)
    per_image = pl.num_programs(0) // 2
    m = step // per_image
    top, left = table_ref[m, 25], table_ref[m, 26]
    first = table_ref[m, 27] + (step - m * per_image) * HOME_ROWS
    col = iota((SIDE, GRID * STRIDE), 0) + left
    spot = iota((SIDE, GRID * STRIDE), 1)
    picks = jnp.where((spot >> 4) * WIN + (spot & 15) == col, 1.0, 0.0)
    picks = jnp.where((spot & 15) < WIN, picks, 0.0).astype(BF16)
    for i in range(HOME_ROWS):
        at = i + first + top
        r = at // WIN
        a = pl.multiple_of((at - r * WIN) * STRIDE, STRIDE)
        slots = [table_ref[m, r * GRID + c] for c in range(GRID)]
        for n in range(arrays):
            tokens = jnp.concatenate([refs[n][slot, pl.ds(a, STRIDE)] for slot in slots], axis=0)
            refs[arrays + n][0, i] = mm(picks, tokens).astype(refs[arrays + n].dtype)


def home(table, sources, dtypes, rows):
    per_image = rows // HOME_ROWS
    return pl.pallas_call(
        home_kernel,
        grid_spec=pltpu.PrefetchScalarGridSpec(
            num_scalar_prefetch=1,
            grid=(2 * per_image,),
            in_specs=[whole(a.shape) for a in sources],
            out_specs=[
                pl.BlockSpec((1, HOME_ROWS, SIDE, D), lambda w, meta: (w // per_image, w % per_image, 0, 0))
                for _ in dtypes
            ],
        ),
        out_shape=[jax.ShapeDtypeStruct((2, rows, SIDE, D), dtype) for dtype in dtypes],
        compiler_params=pltpu.CompilerParams(vmem_limit_bytes=VMEM_LIMIT),
        cost_estimate=pl.CostEstimate(flops=500_000_000, bytes_accessed=20_000_000, transcendentals=0),
    )(table, *sources)


def home_table(plan, offsets, band, band_rows):
    own = np.full((4, 2, WINDOWS), 0, np.int32)
    for b in range(4):
        for slot, (m, w) in enumerate(plan[b]):
            if w >= 0:
                own[b, m, w] = slot
        odd, cap = b % 2, len(plan[b])
        mate = plan[b ^ 1]
        sent = mate[:3] if (b ^ 1) in (0, 3) else mate[NEAR_CROSS : NEAR_CROSS + NEAR_CORE]
        for slot, (m, w) in enumerate(sent):
            own[b, m, w] = cap + slot
        if b in (1, 2):
            for slot, (m, w) in enumerate(plan[3 - b][:NEAR_CROSS]):
                own[b, m, w] = cap + NEAR_CORE + slot
    rows = jnp.asarray(own)[band]
    first = jnp.full((2, 1), band_rows, jnp.int32) * band
    return jnp.concatenate([rows, offsets.astype(jnp.int32), first, jnp.zeros((2, 4), jnp.int32)], axis=1)


def last_fused_kernel(
    meta_ref, dqkv_ref, wqkv_ref, x_ref, dmix_ref, gain_ref, q_ref, bias_ref, sums_ref, fc1_ref, rel_ref,
    all_ref, shard_ref, total_ref, rels_ref, ln_ref,
    grad_ref, ln_acc, *rest,
):
    w = pl.program_id(0)
    end = pl.num_programs(0) - 1
    half = SHARD_ROWS // 2
    streams = []
    for n, order in enumerate(ORDERS):
        own, *got, sems = rest[7 * n : 7 * n + 7]

        def source(x, img, c, n=n):
            row = pl.multiple_of((2 * x + c) * SHARD_ROWS + n * half, half)
            return q_ref.at[img, pl.ds(row, half)]

        streams.append(Halving(source, own, got, sems, order, half))
    one, two = streams
    rest = rest[14:]
    small, rel, ln = [SmallSum(*rest[4 * n : 4 * n + 4]) for n in range(3)]
    back = Homeward(grad_ref, all_ref, rest[12])

    def start():
        greet()
        one.first()
        two.first()

    def prepare():
        for r in range(2):
            small.mine[r : r + 1] = jnp.sum(bias_ref[r], axis=0, keepdims=True)
        for r in range(4):
            small.mine[2 + r : 3 + r] = jnp.sum(sums_ref[r], axis=0, keepdims=True)
            small.mine[6 + r : 7 + r] = jnp.sum(fc1_ref[:, D * r : D * r + D], axis=0, keepdims=True)
        small.mine[10:] = jnp.zeros((6, D), F32)
        rel.mine[...] = rel_ref[:64] + pltpu.roll(rel_ref[64:], 192, 1)
        small.send(0)
        rel.send(0)
        ln_acc[...] = jnp.zeros_like(ln_acc)

    def done(k):
        one.step_done(k)
        two.step_done(k)

    def step(k):
        one.step(k)
        two.step(k)

    def first_done():
        one.first_done()
        two.first_done()
        step(0)

    def middle():
        small.add(0)
        rel.add(0)
        small.send(1)
        rel.send(1)

    def finish():
        small.add(1)
        rel.add(1)
        total_ref[...] = small.mine[...]
        rels_ref[...] = rel.mine[...]

    timeline(
        w,
        {
            0: [start, prepare],
            2: [first_done],
            3: [middle, back.send_core_outer],
            6: [lambda: done(0), lambda: step(1), finish],
            8: [lambda: done(1), lambda: step(2), back.send_cross],
            12: [lambda: done(2), lambda: step(3), back.send_core_inner],
        },
    )

    target = token_target(meta_ref, w)
    dn = jnp.zeros((TW, D), F32)
    for c in range(3):
        cols = slice(D * c, D * c + D)
        dn = dn + mm_nt(dqkv_ref[:, cols], wqkv_ref[:, cols])
    dn = jnp.where(target >= 0, dn, 0.0)
    unit, inverse = norm(x_ref[...].astype(F32))
    ln_acc[0] += fold8(dn * unit)
    ln_acc[1] += fold8(dn)
    grad = dmix_ref[...].astype(F32) + norm_back(dn, unit, inverse, gain_ref[...])
    grad_ref[w] = grad.astype(BF16)

    @pl.when(w == end)
    def _():
        back.keep().start()
        ln.mine[0:1] = jnp.sum(ln_acc[0], axis=0, keepdims=True)
        ln.mine[1:2] = jnp.sum(ln_acc[1], axis=0, keepdims=True)
        ln.mine[2:] = jnp.zeros((6, D), F32)
        ln.send(0)
        done(3)
        ln.add(0)
        ln.send(1)
        shard_ref[:half] = one.result()
        shard_ref[half:] = two.result()
        back.keep().wait()
        back.finish()
        ln.add(1)
        ln_ref[...] = ln.mine[...]


def last_fused(meta, dqkv, wqkv, x, dmix, gain, q_grad, bias_sums, sums, fc1_sum, rel_acc):
    cap = meta.shape[0]
    sds = jax.ShapeDtypeStruct
    half = SHARD_ROWS // 2
    anywhere = pl.BlockSpec(memory_space=pl.ANY)
    sums_out = [((SHARD_ROWS, SHARD_COLS), F32), ((16, D), F32), ((64, 256), F32), ((8, D), F32)]
    return pl.pallas_call(
        last_fused_kernel,
        grid_spec=pltpu.PrefetchScalarGridSpec(
            num_scalar_prefetch=1,
            grid=(cap,),
            in_specs=[
                per_window(TW, 3 * D), whole((D, 3 * D)), per_window(TW, D), per_window(TW, D), whole((1, D)),
                anywhere, whole((2, 8, D)), whole((4, 8, D)), whole((8, FF)), whole((LANES, 256)),
            ],
            out_specs=[anywhere] + [whole(shape) for shape, _ in sums_out],
            scratch_shapes=[pltpu.VMEM((cap, TW, D), BF16), pltpu.VMEM((2, 8, D), F32)]
            + Halving.scratch(half) * 2
            + SmallSum.scratch((16, D)) + SmallSum.scratch((64, 256)) + SmallSum.scratch((8, D))
            + [pltpu.SemaphoreType.DMA((5,))],
        ),
        out_shape=[sds((cap + NEAR_CORE + NEAR_CROSS, TW, D), BF16)] + [sds(shape, dtype) for shape, dtype in sums_out],
        compiler_params=pltpu.CompilerParams(vmem_limit_bytes=VMEM_LIMIT, collective_id=2, has_side_effects=True),
        cost_estimate=pl.CostEstimate(flops=20_000_000_000, bytes_accessed=50_000_000, transcendentals=0),
    )(meta, dqkv, wqkv, x, dmix, gain, q_grad, bias_sums, sums, fc1_sum, rel_acc)


def window_plan(images, bands):
    lists = [[] for _ in range(bands)]
    if images == 2 and bands == 4:
        spans = (
            ((0, 5, 8), (0, 0, 5), (1, 0, 5)),
            ((0, 10, 15), (0, 8, 10), (1, 5, 10)),
            ((1, 10, 15), (1, 15, 17), (0, 15, 20)),
            ((1, 17, 20), (1, 20, 25), (0, 20, 25)),
        )
        lists = [[(m, w) for m, first, last in row for w in range(first, last)] for row in spans]
    else:
        cuts = [
            [(WINDOWS * b + (bands - 1 if m % 2 else 0)) // bands for b in range(bands + 1)] for m in range(images)
        ]
        for m in range(images):
            for b in range(bands):
                lists[b] += [(m, w) for w in range(cuts[m][b], min(cuts[m][b + 1], WINDOWS))]
    cap = max(len(item) for item in lists)
    return np.array([item + [(0, -1)] * (cap - len(item)) for item in lists], np.int32)


HALO = 12


def near(images, bands, band_rows):
    return images == 2 and bands == 4 and band_rows == 16


CORE = [(0, 1), (1, 0), (2, 3), (3, 2)]
CROSS = [(1, 2), (2, 1)]


def extend(rows, band):
    images, band_rows = rows.shape[:2]
    if not near(images, lax.axis_size("band"), band_rows):
        full = lax.all_gather(rows, "band", axis=1, tiled=True)
        return jnp.pad(full, ((0, 0), (6, 6), (0, 0), (0, 0)))
    odd = band % 2 == 1
    top, bottom = rows[:, :HALO], rows[:, -HALO:]
    from_core = lax.ppermute(jnp.where(odd, top, bottom), "band", CORE)
    from_cross = lax.ppermute(jnp.where(odd, bottom[1], top[0]), "band", CROSS)
    zero = jnp.zeros_like(from_cross)
    above = jnp.where(odd, from_core, jnp.stack([zero, from_cross]))
    below = jnp.where(odd, jnp.stack([from_cross, zero]), from_core)
    return jnp.concatenate([above, rows, below], axis=1)


def collect(ext, band, images, band_rows):
    if not near(images, lax.axis_size("band"), band_rows):
        return lax.psum_scatter(ext[:, 6:-6], "band", scatter_dimension=1, tiled=True).astype(F32)
    odd = band % 2 == 1
    above, below = ext[:, :HALO], ext[:, -HALO:]
    from_core = lax.ppermute(jnp.where(odd, above, below), "band", CORE).astype(F32)
    from_cross = lax.ppermute(jnp.where(odd, below[0], above[1]), "band", CROSS).astype(F32)
    zero = jnp.zeros_like(from_cross)
    top = jnp.where(odd, from_core, jnp.stack([from_cross, zero]))
    bottom = jnp.where(odd, jnp.stack([zero, from_cross]), from_core)
    own = ext[:, HALO:-HALO].astype(F32)
    rest = band_rows - HALO
    return own + jnp.pad(top, ((0, 0), (0, rest), (0, 0), (0, 0))) + jnp.pad(bottom, ((0, 0), (rest, 0), (0, 0), (0, 0)))


def shards(
    image_tokens, pad_offsets, ln1_gain, ln1_bias, w_qkv, q_bias, v_bias, rel_rows, rel_cols, w_proj, proj_bias,
    ln2_gain, ln2_bias, w_fc1, fc1_bias, w_fc2, fc2_bias, out_grad,
):
    images, band_rows = image_tokens.shape[:2]
    bands, groups = lax.axis_size("band"), lax.axis_size("img")
    band, group = lax.axis_index("band"), lax.axis_index("img")
    axes = ("img", "band")

    part, wide = w_qkv.shape
    small = jnp.concatenate(
        [
            ln1_gain, ln1_bias, q_bias, v_bias, proj_bias, ln2_gain, ln2_bias, fc2_bias, fc1_bias,
            rel_rows.reshape(-1), rel_cols.reshape(-1),
        ]
    )
    small_rows = -(-small.shape[0] // (wide * 8)) * 8
    small = jnp.pad(small, (0, small_rows * wide - small.shape[0])).reshape(small_rows, wide)
    first = lax.all_gather(jnp.concatenate([w_qkv, small], axis=0), axes, axis=0, tiled=False)
    first = first.reshape(groups, bands, part + small_rows, wide)
    second = lax.all_gather(
        jnp.concatenate([w_fc1, w_fc2.T, w_proj], axis=1), axes, axis=0, tiled=False
    ).reshape(groups, bands * part, -1)
    wqkv = first[:, :, :part].transpose(1, 2, 0, 3).reshape(D, 3 * D)
    tail = first[:, :, part:].reshape(groups, bands, small_rows * wide)
    share = D // groups
    vectors = tail[:, 0, : 8 * share].reshape(groups, 8, share).transpose(1, 0, 2).reshape(8, 1, D).astype(F32)
    fc1_shift = tail[:, 0, 8 * share : 8 * share + FF // groups].reshape(1, FF).astype(F32)
    at = 8 * share + FF // groups
    rels = tail[0, :, at : at + 2 * RELS * (HEAD // bands)].reshape(bands, 2, RELS, HEAD // bands)
    rels = rels.transpose(1, 2, 0, 3).reshape(2, RELS, HEAD)
    gain1, shift1, qb, vb, pb, gain2, shift2, b2 = [vectors[i] for i in range(8)]
    bias = jnp.concatenate([qb, jnp.zeros_like(qb), vb], axis=1)
    inner = FF // groups
    ff = second[:, :, : 2 * inner]
    wproj = second[:, :, 2 * inner :].transpose(1, 0, 2).reshape(D, D)

    plan = jnp.asarray(window_plan(images, bands))[band]
    image, window = plan[:, 0], plan[:, 1]
    close = near(images, bands, band_rows)
    fused = close and groups == 8
    ext_per = band_rows + 2 * HALO if close else bands * band_rows + 12
    base = band_rows * band - HALO if close else -6
    live = window >= 0
    spot = jnp.maximum(window, 0)
    offsets = pad_offsets[image]
    row = spot // GRID * WIN - offsets[:, 0]
    col = spot % GRID * WIN - offsets[:, 1]
    meta = jnp.stack(
        [jnp.where(live, image * ext_per + row - base, HALO), col, row, live.astype(jnp.int32)], axis=1
    ).astype(jnp.int32)
    cap = meta.shape[0]
    ext_rows = images * ext_per

    ka, kb, kback = key_constants()
    ext = extend(image_tokens, band).reshape(ext_rows, SIDE, D)
    x, normed1, qkv, probs, inv, att = attention_forward(
        meta, ext, gain1, shift1, wqkv, bias, rel_table(rels[0], rels[1], True), ka, kb
    )
    gext = extend(out_grad, band).reshape(ext_rows, SIDE, D)
    out_win, g, normed2, act, d_pre, d_mixed, d_att, sums, sum_fc1 = feed_forward(
        meta, gext, x, att, wproj, pb, gain2, shift2, ff, fc1_shift, b2, NEAR_CORE + NEAR_CROSS if fused else 0
    )
    def flat(a):
        return a.reshape(cap * TW, a.shape[-1])

    def weight_grad(left, right):
        return jnp.einsum("td,te->de", flat(left), flat(right), preferred_element_type=F32).astype(BF16)

    d_fc2 = weight_grad(g, act)
    d_fc1 = weight_grad(normed2, d_pre)
    d_proj = weight_grad(att, d_mixed)
    d_qkv, rel_acc, bias_sums, *done = attention_backward(
        meta, qkv, probs, inv, att, d_att, rel_table(rels[0], rels[1], False), kback,
        (d_fc1, d_fc2, out_win) if fused else (),
    )
    d_wqkv = weight_grad(normed1, d_qkv)

    if fused:
        q_grad = jnp.concatenate(
            [d_wqkv.reshape(D, groups, wide), d_proj.reshape(D, groups, share)], axis=2
        ).transpose(1, 0, 2)
        g_fc1, g_fc2, all_out = done
        all_grad, q_shard, total, rel_total, ln_total = last_fused(
            meta, d_qkv, wqkv, x, d_mixed, gain1, q_grad, bias_sums, sums, sum_fc1, rel_acc
        )
        output, input_grad = home(
            home_table(window_plan(images, bands), pad_offsets, band, band_rows), (all_out, all_grad), (BF16, F32),
            band_rows,
        )
        g_qkv, g_proj = q_shard[:, :wide], q_shard[:, wide:]
        ln_total = ln_total[:2]
        bias_total, sum_total, fc1_total = total[:2], total[2:6], total[6:10].reshape(FF)
        own = rel_total.reshape(HEAD, 2, LANES)[:, :, :RELS].transpose(1, 2, 0)
        d_rel_rows, d_rel_cols = own[0][::-1], own[1]
    else:
        out_ext = scatter(meta, out_win, ext_rows).reshape(images, ext_per, SIDE, D)
        output = collect(out_ext, band, images, band_rows).astype(BF16)
        in_ext, sums1 = last_norm(meta, d_qkv, wqkv, x, d_mixed, gain1, ext_rows)
        input_grad = collect(in_ext.reshape(images, ext_per, SIDE, D), band, images, band_rows)

        def reduce(grad):
            grad = lax.psum_scatter(grad, "img", scatter_dimension=1, tiled=True)
            return lax.psum_scatter(grad, "band", scatter_dimension=0, tiled=True).astype(F32)

        g_fc1, g_fc2, g_qkv, g_proj = reduce(d_fc1), reduce(d_fc2), reduce(d_wqkv), reduce(d_proj)
        ln_total, bias_total, sum_total, fc1_total, d_rel_rows, d_rel_cols = lax.psum(
            (jnp.sum(sums1, 1), jnp.sum(bias_sums, 1), jnp.sum(sums, 1), jnp.sum(sum_fc1, 0)) + rel_from(rel_acc), axes
        )

    def img_share(vector):
        n = vector.shape[0] // groups
        return lax.dynamic_slice_in_dim(vector, group * n, n, 0)

    def band_share(table):
        n = table.shape[1] // bands
        return lax.dynamic_slice_in_dim(table, band * n, n, 1)

    return (
        output,
        input_grad,
        img_share(ln_total[0]),
        img_share(ln_total[1]),
        g_qkv,
        img_share(bias_total[0]),
        img_share(bias_total[1]),
        band_share(d_rel_rows),
        band_share(d_rel_cols),
        g_proj,
        img_share(sum_total[3]),
        img_share(sum_total[1]),
        img_share(sum_total[2]),
        g_fc1,
        img_share(fc1_total),
        g_fc2.T,
        img_share(sum_total[0]),
    )


def solution(mesh):
    tokens, vector, matrix = P("img", "band", None, None), P("img"), P("band", "img")
    table, wide = P(None, "band"), P("img", "band")
    return jax.shard_map(
        shards,
        mesh=mesh,
        in_specs=(
            tokens, P("img", None), vector, vector, matrix, vector, vector, table, table, matrix, vector, vector,
            vector, matrix, vector, wide, vector, tokens,
        ),
        out_specs=(
            tokens, tokens, vector, vector, matrix, vector, vector, table, table, matrix, vector, vector, vector,
            matrix, vector, wide, vector,
        ),
        check_vma=False,
    )
```

```python
import functools
import numpy as np
import jax
import jax.numpy as jnp
from jax import lax
from jax.sharding import PartitionSpec as P
from jax.experimental import pallas as pl
from jax.experimental.pallas import tpu as pltpu

D = 768
HEADS = 12
HEAD = 64
FF = 3072
WIN = 14
SIDE = 64
GRID = 5
WINDOWS = 25
RELS = 27
STRIDE = 16
TW = WIN * STRIDE
PAIRS = HEADS // 2
LANES = 128
EPSILON = 1e-06
F32 = jnp.float32
BF16 = jnp.bfloat16
VMEM_LIMIT = 60 * 1024 * 1024
NT = (((1,), (1,)), ((), ()))


def mm(a, b):
    return jnp.dot(a, b, preferred_element_type=F32)


def mm_nt(a, b):
    return lax.dot_general(a, b, NT, preferred_element_type=F32)


def iota(shape, dim):
    return lax.broadcasted_iota(jnp.int32, shape, dim)


def token_target(meta_ref, w):
    t = iota((TW, 1), 0)
    a, b = t >> 4, t & 15
    col = meta_ref[w, 1] + b
    row = meta_ref[w, 2] + a
    ok = (b < WIN) & (col >= 0) & (col < SIDE) & (row >= 0) & (row < SIDE) & (meta_ref[w, 3] > 0)
    return jnp.where(ok, ((a & 3) << 6) + col, -1)


def take_window(target, rows_ref):
    picks = jnp.where(iota((TW, 256), 1) == target, 1.0, 0.0).astype(BF16)
    parts = []
    for q in range(3):
        src = rows_ref[4 * q : 4 * q + 4].reshape(256, D)
        parts.append(mm(picks[64 * q : 64 * q + 64], src))
    src = rows_ref[12:14].reshape(128, D)
    parts.append(mm(picks[192:224, :128], src))
    return jnp.concatenate(parts, axis=0)


def norm(values):
    mean = jnp.sum(values, axis=-1, keepdims=True) * (1.0 / D)
    centred = values - mean
    inverse = lax.rsqrt(jnp.sum(centred * centred, axis=-1, keepdims=True) * (1.0 / D) + EPSILON)
    return centred * inverse, inverse


def norm_back(grad, unit, inverse, gain):
    s = grad * gain
    m1 = jnp.sum(s, axis=-1, keepdims=True) * (1.0 / D)
    m2 = jnp.sum(s * unit, axis=-1, keepdims=True) * (1.0 / D)
    return inverse * (s - m1 - unit * m2)


def fold8(x):
    return jnp.sum(x.reshape(x.shape[0] // 8, 8, x.shape[1]), axis=0)


def roll_rows(x, sign):
    out = []
    for a in range(WIN):
        piece = x[STRIDE * a : STRIDE * a + STRIDE]
        by = (sign * (13 - a)) % LANES
        out.append(pltpu.roll(piece, by, 1) if by else piece)
    return jnp.concatenate(out, axis=0)


def roll_cols(x, first):
    out = []
    for a in range(WIN):
        piece = x[STRIDE * a : STRIDE * a + STRIDE]
        out.append(pltpu.roll(piece, first, 1, stride=1, stride_axis=0))
    return jnp.concatenate(out, axis=0)


def attn_fwd_pair(q, k8, v, table, keys_a, keys_b, p_ref, p):
    lane = iota((TW, LANES), 1)
    low_half = lane < 64
    rc = mm(q, table)
    both = jnp.where((lane & 31) < 16, roll_rows(rc[:, :LANES], -1), roll_cols(rc[:, LANES:], 3))
    high = both.astype(BF16)
    rest = (both - high.astype(F32)).astype(BF16)
    extra = jnp.where((lane & 63) < 32, high, rest)
    extra = jnp.where((lane & 63) == 14, jnp.ones_like(extra), extra)
    left = jnp.concatenate([q, extra], axis=1)
    zero = jnp.zeros_like(k8)
    wide_v = jnp.concatenate([v, jnp.ones_like(v)], axis=1)
    outs, invs = [], []
    for h in range(2):
        keys = jnp.concatenate(
            [jnp.where(low_half if h == 0 else ~low_half, k8, zero), (keys_a, keys_b)[h]], axis=1
        )
        s = mm_nt(left, keys)
        e = jnp.exp(s - jnp.max(s, axis=-1, keepdims=True)).astype(BF16)
        p_ref[2 * p + h] = e
        o = mm(e, wide_v)
        inv = 1.0 / o[:, LANES:]
        outs.append(o[:, :LANES] * inv)
        invs.append(inv)
    att = jnp.where(low_half, outs[0], outs[1]).astype(BF16)
    inv = jnp.where(low_half, invs[0], invs[1])
    return att, inv


def fwd_kernel(
    meta_ref, rows_ref, grows_ref, vec_ref, wqkv_ref, table_ref, ka_ref, kb_ref,
    x_ref, g_ref, n_ref, qkv_ref, p_ref, inv_ref, att_ref, *weights,
):
    w = pl.program_id(0)
    if weights:
        blocks_ref, (wqkv_ref, wproj_ref) = wqkv_ref, weights

        @pl.when(w == 0)
        def _():
            share = D // blocks_ref.shape[0]
            for b in range(blocks_ref.shape[1]):
                rows = slice(SHARD_ROWS * b, SHARD_ROWS * b + SHARD_ROWS)
                parts = [blocks_ref[i, b, :SHARD_ROWS] for i in range(blocks_ref.shape[0])]
                wqkv_ref[rows] = jnp.concatenate([part[:, : 3 * share] for part in parts], axis=1)
                wproj_ref[rows] = jnp.concatenate([part[:, 3 * share :] for part in parts], axis=1)

    target = token_target(meta_ref, w)
    x = take_window(target, rows_ref)
    x_ref[...] = x.astype(BF16)
    g_ref[...] = take_window(target, grows_ref).astype(BF16)
    unit, _ = norm(x)
    normed = jnp.where(target >= 0, unit * vec_ref[0:1] + vec_ref[1:2], 0.0).astype(BF16)
    n_ref[...] = normed
    for c in range(9):
        cols = slice(256 * c, 256 * c + 256)
        y = mm(normed, wqkv_ref[:, cols])
        if c < 3:
            y = y + vec_ref[2:3, cols]
        elif c >= 6:
            y = y + vec_ref[3:4, 256 * (c - 6) : 256 * (c - 6) + 256]
        else:
            y = y.astype(BF16).astype(F32) * 0.125
        qkv_ref[:, cols] = y.astype(BF16)

    for p in range(PAIRS):
        a = slice(LANES * p, LANES * p + LANES)
        q = qkv_ref[:, LANES * p : LANES * p + LANES]
        k8 = qkv_ref[:, D + LANES * p : D + LANES * p + LANES]
        v = qkv_ref[:, 2 * D + LANES * p : 2 * D + LANES * p + LANES]
        att, inv = attn_fwd_pair(q, k8, v, table_ref[...], ka_ref[...], kb_ref[...], p_ref, p)
        att_ref[:, a] = att
        inv_ref[:, a] = inv


def rows_spec(rows):
    return pl.BlockSpec(
        (pl.Element(rows), pl.Element(SIDE), pl.Element(D)), lambda w, meta: (meta[w, 0], 0, 0)
    )


def whole(shape, buffers=1):
    zeros = (0,) * len(shape)
    return pl.BlockSpec(shape, lambda w, meta: zeros, pipeline_mode=pl.Buffered(buffers))


def per_window(*tail):
    zeros = (0,) * len(tail)
    return pl.BlockSpec((None,) + tail, lambda w, meta: (w,) + zeros)


def key_constants():
    t = np.arange(TW)
    kr, kc = t >> 4, t & 15
    real = kc < WIN
    base = np.zeros((TW, 64), np.float32)
    for off in (0, 32):
        base[t[real], off + kr[real]] = 1.0
        base[t[real], off + 16 + kc[real]] = 1.0
    back = np.zeros_like(base)
    back[t[real], kr[real]] = 1.0
    back[t[real], 16 + 13 - kc[real]] = 1.0
    base[~real, 14] = -1e30
    none = np.zeros_like(base)
    ka = np.concatenate([base, none], 1)
    kb = np.concatenate([none, base], 1)
    back = np.concatenate([back, back], 1)
    return jnp.asarray(ka, BF16), jnp.asarray(kb, BF16), jnp.asarray(back, BF16)


def rel_table(rel_rows, rel_cols, forward):
    def wide(rel):
        turned = jnp.pad(rel.T, ((0, 0), (0, 32 - RELS)))
        twice = jnp.concatenate([turned, turned], axis=1)
        none = jnp.zeros_like(twice)
        return jnp.concatenate(
            [jnp.concatenate([twice, none], 1), jnp.concatenate([none, twice], 1)], 0
        )

    return jnp.concatenate([wide(rel_rows[::-1]), wide(rel_cols[::-1] if forward else rel_cols)], axis=1)


def attention_forward(meta, ext, gext, vectors, wqkv, table, ka, kb):
    cap = meta.shape[0]
    weights = [(D, 3 * D), (D, D)] if wqkv.ndim == 4 else []
    sds = jax.ShapeDtypeStruct
    return pl.pallas_call(
        fwd_kernel,
        grid_spec=pltpu.PrefetchScalarGridSpec(
            num_scalar_prefetch=1,
            grid=(cap,),
            in_specs=[
                rows_spec(WIN), rows_spec(WIN), whole((8, D)), whole(wqkv.shape),
                whole((LANES, 256)), whole((TW, LANES)), whole((TW, LANES)),
            ],
            out_specs=[
                per_window(TW, D), per_window(TW, D), per_window(TW, D), per_window(TW, 3 * D),
                per_window(HEADS, TW, TW), per_window(TW, D), per_window(TW, D),
            ] + [whole(shape) for shape in weights],
        ),
        out_shape=[
            sds((cap, TW, D), BF16), sds((cap, TW, D), BF16), sds((cap, TW, D), BF16), sds((cap, TW, 3 * D), BF16),
            sds((cap, HEADS, TW, TW), BF16), sds((cap, TW, D), F32), sds((cap, TW, D), BF16),
        ] + [sds(shape, BF16) for shape in weights],
        compiler_params=pltpu.CompilerParams(vmem_limit_bytes=VMEM_LIMIT),
        cost_estimate=pl.CostEstimate(flops=40_000_000_000, bytes_accessed=80_000_000, transcendentals=8_000_000),
    )(meta, ext, gext, vectors, wqkv, table, ka, kb)


def phi_parts(u):
    e = jnp.exp(u * u * -0.5)
    t = 1.0 / (1.0 + (0.3275911 * 0.7071067811865476) * jnp.abs(u))
    poly = t * (0.254829592 + t * (-0.284496736 + t * (1.421413741 + t * (-1.453152027 + t * 1.061405429))))
    tail = 0.5 * poly * e
    return jnp.where(u >= 0, 1.0 - tail, tail), e * 0.3989422804014327


def mlp_kernel(
    g_ref, x_ref, att_ref, wproj_ref, vec_ref, ff_ref, b1_ref,
    out_ref, n2_ref, act_ref, dpre_ref, dmix_ref, datt_ref, sums_ref, sum1_ref,
    acc_ref, dn_ref,
):
    @pl.when(pl.program_id(0) == 0)
    def _():
        sums_ref[...] = jnp.zeros_like(sums_ref)
        sum1_ref[...] = jnp.zeros_like(sum1_ref)

    gb = g_ref[...]
    g = gb.astype(F32)
    sums_ref[0] += fold8(g)
    hidden = x_ref[...].astype(F32) + mm(att_ref[...], wproj_ref[...]) + vec_ref[4:5]
    unit, inverse = norm(hidden)
    n2 = (unit * vec_ref[5:6] + vec_ref[6:7]).astype(BF16)
    n2_ref[...] = n2
    acc_ref[...] = hidden + vec_ref[7:8]
    parts, inner = ff_ref.shape[0], ff_ref.shape[2] // 2
    join = max(1, 768 // inner)
    chunk = inner * join
    for c in range(parts // join):
        cols = slice(chunk * c, chunk * c + chunk)
        blocks = range(join * c, join * c + join)
        w1 = jnp.concatenate([ff_ref[i, :, :inner] for i in blocks], axis=1)
        w2t = jnp.concatenate([ff_ref[i, :, inner:] for i in blocks], axis=1)
        u = mm(n2, w1) + b1_ref[:, cols]
        dact = mm(gb, w2t)
        cdf, pdf = phi_parts(u)
        act = (u * cdf).astype(BF16)
        act_ref[:, cols] = act
        acc_ref[...] += mm_nt(act, w2t)
        dpre32 = dact * (cdf + u * pdf)
        dpre = dpre32.astype(BF16)
        dpre_ref[:, cols] = dpre
        sum1_ref[:, cols] += fold8(dpre32)
        step = mm_nt(dpre, w1)
        if c == 0:
            dn_ref[...] = step
        else:
            dn_ref[...] += step
    out_ref[...] = acc_ref[...].astype(BF16)
    dn = dn_ref[...]
    sums_ref[1] += fold8(dn * unit)
    sums_ref[2] += fold8(dn)
    dh = g + norm_back(dn, unit, inverse, vec_ref[5:6])
    dmix = dh.astype(BF16)
    dmix_ref[...] = dmix
    sums_ref[3] += fold8(dh)
    datt_ref[...] = mm_nt(dmix, wproj_ref[...]).astype(BF16)


def tile_rows(rows):
    return next(t for t in (416, 448, 224) if rows % t == 0)


def feed_forward(g, x, att, wproj, vectors, ff, b1, spare):
    cap = g.shape[0]
    rows = cap * TW
    tile = tile_rows(rows)
    sds = jax.ShapeDtypeStruct

    def tiled(width):
        return pl.BlockSpec((tile, width), lambda i: (i, 0))

    def kept(shape):
        zeros = (0,) * len(shape)
        return pl.BlockSpec(shape, lambda i: zeros, pipeline_mode=pl.Buffered(1))

    out, *rest = pl.pallas_call(
        mlp_kernel,
        grid=(rows // tile,),
        in_specs=[
            tiled(D), tiled(D), tiled(D), kept((D, D)), kept((8, D)), kept(ff.shape), kept((1, FF)),
        ],
        out_specs=[tiled(D), tiled(D), tiled(FF), tiled(FF), tiled(D), tiled(D), kept((4, 8, D)), kept((8, FF))],
        scratch_shapes=[pltpu.VMEM((tile, D), F32), pltpu.VMEM((tile, D), F32)],
        out_shape=[
            sds((rows + spare * TW, D), BF16), sds((rows, D), BF16), sds((rows, FF), BF16), sds((rows, FF), BF16),
            sds((rows, D), BF16), sds((rows, D), BF16), sds((4, 8, D), F32), sds((8, FF), F32),
        ],
        compiler_params=pltpu.CompilerParams(vmem_limit_bytes=VMEM_LIMIT),
        cost_estimate=pl.CostEstimate(flops=60_000_000_000, bytes_accessed=80_000_000, transcendentals=8_000_000),
    )(g.reshape(rows, D), x.reshape(rows, D), att.reshape(rows, D), wproj, vectors, ff, b1)
    return out.reshape(cap + spare, TW, D), rest[0], rest[1], rest[2], *[a.reshape(cap, TW, D) for a in rest[3:5]], *rest[5:]


MESH = pl.DeviceIdType.MESH
SHARD_ROWS = 192
SHARD_COLS = 384


def place():
    img, band = lax.axis_index("img"), lax.axis_index("band")
    return {"zh": img // 4, "zl": img // 2 % 2, "y": img % 2, "x": band // 2, "c": band % 2}


def partner(dim):
    img, band = lax.axis_index("img"), lax.axis_index("band")
    at = place()[dim]
    step = {"zh": 4, "zl": 2, "y": 1, "x": 2, "c": 1}[dim]
    move = step - 2 * step * at
    return (img, band + move) if dim in ("x", "c") else (img + move, band)


def peers():
    img, band = lax.axis_index("img"), lax.axis_index("band")
    return [(img, (band + d) % 4) for d in range(1, 4)], [((img + d) % 8, band) for d in range(1, 8)]


def greet():
    barrier = pltpu.get_barrier_semaphore()
    near_by, far = peers()
    for device in near_by + far:
        pl.semaphore_signal(barrier, inc=1, device_id=device, device_id_type=MESH)
    pl.semaphore_wait(barrier, 10)


class Halving:
    AXES = ("x", "zh", "zl", "y")

    def __init__(self, source, own, got, sems, order, rows):
        self.source, self.own, self.got, self.sems, self.order, self.rows = source, own, got, sems, order, rows
        self.at = place()

    @staticmethod
    def scratch(rows):
        shapes = [(2, 2, 2, 2), (2, 2, 2, 2), (2, 2, 2), (2, 2), (2,), (1,)]
        return [pltpu.VMEM(s + (rows, SHARD_COLS), BF16) for s in shapes] + [pltpu.SemaphoreType.DMA((11,))]

    def first(self):
        c = self.at["c"]
        send, recv, local = self.sems.at[0], self.sems.at[1], self.sems.at[10]
        for x in range(2):
            for img in range(8):
                spot = (x, img // 4, img // 2 % 2, img % 2)
                pltpu.make_async_remote_copy(
                    src_ref=self.source(x, img, 1 - c), dst_ref=self.got[0].at[spot], send_sem=send, recv_sem=recv,
                    device_id=partner("c"), device_id_type=MESH,
                ).start()
                pltpu.make_async_copy(self.source(x, img, c), self.own.at[spot], local).start()

    def first_done(self):
        send, recv, local = self.sems.at[0], self.sems.at[1], self.sems.at[10]
        whole = pltpu.make_async_remote_copy(
            src_ref=self.got[0], dst_ref=self.got[0], send_sem=send, recv_sem=recv,
            device_id=partner("c"), device_id_type=MESH,
        )
        whole.wait_send()
        whole.wait_recv()
        pltpu.make_async_copy(self.got[0], self.own, local).wait()

        def add(i, _):
            spot = (i // 8, i // 4 % 2, i // 2 % 2, i % 2)
            self.own[spot] = (self.own[spot].astype(F32) + self.got[0][spot].astype(F32)).astype(BF16)
            return 0

        lax.fori_loop(0, 16, add, 0)

    def index(self, k, dim=None):
        spot = []
        for axis in self.AXES:
            if axis == dim:
                spot.append(1 - self.at[axis])
            elif axis in self.order[:k]:
                spot.append(self.at[axis])
            else:
                spot.append(slice(None))
        return tuple(spot)

    def copy(self, k):
        dim = self.order[k]
        src = self.own.at[self.index(k, dim)]
        dst = self.got[k + 1].at[0] if k == 3 else self.got[k + 1]
        return pltpu.make_async_remote_copy(
            src_ref=src, dst_ref=dst, send_sem=self.sems.at[2 + 2 * k], recv_sem=self.sems.at[3 + 2 * k],
            device_id=partner(dim), device_id_type=MESH,
        )

    def step(self, k):
        self.copy(k).start()

    def step_done(self, k):
        self.copy(k).wait()
        done = self.order[: k + 1]
        free = [axis for axis in self.AXES if axis not in done]
        count = 2 ** len(free)

        def add(i, _):
            bits = {axis: (i // 2 ** (len(free) - 1 - j)) % 2 for j, axis in enumerate(free)}
            spot = tuple(bits[axis] if axis in bits else self.at[axis] for axis in self.AXES)
            self.own[spot] = (self.own[spot].astype(F32) + self.got[k + 1][tuple(bits[axis] for axis in free)].astype(F32)).astype(BF16)
            return 0

        if k < 3:
            lax.fori_loop(0, count, add, 0)

    def result(self):
        spot = tuple(self.at[axis] for axis in self.AXES)
        return self.own[spot].astype(F32) + self.got[4][0].astype(F32)


ORDERS = (("x", "y", "zh", "zl"), ("y", "x", "zh", "zl"))


def wide_source(ref, part):
    half = SHARD_ROWS // 2

    def source(x, img, c):
        row = pl.multiple_of((2 * x + c) * SHARD_ROWS + part * half, half)
        return ref.at[pl.ds(row, half), pl.ds(img * SHARD_COLS, SHARD_COLS)]

    return source


def each(group, name, *args):
    def body():
        for stream in group:
            getattr(stream, name)(*args)

    return body


def timeline(w, moments):
    for when, bodies in moments.items():
        @pl.when(w == when)
        def _(bodies=bodies):
            for body in bodies:
                body()


NEAR_CORE = 7
NEAR_CROSS = 5
CROSS_ROWS = 160


class Homeward:
    def __init__(self, windows, everything, sems):
        self.windows, self.all, self.sems = windows, everything, sems
        self.cap = everything.shape[0] - NEAR_CORE - NEAR_CROSS
        self.band = lax.axis_index("band")

    def inner(self):
        return (self.band == 1) | (self.band == 2)

    def outer(self):
        return (self.band == 0) | (self.band == 3)

    def keep(self):
        return pltpu.make_async_copy(self.windows, self.all.at[pl.ds(0, self.cap)], self.sems.at[4])

    def to_core(self, first, count):
        return pltpu.make_async_remote_copy(
            src_ref=self.windows.at[pl.ds(first, count)], dst_ref=self.all.at[pl.ds(self.cap, count)],
            send_sem=self.sems.at[0], recv_sem=self.sems.at[1], device_id=partner("c"), device_id_type=MESH,
        )

    def to_cross(self, sending):
        img = lax.axis_index("img")
        skip = (2 - self.band) if sending else (self.band - 1)
        rows = pl.ds(pl.multiple_of(skip * (TW - CROSS_ROWS), TW - CROSS_ROWS), CROSS_ROWS)
        return pltpu.make_async_remote_copy(
            src_ref=self.windows.at[pl.ds(0, NEAR_CROSS), rows],
            dst_ref=self.all.at[pl.ds(self.cap + NEAR_CORE, NEAR_CROSS), rows],
            send_sem=self.sems.at[2], recv_sem=self.sems.at[3], device_id=(img, 3 - self.band), device_id_type=MESH,
        )

    def send_cross(self):
        pl.when(self.inner())(lambda: self.to_cross(True).start())

    def send_core_inner(self):
        pl.when(self.inner())(lambda: self.to_core(NEAR_CROSS, NEAR_CORE).start())

    def send_core_outer(self):
        pl.when(self.outer())(lambda: self.to_core(0, 3).start())

    def finish(self):
        @pl.when(self.inner())
        def _():
            self.to_core(NEAR_CROSS, NEAR_CORE).wait_send()
            self.to_core(0, 3).wait_recv()
            self.to_cross(True).wait_send()
            self.to_cross(False).wait_recv()

        @pl.when(self.outer())
        def _():
            self.to_core(0, 3).wait_send()
            self.to_core(NEAR_CROSS, NEAR_CORE).wait_recv()


class Gather:
    def __init__(self, block, out, sems):
        self.block, self.out, self.sems = block, out, sems
        img, self.band = lax.axis_index("img"), lax.axis_index("band")
        self.z, self.y = img // 2, img % 2
        self.x, self.c = self.band // 2, self.band % 2

    def where(self, dz, fx, fy):
        img = (self.z + 4 - dz) % 4 * 2 + (1 - self.y if fy else self.y)
        return img, (1 - self.x if fx else self.x) * 2 + self.c

    def move(self, k, dz, fx, fy, device):
        img, band = self.where(dz, fx, fy)
        own = (dz, fx, fy) == (0, 0, 0)
        return pltpu.make_async_remote_copy(
            src_ref=self.block if own else self.out.at[img, band], dst_ref=self.out.at[img, band],
            send_sem=self.sems.at[0, k], recv_sem=self.sems.at[1, k], device_id=device, device_id_type=MESH,
        )

    def along_z(self, d):
        return self.move(d - 1, 0, 0, 0, ((self.z + d) % 4 * 2 + self.y, self.band))

    def along_x(self, dz):
        return self.move(3 + dz, dz, 0, 0, partner("x"))

    def along_y(self, fx, dz):
        return self.move(7 + 4 * fx + dz, dz, fx, 0, partner("y"))

    def to_core(self, fy, fx, dz):
        return self.move(15 + 8 * fy + 4 * fx + dz, dz, fx, fy, partner("c"))

    def keep(self):
        img, band = self.where(0, 0, 0)
        return pltpu.make_async_copy(self.block, self.out.at[img, band], self.sems.at[0, 31])

    def pass_on(self, dz):
        self.along_x(dz).start()
        self.along_y(0, dz).start()
        self.to_core(0, 0, dz).start()

    def begin(self):
        self.keep().start()
        for d in range(1, 4):
            self.along_z(d).start()
        self.pass_on(0)

    def run(self):
        for dz in range(1, 4):
            self.along_z(dz).wait_recv()
            self.pass_on(dz)
        for dz in range(4):
            self.along_x(dz).wait_recv()
            self.along_y(1, dz).start()
            self.to_core(0, 1, dz).start()
        for fx in range(2):
            for dz in range(4):
                self.along_y(fx, dz).wait_recv()
                self.to_core(1, fx, dz).start()
        for d in range(1, 4):
            self.along_z(d).wait_send()
        for dz in range(4):
            self.along_x(dz).wait_send()
            for fx in range(2):
                self.along_y(fx, dz).wait_send()
                for fy in range(2):
                    self.to_core(fy, fx, dz).wait()
        self.keep().wait()


class Edges:
    def __init__(self, rows, ext, zero, sems):
        self.rows, self.ext, self.zero, self.sems = rows, ext, zero, sems
        self.band = lax.axis_index("band")
        self.own_rows = rows.shape[1]

    def inner(self):
        return (self.band == 1) | (self.band == 2)

    def keep(self):
        return pltpu.make_async_copy(self.rows, self.ext.at[:, pl.ds(HALO, self.own_rows)], self.sems.at[0])

    def empty(self):
        at = self.band // 3 * (HALO + self.own_rows)
        return [
            pltpu.make_async_copy(self.zero, self.ext.at[m, pl.ds(at, HALO)], self.sems.at[1 + m]) for m in range(2)
        ]

    def core(self, sending):
        odd = self.band % 2
        far = self.own_rows - HALO
        there = (1 - odd if sending else odd) * 0 + (odd if sending else 1 - odd) * (HALO + self.own_rows)
        return pltpu.make_async_remote_copy(
            src_ref=self.rows.at[:, pl.ds((1 - odd) * far, HALO)], dst_ref=self.ext.at[:, pl.ds(there, HALO)],
            send_sem=self.sems.at[3], recv_sem=self.sems.at[4], device_id=partner("c"), device_id_type=MESH,
        )

    def cross(self, sending):
        img = lax.axis_index("img")
        m = 2 - self.band
        far = self.own_rows - HALO
        to = m if sending else 1 - m
        there = (1 - to) * (HALO + self.own_rows)
        return pltpu.make_async_remote_copy(
            src_ref=self.rows.at[m, pl.ds(m * far, HALO)], dst_ref=self.ext.at[to, pl.ds(there, HALO)],
            send_sem=self.sems.at[5], recv_sem=self.sems.at[6], device_id=(img, 3 - self.band), device_id_type=MESH,
        )

    def start(self):
        pl.when(self.inner())(lambda: self.cross(True).start())
        self.core(True).start()
        self.keep().start()

        @pl.when(jnp.logical_not(self.inner()))
        def _():
            for copy in self.empty():
                copy.start()

    def finish(self):
        self.core(True).wait_send()
        self.core(False).wait_recv()
        self.keep().wait()

        @pl.when(self.inner())
        def _():
            self.cross(True).wait_send()
            self.cross(False).wait_recv()

        @pl.when(jnp.logical_not(self.inner()))
        def _():
            for copy in self.empty():
                copy.wait()


def entry_kernel(
    block_ref, x_ref, g_ref, all_ref, xext_ref, gext_ref, zero_ref, xin_ref, gin_ref, lsems, gsems, xsems, esems,
):
    loads = [pltpu.make_async_copy(x_ref, xin_ref, lsems.at[0]), pltpu.make_async_copy(g_ref, gin_ref, lsems.at[1])]
    for load in loads:
        load.start()
    zero_ref[...] = jnp.zeros_like(zero_ref)
    edges = [Edges(xin_ref, xext_ref, zero_ref, xsems), Edges(gin_ref, gext_ref, zero_ref, esems)]
    greet()
    gather = Gather(block_ref, all_ref, gsems)
    gather.begin()
    for load, item in zip(loads, edges):
        load.wait()
        item.start()
    gather.run()
    for item in edges:
        item.finish()


def entry(block, x, g):
    sds = jax.ShapeDtypeStruct
    ext = sds((2, x.shape[1] + 2 * HALO, SIDE, D), BF16)
    inside, anywhere = pl.BlockSpec(memory_space=pltpu.VMEM), pl.BlockSpec(memory_space=pl.ANY)
    return pl.pallas_call(
        entry_kernel,
        in_specs=[inside, anywhere, anywhere],
        out_specs=[anywhere] * 3,
        out_shape=[sds((8, 4) + block.shape, BF16), ext, ext],
        scratch_shapes=[
            pltpu.VMEM((HALO, SIDE, D), BF16), pltpu.VMEM(x.shape, BF16), pltpu.VMEM(x.shape, BF16),
            pltpu.SemaphoreType.DMA((2,)), pltpu.SemaphoreType.DMA((2, 32)), pltpu.SemaphoreType.DMA((7,)),
            pltpu.SemaphoreType.DMA((7,)),
        ],
        compiler_params=pltpu.CompilerParams(vmem_limit_bytes=VMEM_LIMIT, collective_id=3, has_side_effects=True),
    )(block, x, g)


def attn_bwd_kernel(
    meta_ref, qkv_ref, p_ref, inv_ref, att_ref, datt_ref, table_ref, kback_ref, *rest,
):
    w = pl.program_id(0)
    if len(rest) == 3:
        dqkv_ref, rel_ref, bias_ref = rest
        streams = None
    else:
        fc1_ref, fc2_ref, dqkv_ref, rel_ref, bias_ref, part_ref, sum2_ref = rest[:7]
        half = SHARD_ROWS // 2
        streams = []
        for n in range(4):
            own, *got, sems = rest[7 + 7 * n : 14 + 7 * n]
            source = wide_source(fc2_ref if n < 2 else fc1_ref, n % 2)
            streams.append(Halving(source, own, got, sems, ORDERS[n % 2], half))
        ones, twos = streams[:2], streams[2:]
        timeline(
            w,
            {
                0: [greet, each(streams, "first")],
                2: [each(ones, "first_done"), each(ones, "step", 0), each(twos, "first_done")],
                5: [each(ones, "step_done", 0), each(ones, "step", 1), each(twos, "step", 0)],
                7: [each(ones, "step_done", 1), each(ones, "step", 2)],
                10: [each(twos, "step_done", 0), each(twos, "step", 1), each(ones, "step_done", 2), each(ones, "step", 3)],
            },
        )

    @pl.when(w == 0)
    def _():
        rel_ref[...] = jnp.zeros_like(rel_ref)
        bias_ref[...] = jnp.zeros_like(bias_ref)

    lane = iota((TW, LANES), 1)
    low_half = lane < 64
    onehot = kback_ref[...]
    for p in range(PAIRS):
        q = qkv_ref[:, LANES * p : LANES * p + LANES]
        k8 = qkv_ref[:, D + LANES * p : D + LANES * p + LANES]
        v = qkv_ref[:, 2 * D + LANES * p : 2 * D + LANES * p + LANES]
        cols = slice(LANES * p, LANES * p + LANES)
        da = datt_ref[:, cols].astype(F32) * inv_ref[:, cols]
        da_low = da.astype(BF16)
        prod = da_low.astype(F32) * att_ref[:, cols].astype(F32)
        keys = jnp.concatenate([k8, onehot], axis=1)
        da_t = da.T.astype(BF16)
        q_t = q.astype(F32).T.astype(BF16)
        zero = jnp.zeros_like(v)
        dqx, dv_t, dk_t = [], [], []
        for h in range(2):
            mine = low_half if h == 0 else ~low_half
            centre = jnp.sum(jnp.where(mine, prod, 0.0), axis=-1, keepdims=True)
            dp = mm_nt(da_low, jnp.where(mine, v, zero))
            e = p_ref[2 * p + h]
            ds = (e.astype(F32) * (dp - centre)).astype(BF16)
            dqx.append(mm(ds, keys))
            dv_t.append(mm(da_t[64 * h : 64 * h + 64], e))
            dk_t.append(mm(q_t[64 * h : 64 * h + 64], ds))
        dq = jnp.where(low_half, dqx[0][:, :LANES], dqx[1][:, :LANES])
        drc = jnp.where(low_half, dqx[0][:, LANES:], dqx[1][:, LANES:])
        part = lane & 63
        rows = roll_rows(jnp.where(part < 16, drc, 0.0), 1)
        cols_part = roll_cols(jnp.where((part >= 16) & (part < 32), drc, 0.0), LANES - 16)
        skew = jnp.concatenate([rows, cols_part], axis=1).astype(BF16)
        dq = dq + mm_nt(skew, table_ref[...])
        rel_ref[...] += mm(q_t, skew)
        dv = jnp.concatenate(dv_t, axis=0).T
        dk = (jnp.concatenate(dk_t, axis=0) * 0.125).T
        dqkv_ref[:, cols] = dq.astype(BF16)
        dqkv_ref[:, D + LANES * p : D + LANES * p + LANES] = dk.astype(BF16)
        dqkv_ref[:, 2 * D + LANES * p : 2 * D + LANES * p + LANES] = dv.astype(BF16)
        bias_ref[0, :, cols] += fold8(dq)
        bias_ref[1, :, cols] += fold8(dv)

    if streams:
        @pl.when(w == pl.num_programs(0) - 1)
        def _():
            each(ones, "step_done", 3)()
            sum2_ref[:half] = ones[0].result()
            sum2_ref[half:] = ones[1].result()
            each(twos, "step_done", 1)()
            for n, stream in enumerate(twos):
                part_ref[n] = stream.own[stream.at["x"], :, :, stream.at["y"]]


def attention_backward(meta, qkv, p, inv, att, datt, table, kback, beside=()):
    cap = meta.shape[0]
    sds = jax.ShapeDtypeStruct
    anywhere = pl.BlockSpec(memory_space=pl.ANY)
    shard = (SHARD_ROWS, SHARD_COLS)
    more_specs, more_outs, scratch, extra = [], [], [], {}
    if beside:
        part = (2, 2, 2, SHARD_ROWS // 2, SHARD_COLS)
        more_specs = [whole(part), whole(shard)]
        more_outs = [sds(part, BF16), sds(shard, F32)]
        scratch = Halving.scratch(SHARD_ROWS // 2) * 4
        extra = dict(collective_id=1, has_side_effects=True)
    return pl.pallas_call(
        attn_bwd_kernel,
        grid_spec=pltpu.PrefetchScalarGridSpec(
            num_scalar_prefetch=1,
            grid=(cap,),
            in_specs=[
                per_window(TW, 3 * D), per_window(HEADS, TW, TW), per_window(TW, D), per_window(TW, D),
                per_window(TW, D), whole((LANES, 256)), whole((TW, LANES)),
            ] + [anywhere] * len(beside),
            out_specs=[per_window(TW, 3 * D), whole((LANES, 256)), whole((2, 8, D))] + more_specs,
            scratch_shapes=scratch,
        ),
        out_shape=[sds((cap, TW, 3 * D), BF16), sds((LANES, 256), F32), sds((2, 8, D), F32)] + more_outs,
        compiler_params=pltpu.CompilerParams(vmem_limit_bytes=VMEM_LIMIT, **extra),
        cost_estimate=pl.CostEstimate(flops=60_000_000_000, bytes_accessed=80_000_000, transcendentals=0),
    )(meta, qkv, p, inv, att, datt, table, kback, *beside)


def rel_from(acc):
    def one(block):
        own = block[:64, :32] + block[64:, 64:96]
        return own[:, :RELS].T

    return one(acc[:, :LANES])[::-1], one(acc[:, LANES:])


def put_window(target, y, acc_ref, row0):
    picks = jnp.where(iota((TW, 256), 1) == target, 1.0, 0.0).astype(BF16)
    for q in range(4):
        n = 4 if q < 3 else 2
        t = slice(64 * q, 64 * q + STRIDE * n)
        part = lax.dot_general(
            picks[t, : 64 * n], y[t], (((0,), (0,)), ((), ())), preferred_element_type=F32
        )
        acc_ref[pl.ds(row0 + 4 * q, n)] += part.reshape(n, SIDE, D).astype(acc_ref.dtype)


def scatter_kernel(meta_ref, y_ref, ext_ref, acc_ref):
    w = pl.program_id(0)

    @pl.when(w == 0)
    def _():
        acc_ref[...] = jnp.zeros_like(acc_ref)

    put_window(token_target(meta_ref, w), y_ref[...], acc_ref, meta_ref[w, 0])

    @pl.when(w == pl.num_programs(0) - 1)
    def _():
        def copy(i, _):
            ext_ref[i] = acc_ref[i].astype(BF16)
            return 0
        lax.fori_loop(0, ext_ref.shape[0], copy, 0)


def scatter(meta, y, ext_rows):
    cap = meta.shape[0]
    return pl.pallas_call(
        scatter_kernel,
        grid_spec=pltpu.PrefetchScalarGridSpec(
            num_scalar_prefetch=1,
            grid=(cap,),
            in_specs=[per_window(TW, D)],
            out_specs=whole((ext_rows, SIDE, D)),
            scratch_shapes=[pltpu.VMEM((ext_rows, SIDE, D), F32)],
        ),
        out_shape=jax.ShapeDtypeStruct((ext_rows, SIDE, D), BF16),
        compiler_params=pltpu.CompilerParams(vmem_limit_bytes=VMEM_LIMIT),
        cost_estimate=pl.CostEstimate(flops=5_000_000_000, bytes_accessed=20_000_000, transcendentals=0),
    )(meta, y)


def last_kernel(
    meta_ref, dqkv_ref, wqkv_ref, x_ref, dmix_ref, gain_ref, ext_ref, sums_ref, acc_ref,
):
    w = pl.program_id(0)

    @pl.when(w == 0)
    def _():
        acc_ref[...] = jnp.zeros_like(acc_ref)
        sums_ref[...] = jnp.zeros_like(sums_ref)

    target = token_target(meta_ref, w)
    dn = jnp.zeros((TW, D), F32)
    for c in range(3):
        cols = slice(D * c, D * c + D)
        dn = dn + mm_nt(dqkv_ref[:, cols], wqkv_ref[:, cols])
    dn = jnp.where(target >= 0, dn, 0.0)
    unit, inverse = norm(x_ref[...].astype(F32))
    sums_ref[0] += fold8(dn * unit)
    sums_ref[1] += fold8(dn)
    grad = dmix_ref[...].astype(F32) + norm_back(dn, unit, inverse, gain_ref[0:1])
    put_window(target, grad.astype(BF16), acc_ref, meta_ref[w, 0])

    @pl.when(w == pl.num_programs(0) - 1)
    def _():
        def copy(i, _):
            ext_ref[i] = acc_ref[i].astype(BF16)
            return 0
        lax.fori_loop(0, ext_ref.shape[0], copy, 0)


def last_norm(meta, dqkv, wqkv, x, dmix, gain, ext_rows):
    cap = meta.shape[0]
    sds = jax.ShapeDtypeStruct
    return pl.pallas_call(
        last_kernel,
        grid_spec=pltpu.PrefetchScalarGridSpec(
            num_scalar_prefetch=1,
            grid=(cap,),
            in_specs=[
                per_window(TW, 3 * D), whole((D, 3 * D)), per_window(TW, D), per_window(TW, D), whole((8, D)),
            ],
            out_specs=[whole((ext_rows, SIDE, D)), whole((2, 8, D))],
            scratch_shapes=[pltpu.VMEM((ext_rows, SIDE, D), F32)],
        ),
        out_shape=[sds((ext_rows, SIDE, D), BF16), sds((2, 8, D), F32)],
        compiler_params=pltpu.CompilerParams(vmem_limit_bytes=VMEM_LIMIT),
        cost_estimate=pl.CostEstimate(flops=15_000_000_000, bytes_accessed=30_000_000, transcendentals=0),
    )(meta, dqkv, wqkv, x, dmix, gain)


class SmallSum:
    def __init__(self, mine, got_band, got_img, sems):
        self.mine, self.got, self.sems = mine, (got_band, got_img), sems

    @staticmethod
    def scratch(shape):
        return [
            pltpu.VMEM(shape, F32), pltpu.VMEM((3,) + shape, F32), pltpu.VMEM((7,) + shape, F32),
            pltpu.SemaphoreType.DMA((2, 2, 7)),
        ]

    def copies(self, k):
        return [
            pltpu.make_async_remote_copy(
                src_ref=self.mine, dst_ref=self.got[k].at[d], send_sem=self.sems.at[k, 0, d],
                recv_sem=self.sems.at[k, 1, d], device_id=device, device_id_type=MESH,
            )
            for d, device in enumerate(peers()[k])
        ]

    def send(self, k):
        for copy in self.copies(k):
            copy.start()

    def add(self, k):
        copies = self.copies(k)
        for copy in copies:
            copy.wait()
        total = self.mine[...]
        for d in range(len(copies)):
            total = total + self.got[k][d]
        self.mine[...] = total


HOME_ROWS = 8


def home_kernel(
    table_ref, own_ref, core_ref, cross_ref, grad_ref, total_ref, ln_ref, rel_ref, q_ref, fc2_ref,
    output_ref, input_grad_ref, vec_refs, b1_ref, relr_ref, relc_ref, wq_ref, wp_ref, w2_ref,
    out_ref, sems,
):
    step = pl.program_id(0)
    per_image = pl.num_programs(0) // 2
    m = step // per_image
    top, left = table_ref[m, 25], table_ref[m, 26]
    first = table_ref[m, 27] + (step - m * per_image) * HOME_ROWS
    group, band = table_ref[m, 28], table_ref[m, 29]

    @pl.when(step == 0)
    def _():
        cap = own_ref.shape[0]
        loads = [
            pltpu.make_async_copy(ref, out_ref.at[pl.ds(at, ref.shape[0])], sems.at[n])
            for n, (ref, at) in enumerate(((own_ref, 0), (core_ref, cap), (cross_ref, cap + NEAR_CORE)))
        ]
        for load in loads:
            load.start()
        share = vec_refs[0].shape[1]

        def cut(rows, width):
            mine = jnp.zeros((rows.shape[0], width), F32)
            for i in range(rows.shape[1] // width):
                mine = mine + jnp.where(group % (rows.shape[1] // width) == i, rows[:, width * i : width * i + width], 0.0)
            return mine

        ln, total = cut(ln_ref[...], share), cut(total_ref[...], share)
        for ref, row in zip(vec_refs, (ln[0:1], ln[1:2], total[0:1], total[1:2], total[5:6], total[3:4], total[4:5], total[2:3])):
            ref[...] = row
        b1_ref[...] = cut(total_ref[pl.ds(6 + group // 2, 1)], SHARD_COLS)
        features = relr_ref.shape[1]
        turned = rel_ref[pl.ds(pl.multiple_of(band * features, features), features)].T
        for j in range(RELS):
            relr_ref[j : j + 1] = turned[RELS - 1 - j : RELS - j]
        relc_ref[...] = turned[LANES : LANES + RELS]
        wq_ref[...] = q_ref[:, : 3 * share]
        wp_ref[...] = q_ref[:, 3 * share :]
        w2_ref[...] = fc2_ref[...].T
        for load in loads:
            load.wait()

    col = iota((SIDE, GRID * STRIDE), 0) + left
    spot = iota((SIDE, GRID * STRIDE), 1)
    picks = jnp.where((spot >> 4) * WIN + (spot & 15) == col, 1.0, 0.0)
    picks = jnp.where((spot & 15) < WIN, picks, 0.0).astype(BF16)
    for i in range(HOME_ROWS):
        at = i + first + top
        r = at // WIN
        a = pl.multiple_of((at - r * WIN) * STRIDE, STRIDE)
        slots = [table_ref[m, r * GRID + c] for c in range(GRID)]
        for source, target in ((out_ref, output_ref), (grad_ref, input_grad_ref)):
            tokens = jnp.concatenate([source[slot, pl.ds(a, STRIDE)] for slot in slots], axis=0)
            target[0, i] = mm(picks, tokens).astype(target.dtype)


def home(table, sources, rows):
    per_image = rows // HOME_ROWS
    sds = jax.ShapeDtypeStruct
    tiled = pl.BlockSpec((1, HOME_ROWS, SIDE, D), lambda w, meta: (w // per_image, w % per_image, 0, 0))
    shapes = [[(1, D // 8)] * 8, (1, FF // 8)] + [(RELS, HEAD // 4)] * 2 + [
        (SHARD_ROWS, 3 * D // 8), (SHARD_ROWS, D // 8), (SHARD_COLS, SHARD_ROWS),
    ]
    is_shape = lambda shape: isinstance(shape, tuple)
    return pl.pallas_call(
        home_kernel,
        grid_spec=pltpu.PrefetchScalarGridSpec(
            num_scalar_prefetch=1,
            grid=(2 * per_image,),
            in_specs=[pl.BlockSpec(memory_space=pl.ANY)] * 3 + [whole(a.shape) for a in sources[3:]],
            scratch_shapes=[pltpu.VMEM(sources[3].shape, BF16), pltpu.SemaphoreType.DMA((3,))],
            out_specs=[tiled, tiled] + jax.tree.map(whole, shapes, is_leaf=is_shape),
        ),
        out_shape=[sds((2, rows, SIDE, D), BF16), sds((2, rows, SIDE, D), F32)]
        + jax.tree.map(lambda shape: sds(shape, F32), shapes, is_leaf=is_shape),
        compiler_params=pltpu.CompilerParams(vmem_limit_bytes=VMEM_LIMIT),
        cost_estimate=pl.CostEstimate(flops=500_000_000, bytes_accessed=20_000_000, transcendentals=0),
    )(table, *sources)


def home_table(plan, offsets, group, band, band_rows):
    own = np.full((4, 2, WINDOWS), 0, np.int32)
    for b in range(4):
        for slot, (m, w) in enumerate(plan[b]):
            if w >= 0:
                own[b, m, w] = slot
        odd, cap = b % 2, len(plan[b])
        mate = plan[b ^ 1]
        sent = mate[:3] if (b ^ 1) in (0, 3) else mate[NEAR_CROSS : NEAR_CROSS + NEAR_CORE]
        for slot, (m, w) in enumerate(sent):
            own[b, m, w] = cap + slot
        if b in (1, 2):
            for slot, (m, w) in enumerate(plan[3 - b][:NEAR_CROSS]):
                own[b, m, w] = cap + NEAR_CORE + slot
    rows = jnp.asarray(own)[band]
    first = jnp.full((2, 1), band_rows, jnp.int32) * band
    spot = jnp.broadcast_to(jnp.stack([group, band]).astype(jnp.int32), (2, 2))
    return jnp.concatenate([rows, offsets.astype(jnp.int32), first, spot, jnp.zeros((2, 2), jnp.int32)], axis=1)


def last_fused_kernel(
    meta_ref, dqkv_ref, wqkv_ref, x_ref, dmix_ref, gain_ref, dwq_ref, dwp_ref, bias_ref, sums_ref, fc1_ref, rel_ref,
    all_ref, shard_ref, total_ref, rels_ref, ln_ref,
    grad_ref, ln_acc, q_ref, *rest,
):
    w = pl.program_id(0)
    end = pl.num_programs(0) - 1
    half = SHARD_ROWS // 2
    streams = []
    for n, order in enumerate(ORDERS):
        own, *got, sems = rest[7 * n : 7 * n + 7]

        def source(x, img, c, n=n):
            row = pl.multiple_of((2 * x + c) * SHARD_ROWS + n * half, half)
            return q_ref.at[img, pl.ds(row, half)]

        streams.append(Halving(source, own, got, sems, order, half))
    rest = rest[14:]
    small, rel, ln = [SmallSum(*rest[4 * n : 4 * n + 4]) for n in range(3)]
    back = Homeward(grad_ref, all_ref, rest[12])

    def start():
        groups = q_ref.shape[0]
        wide, share = 3 * D // groups, D // groups
        for i in range(groups):
            q_ref[i] = jnp.concatenate(
                [dwq_ref[:, wide * i : wide * i + wide], dwp_ref[:, share * i : share * i + share]], axis=1
            )
        greet()
        each(streams, "first")()

    def prepare():
        for r in range(2):
            small.mine[r : r + 1] = jnp.sum(bias_ref[r], axis=0, keepdims=True)
        for r in range(4):
            small.mine[2 + r : 3 + r] = jnp.sum(sums_ref[r], axis=0, keepdims=True)
            small.mine[6 + r : 7 + r] = jnp.sum(fc1_ref[:, D * r : D * r + D], axis=0, keepdims=True)
        small.mine[10:] = jnp.zeros((6, D), F32)
        rel.mine[...] = rel_ref[:64] + pltpu.roll(rel_ref[64:], 192, 1)
        small.send(0)
        rel.send(0)
        ln_acc[...] = jnp.zeros_like(ln_acc)

    def middle():
        small.add(0)
        rel.add(0)
        small.send(1)
        rel.send(1)

    def finish():
        small.add(1)
        rel.add(1)
        total_ref[...] = small.mine[...]
        rels_ref[...] = rel.mine[...]

    timeline(
        w,
        {
            0: [start, prepare],
            2: [each(streams, "first_done"), each(streams, "step", 0)],
            3: [middle, back.send_core_outer],
            6: [each(streams, "step_done", 0), each(streams, "step", 1), finish],
            8: [each(streams, "step_done", 1), each(streams, "step", 2), back.send_cross],
            12: [each(streams, "step_done", 2), each(streams, "step", 3), back.send_core_inner],
        },
    )

    target = token_target(meta_ref, w)
    dn = jnp.zeros((TW, D), F32)
    for c in range(3):
        cols = slice(D * c, D * c + D)
        dn = dn + mm_nt(dqkv_ref[:, cols], wqkv_ref[:, cols])
    dn = jnp.where(target >= 0, dn, 0.0)
    unit, inverse = norm(x_ref[...].astype(F32))
    ln_acc[0] += fold8(dn * unit)
    ln_acc[1] += fold8(dn)
    grad = dmix_ref[...].astype(F32) + norm_back(dn, unit, inverse, gain_ref[0:1])
    grad_ref[w] = grad.astype(BF16)

    @pl.when(w == end)
    def _():
        back.keep().start()
        ln.mine[0:1] = jnp.sum(ln_acc[0], axis=0, keepdims=True)
        ln.mine[1:2] = jnp.sum(ln_acc[1], axis=0, keepdims=True)
        ln.mine[2:] = jnp.zeros((6, D), F32)
        ln.send(0)
        each(streams, "step_done", 3)()
        ln.add(0)
        ln.send(1)
        for n, stream in enumerate(streams):
            shard_ref[half * n : half * n + half] = stream.result()
        back.keep().wait()
        back.finish()
        ln.add(1)
        ln_ref[...] = ln.mine[...]


def last_fused(meta, dqkv, wqkv, x, dmix, gain, dwq, dwp, bias_sums, sums, fc1_sum, rel_acc):
    cap = meta.shape[0]
    sds = jax.ShapeDtypeStruct
    half = SHARD_ROWS // 2
    anywhere = pl.BlockSpec(memory_space=pl.ANY)
    sums_out = [((SHARD_ROWS, SHARD_COLS), F32), ((16, D), F32), ((64, 256), F32), ((8, D), F32)]
    return pl.pallas_call(
        last_fused_kernel,
        grid_spec=pltpu.PrefetchScalarGridSpec(
            num_scalar_prefetch=1,
            grid=(cap,),
            in_specs=[
                per_window(TW, 3 * D), whole((D, 3 * D)), per_window(TW, D), per_window(TW, D), whole((8, D)),
                whole((D, 3 * D)), whole((D, D)), whole((2, 8, D)), whole((4, 8, D)), whole((8, FF)), whole((LANES, 256)),
            ],
            out_specs=[anywhere] + [whole(shape) for shape, _ in sums_out],
            scratch_shapes=[
                pltpu.VMEM((cap, TW, D), BF16), pltpu.VMEM((2, 8, D), F32), pltpu.VMEM((8, D, SHARD_COLS), BF16)
            ]
            + Halving.scratch(half) * 2
            + SmallSum.scratch((16, D)) + SmallSum.scratch((64, 256)) + SmallSum.scratch((8, D))
            + [pltpu.SemaphoreType.DMA((5,))],
        ),
        out_shape=[sds((cap + NEAR_CORE + NEAR_CROSS, TW, D), BF16)] + [sds(shape, dtype) for shape, dtype in sums_out],
        compiler_params=pltpu.CompilerParams(vmem_limit_bytes=VMEM_LIMIT, collective_id=2, has_side_effects=True),
        cost_estimate=pl.CostEstimate(flops=20_000_000_000, bytes_accessed=50_000_000, transcendentals=0),
    )(meta, dqkv, wqkv, x, dmix, gain, dwq, dwp, bias_sums, sums, fc1_sum, rel_acc)


def window_plan(images, bands):
    lists = [[] for _ in range(bands)]
    if images == 2 and bands == 4:
        spans = (
            ((0, 5, 8), (0, 0, 5), (1, 0, 5)),
            ((0, 10, 15), (0, 8, 10), (1, 5, 10)),
            ((1, 10, 15), (1, 15, 17), (0, 15, 20)),
            ((1, 17, 20), (1, 20, 25), (0, 20, 25)),
        )
        lists = [[(m, w) for m, first, last in row for w in range(first, last)] for row in spans]
    else:
        cuts = [
            [(WINDOWS * b + (bands - 1 if m % 2 else 0)) // bands for b in range(bands + 1)] for m in range(images)
        ]
        for m in range(images):
            for b in range(bands):
                lists[b] += [(m, w) for w in range(cuts[m][b], min(cuts[m][b + 1], WINDOWS))]
    cap = max(len(item) for item in lists)
    return np.array([item + [(0, -1)] * (cap - len(item)) for item in lists], np.int32)


HALO = 12


def near(images, bands, band_rows):
    return images == 2 and bands == 4 and band_rows == 16


CORE = [(0, 1), (1, 0), (2, 3), (3, 2)]
CROSS = [(1, 2), (2, 1)]


def extend(rows, band):
    images, band_rows = rows.shape[:2]
    if not near(images, lax.axis_size("band"), band_rows):
        full = lax.all_gather(rows, "band", axis=1, tiled=True)
        return jnp.pad(full, ((0, 0), (6, 6), (0, 0), (0, 0)))
    odd = band % 2 == 1
    top, bottom = rows[:, :HALO], rows[:, -HALO:]
    from_core = lax.ppermute(jnp.where(odd, top, bottom), "band", CORE)
    from_cross = lax.ppermute(jnp.where(odd, bottom[1], top[0]), "band", CROSS)
    zero = jnp.zeros_like(from_cross)
    above = jnp.where(odd, from_core, jnp.stack([zero, from_cross]))
    below = jnp.where(odd, jnp.stack([from_cross, zero]), from_core)
    return jnp.concatenate([above, rows, below], axis=1)


def collect(ext, band, images, band_rows):
    if not near(images, lax.axis_size("band"), band_rows):
        return lax.psum_scatter(ext[:, 6:-6], "band", scatter_dimension=1, tiled=True).astype(F32)
    odd = band % 2 == 1
    above, below = ext[:, :HALO], ext[:, -HALO:]
    from_core = lax.ppermute(jnp.where(odd, above, below), "band", CORE).astype(F32)
    from_cross = lax.ppermute(jnp.where(odd, below[0], above[1]), "band", CROSS).astype(F32)
    zero = jnp.zeros_like(from_cross)
    top = jnp.where(odd, from_core, jnp.stack([from_cross, zero]))
    bottom = jnp.where(odd, jnp.stack([zero, from_cross]), from_core)
    own = ext[:, HALO:-HALO].astype(F32)
    rest = band_rows - HALO
    return own + jnp.pad(top, ((0, 0), (0, rest), (0, 0), (0, 0))) + jnp.pad(bottom, ((0, 0), (rest, 0), (0, 0), (0, 0)))


def shards(
    image_tokens, pad_offsets, ln1_gain, ln1_bias, w_qkv, q_bias, v_bias, rel_rows, rel_cols, w_proj, proj_bias,
    ln2_gain, ln2_bias, w_fc1, fc1_bias, w_fc2, fc2_bias, out_grad,
):
    images, band_rows = image_tokens.shape[:2]
    bands, groups = lax.axis_size("band"), lax.axis_size("img")
    band, group = lax.axis_index("band"), lax.axis_index("img")
    axes = ("img", "band")

    part, wide = w_qkv.shape
    close = near(images, bands, band_rows)
    fused = close and groups == 8
    small = jnp.concatenate(
        [
            ln1_gain, ln1_bias, q_bias, v_bias, proj_bias, ln2_gain, ln2_bias, fc2_bias, fc1_bias,
            rel_rows.reshape(-1), rel_cols.reshape(-1),
        ]
    )
    block_cols = wide + w_proj.shape[1]
    small_rows = -(-small.shape[0] // (block_cols * 16)) * 16
    small = jnp.pad(small, (0, small_rows * block_cols - small.shape[0])).reshape(small_rows, block_cols)
    block = jnp.concatenate([jnp.concatenate([w_qkv, w_proj], axis=1), small], axis=0)
    if fused:
        first, ext, gext = entry(block, image_tokens, out_grad)
    else:
        first = lax.all_gather(block, axes, axis=0, tiled=False).reshape(groups, bands, part + small_rows, block_cols)
        ext, gext = extend(image_tokens, band), extend(out_grad, band)
    ff = lax.all_gather(jnp.concatenate([w_fc1, w_fc2.T], axis=1), axes, axis=0, tiled=False).reshape(
        groups, bands * part, -1
    )
    tail = first[:, :, part:].reshape(groups, bands, small_rows * block_cols)
    share = D // groups
    vectors = tail[:, 0, : 8 * share].reshape(groups, 8, share).transpose(1, 0, 2).reshape(8, D).astype(F32)
    fc1_shift = tail[:, 0, 8 * share : 8 * share + FF // groups].reshape(1, FF).astype(F32)
    at = 8 * share + FF // groups
    rels = tail[0, :, at : at + 2 * RELS * (HEAD // bands)].reshape(bands, 2, RELS, HEAD // bands)
    rels = rels.transpose(1, 2, 0, 3).reshape(2, RELS, HEAD)
    plan = jnp.asarray(window_plan(images, bands))[band]
    image, window = plan[:, 0], plan[:, 1]
    ext_per = band_rows + 2 * HALO if close else bands * band_rows + 12
    base = band_rows * band - HALO if close else -6
    live = window >= 0
    spot = jnp.maximum(window, 0)
    offsets = pad_offsets[image]
    row = spot // GRID * WIN - offsets[:, 0]
    col = spot % GRID * WIN - offsets[:, 1]
    meta = jnp.stack(
        [jnp.where(live, image * ext_per + row - base, HALO), col, row, live.astype(jnp.int32)], axis=1
    ).astype(jnp.int32)
    cap = meta.shape[0]
    ext_rows = images * ext_per

    ka, kb, kback = key_constants()
    ext, gext = ext.reshape(ext_rows, SIDE, D), gext.reshape(ext_rows, SIDE, D)
    if not fused:
        weights = first[:, :, :part].transpose(1, 2, 0, 3)
        wqkv, wproj = weights[..., :wide].reshape(D, 3 * D), weights[..., wide:].reshape(D, D)
    x, g, normed1, qkv, probs, inv, att, *weights = attention_forward(
        meta, ext, gext, vectors, first if fused else wqkv, rel_table(rels[0], rels[1], True), ka, kb
    )
    if fused:
        wqkv, wproj = weights
    out_win, normed2, act, d_pre, d_mixed, d_att, sums, sum_fc1 = feed_forward(
        g, x, att, wproj, vectors, ff, fc1_shift, 0
    )

    def flat(a):
        return a.reshape(-1, a.shape[-1])

    def weight_grad(left, right):
        return jnp.einsum("td,te->de", flat(left), flat(right), preferred_element_type=F32).astype(BF16)

    if fused:
        inner = (band == 1) | (band == 2)
        to_core = lax.dynamic_slice_in_dim(out_win, jnp.where(inner, NEAR_CROSS, 0), NEAR_CORE, 0)
        core_out = lax.ppermute(to_core, "band", CORE)
        cross_out = lax.ppermute(out_win[:NEAR_CROSS], "band", CROSS)
    d_fc2 = weight_grad(g, act)
    d_fc1 = weight_grad(normed2, d_pre)
    d_proj = weight_grad(att, d_mixed)
    if fused:
        d_fc1, d_fc2, core_out, cross_out = lax.optimization_barrier((d_fc1, d_fc2, core_out, cross_out))
    d_qkv, rel_acc, bias_sums, *done = attention_backward(
        meta, qkv, probs, inv, att, d_att, rel_table(rels[0], rels[1], False), kback,
        (d_fc1, d_fc2) if fused else (),
    )
    d_wqkv = weight_grad(normed1, d_qkv)

    if fused:
        partial, g_fc2 = done

        def fold(value, axis, bit, step):
            mine = lax.dynamic_index_in_dim(value, bit, axis, keepdims=False)
            other = lax.dynamic_index_in_dim(value, 1 - bit, axis, keepdims=False)
            came = lax.ppermute(other, "img", [(i, i ^ step) for i in range(groups)])
            return mine.astype(F32) + came.astype(F32)

        partial = fold(partial, 1, group // 4, 4).astype(BF16)
        g_fc1 = fold(partial, 1, group // 2 % 2, 2).reshape(part, FF // groups)
        all_grad, q_shard, total, rel_total, ln_total = last_fused(
            meta, d_qkv, wqkv, x, d_mixed, vectors, d_wqkv, d_proj, bias_sums, sums, sum_fc1, rel_acc
        )
        output, input_grad, shares, b1_share, d_rel_rows, d_rel_cols, g_qkv, g_proj, g_fc2 = home(
            home_table(window_plan(images, bands), pad_offsets, group, band, band_rows),
            (out_win, core_out, cross_out, all_grad, total, ln_total, rel_total, q_shard, g_fc2), band_rows,
        )
        ln1g, ln1b, qb, vb, pb, ln2g, ln2b, b2 = [share.reshape(-1) for share in shares]
        return (
            output, input_grad, ln1g, ln1b, g_qkv, qb, vb, d_rel_rows, d_rel_cols, g_proj, pb, ln2g, ln2b, g_fc1,
            b1_share.reshape(-1), g_fc2, b2,
        )
    else:
        out_ext = scatter(meta, out_win, ext_rows).reshape(images, ext_per, SIDE, D)
        output = collect(out_ext, band, images, band_rows).astype(BF16)
        in_ext, sums1 = last_norm(meta, d_qkv, wqkv, x, d_mixed, vectors, ext_rows)
        input_grad = collect(in_ext.reshape(images, ext_per, SIDE, D), band, images, band_rows)

        def reduce(grad):
            grad = lax.psum_scatter(grad, "img", scatter_dimension=1, tiled=True)
            return lax.psum_scatter(grad, "band", scatter_dimension=0, tiled=True).astype(F32)

        g_fc1, g_fc2, g_qkv, g_proj = reduce(d_fc1), reduce(d_fc2), reduce(d_wqkv), reduce(d_proj)
        ln_total, bias_total, sum_total, fc1_total, d_rel_rows, d_rel_cols = lax.psum(
            (jnp.sum(sums1, 1), jnp.sum(bias_sums, 1), jnp.sum(sums, 1), jnp.sum(sum_fc1, 0)) + rel_from(rel_acc), axes
        )

    def img_share(vector):
        n = vector.shape[0] // groups
        return lax.dynamic_slice_in_dim(vector, group * n, n, 0)

    def band_share(table):
        n = table.shape[1] // bands
        return lax.dynamic_slice_in_dim(table, band * n, n, 1)

    return (
        output,
        input_grad,
        img_share(ln_total[0]),
        img_share(ln_total[1]),
        g_qkv,
        img_share(bias_total[0]),
        img_share(bias_total[1]),
        band_share(d_rel_rows),
        band_share(d_rel_cols),
        g_proj,
        img_share(sum_total[3]),
        img_share(sum_total[1]),
        img_share(sum_total[2]),
        g_fc1,
        img_share(fc1_total),
        g_fc2.T,
        img_share(sum_total[0]),
    )


def solution(mesh):
    tokens, vector, matrix = P("img", "band", None, None), P("img"), P("band", "img")
    table, wide = P(None, "band"), P("img", "band")
    return jax.shard_map(
        shards,
        mesh=mesh,
        in_specs=(
            tokens, P("img", None), vector, vector, matrix, vector, vector, table, table, matrix, vector, vector,
            vector, matrix, vector, wide, vector, tokens,
        ),
        out_specs=(
            tokens, tokens, vector, vector, matrix, vector, vector, table, table, matrix, vector, vector, vector,
            matrix, vector, wide, vector,
        ),
        check_vma=False,
    )
```

```python
import functools
import numpy as np
import jax
import jax.numpy as jnp
from jax import lax
from jax.sharding import PartitionSpec as P
from jax.experimental import pallas as pl
from jax.experimental.pallas import tpu as pltpu

D = 768
HEADS = 12
HEAD = 64
FF = 3072
WIN = 14
SIDE = 64
GRID = 5
WINDOWS = 25
RELS = 27
STRIDE = 16
TW = WIN * STRIDE
PAIRS = HEADS // 2
LANES = 128
EPSILON = 1e-06
F32 = jnp.float32
BF16 = jnp.bfloat16
VMEM_LIMIT = 60 * 1024 * 1024
NT = (((1,), (1,)), ((), ()))


def mm(a, b):
    return jnp.dot(a, b, preferred_element_type=F32)


def mm_nt(a, b):
    return lax.dot_general(a, b, NT, preferred_element_type=F32)


def iota(shape, dim):
    return lax.broadcasted_iota(jnp.int32, shape, dim)


def token_target(meta_ref, w):
    t = iota((TW, 1), 0)
    a, b = t >> 4, t & 15
    col = meta_ref[w, 1] + b
    row = meta_ref[w, 2] + a
    ok = (b < WIN) & (col >= 0) & (col < SIDE) & (row >= 0) & (row < SIDE) & (meta_ref[w, 3] > 0)
    return jnp.where(ok, ((a & 3) << 6) + col, -1)


def take_window(target, rows_ref):
    picks = jnp.where(iota((TW, 256), 1) == target, 1.0, 0.0).astype(BF16)
    parts = []
    for q in range(3):
        src = rows_ref[4 * q : 4 * q + 4].reshape(256, D)
        parts.append(mm(picks[64 * q : 64 * q + 64], src))
    src = rows_ref[12:14].reshape(128, D)
    parts.append(mm(picks[192:224, :128], src))
    return jnp.concatenate(parts, axis=0)


def norm(values):
    mean = jnp.sum(values, axis=-1, keepdims=True) * (1.0 / D)
    centred = values - mean
    inverse = lax.rsqrt(jnp.sum(centred * centred, axis=-1, keepdims=True) * (1.0 / D) + EPSILON)
    return centred * inverse, inverse


def norm_back(grad, unit, inverse, gain):
    s = grad * gain
    m1 = jnp.sum(s, axis=-1, keepdims=True) * (1.0 / D)
    m2 = jnp.sum(s * unit, axis=-1, keepdims=True) * (1.0 / D)
    return inverse * (s - m1 - unit * m2)


def fold8(x):
    return jnp.sum(x.reshape(x.shape[0] // 8, 8, x.shape[1]), axis=0)


def roll_rows(x, forward):
    out = []
    for a in range(WIN):
        piece = x[STRIDE * a : STRIDE * a + STRIDE]
        by = (a - 13) % LANES if forward else a
        out.append(pltpu.roll(piece, by, 1) if by else piece)
    return jnp.concatenate(out, axis=0)


def roll_cols(x, first):
    out = []
    for a in range(WIN):
        piece = x[STRIDE * a : STRIDE * a + STRIDE]
        out.append(pltpu.roll(piece, first, 1, stride=1, stride_axis=0))
    return jnp.concatenate(out, axis=0)


def attn_fwd_pair(q, k8, v, table, keys_a, keys_b, p_ref, p):
    lane = iota((TW, LANES), 1)
    low_half = lane < 64
    rc = mm(q, table)
    both = jnp.where((lane & 31) < 16, roll_rows(rc[:, :LANES], True), roll_cols(rc[:, LANES:], 3))
    high = both.astype(BF16)
    rest = (both - high.astype(F32)).astype(BF16)
    extra = jnp.where((lane & 63) < 32, high, rest)
    extra = jnp.where((lane & 63) == 14, jnp.ones_like(extra), extra)
    left = jnp.concatenate([q, extra], axis=1)
    zero = jnp.zeros_like(k8)
    wide_v = jnp.concatenate([v, jnp.ones_like(v)], axis=1)
    outs, invs = [], []
    for h in range(2):
        keys = jnp.concatenate(
            [jnp.where(low_half if h == 0 else ~low_half, k8, zero), (keys_a, keys_b)[h]], axis=1
        )
        s = mm_nt(left, keys)
        e = jnp.exp(s - jnp.max(s, axis=-1, keepdims=True)).astype(BF16)
        p_ref[2 * p + h] = e
        o = mm(e, wide_v)
        inv = 1.0 / o[:, LANES:]
        outs.append(o[:, :LANES] * inv)
        invs.append(inv)
    att = jnp.where(low_half, outs[0], outs[1]).astype(BF16)
    inv = jnp.where(low_half, invs[0], invs[1])
    return att, inv


def fwd_kernel(
    meta_ref, rows_ref, grows_ref, vec_ref, wqkv_ref, table_ref, ka_ref, kb_ref,
    x_ref, g_ref, n_ref, qkv_ref, p_ref, inv_ref, att_ref, *weights,
):
    w = pl.program_id(0)
    if weights:
        blocks_ref, (wqkv_ref, wproj_ref) = wqkv_ref, weights

        @pl.when(w == 0)
        def _():
            share = D // blocks_ref.shape[0]
            for b in range(blocks_ref.shape[1]):
                rows = slice(SHARD_ROWS * b, SHARD_ROWS * b + SHARD_ROWS)
                parts = [blocks_ref[i, b, :SHARD_ROWS] for i in range(blocks_ref.shape[0])]
                wqkv_ref[rows] = jnp.concatenate([part[:, : 3 * share] for part in parts], axis=1)
                wproj_ref[rows] = jnp.concatenate([part[:, 3 * share :] for part in parts], axis=1)

    target = token_target(meta_ref, w)
    x = take_window(target, rows_ref)
    x_ref[...] = x.astype(BF16)
    g_ref[...] = take_window(target, grows_ref).astype(BF16)
    unit, _ = norm(x)
    normed = jnp.where(target >= 0, unit * vec_ref[0:1] + vec_ref[1:2], 0.0).astype(BF16)
    n_ref[...] = normed
    for c in range(9):
        cols = slice(256 * c, 256 * c + 256)
        y = mm(normed, wqkv_ref[:, cols])
        if c < 3:
            y = y + vec_ref[2:3, cols]
        elif c >= 6:
            y = y + vec_ref[3:4, 256 * (c - 6) : 256 * (c - 6) + 256]
        else:
            y = y.astype(BF16).astype(F32) * 0.125
        qkv_ref[:, cols] = y.astype(BF16)

    for p in range(PAIRS):
        a = slice(LANES * p, LANES * p + LANES)
        q = qkv_ref[:, LANES * p : LANES * p + LANES]
        k8 = qkv_ref[:, D + LANES * p : D + LANES * p + LANES]
        v = qkv_ref[:, 2 * D + LANES * p : 2 * D + LANES * p + LANES]
        att, inv = attn_fwd_pair(q, k8, v, table_ref[...], ka_ref[...], kb_ref[...], p_ref, p)
        att_ref[:, a] = att
        inv_ref[:, a] = inv


def rows_spec(rows):
    return pl.BlockSpec(
        (pl.Element(rows), pl.Element(SIDE), pl.Element(D)), lambda w, meta: (meta[w, 0], 0, 0)
    )


def whole(shape, buffers=1):
    zeros = (0,) * len(shape)
    return pl.BlockSpec(shape, lambda w, meta: zeros, pipeline_mode=pl.Buffered(buffers))


def per_window(*tail):
    zeros = (0,) * len(tail)
    return pl.BlockSpec((None,) + tail, lambda w, meta: (w,) + zeros)


def key_constants():
    t = np.arange(TW)
    kr, kc = t >> 4, t & 15
    real = kc < WIN
    base = np.zeros((TW, 64), np.float32)
    for off in (0, 32):
        base[t[real], off + kr[real]] = 1.0
        base[t[real], off + 16 + kc[real]] = 1.0
    back = np.zeros_like(base)
    back[t[real], 13 - kr[real]] = 1.0
    back[t[real], 16 + 13 - kc[real]] = 1.0
    base[~real, 14] = -1e30
    none = np.zeros_like(base)
    ka = np.concatenate([base, none], 1)
    kb = np.concatenate([none, base], 1)
    back = np.concatenate([back, back], 1)
    return jnp.asarray(ka, BF16), jnp.asarray(kb, BF16), jnp.asarray(back, BF16)


def rel_table(rel_rows, rel_cols, forward):
    def wide(rel):
        turned = jnp.pad(rel, ((0, 0), (0, 32 - RELS)))
        twice = jnp.concatenate([turned, turned], axis=1)
        none = jnp.zeros_like(twice)
        return jnp.concatenate(
            [jnp.concatenate([twice, none], 1), jnp.concatenate([none, twice], 1)], 0
        )

    turn = (lambda rel: rel[:, ::-1]) if forward else (lambda rel: rel)
    return jnp.concatenate([wide(turn(rel_rows)), wide(turn(rel_cols))], axis=1)


def attention_forward(meta, ext, gext, vectors, wqkv, table, ka, kb):
    cap = meta.shape[0]
    weights = [(D, 3 * D), (D, D)] if wqkv.ndim == 4 else []
    sds = jax.ShapeDtypeStruct
    return pl.pallas_call(
        fwd_kernel,
        grid_spec=pltpu.PrefetchScalarGridSpec(
            num_scalar_prefetch=1,
            grid=(cap,),
            in_specs=[
                rows_spec(WIN), rows_spec(WIN), whole((8, D)), whole(wqkv.shape),
                whole((LANES, 256)), whole((TW, LANES)), whole((TW, LANES)),
            ],
            out_specs=[
                per_window(TW, D), per_window(TW, D), per_window(TW, D), per_window(TW, 3 * D),
                per_window(HEADS, TW, TW), per_window(TW, D), per_window(TW, D),
            ] + [whole(shape) for shape in weights],
        ),
        out_shape=[
            sds((cap, TW, D), BF16), sds((cap, TW, D), BF16), sds((cap, TW, D), BF16), sds((cap, TW, 3 * D), BF16),
            sds((cap, HEADS, TW, TW), BF16), sds((cap, TW, D), F32), sds((cap, TW, D), BF16),
        ] + [sds(shape, BF16) for shape in weights],
        compiler_params=pltpu.CompilerParams(vmem_limit_bytes=VMEM_LIMIT),
        cost_estimate=pl.CostEstimate(flops=40_000_000_000, bytes_accessed=80_000_000, transcendentals=8_000_000),
    )(meta, ext, gext, vectors, wqkv, table, ka, kb)


def phi_parts(u):
    e = jnp.exp(u * u * -0.5)
    t = 1.0 / (1.0 + (0.3275911 * 0.7071067811865476) * jnp.abs(u))
    poly = t * (0.254829592 + t * (-0.284496736 + t * (1.421413741 + t * (-1.453152027 + t * 1.061405429))))
    tail = 0.5 * poly * e
    return jnp.where(u >= 0, 1.0 - tail, tail), e * 0.3989422804014327


def mlp_kernel(
    g_ref, x_ref, att_ref, wproj_ref, vec_ref, ff_ref, b1_ref,
    out_ref, n2_ref, act_ref, dpre_ref, dmix_ref, datt_ref, sums_ref, sum1_ref,
    acc_ref, dn_ref,
):
    @pl.when(pl.program_id(0) == 0)
    def _():
        sums_ref[...] = jnp.zeros_like(sums_ref)
        sum1_ref[...] = jnp.zeros_like(sum1_ref)

    gb = g_ref[...]
    g = gb.astype(F32)
    sums_ref[0] += fold8(g)
    hidden = x_ref[...].astype(F32) + mm(att_ref[...], wproj_ref[...]) + vec_ref[4:5]
    unit, inverse = norm(hidden)
    n2 = (unit * vec_ref[5:6] + vec_ref[6:7]).astype(BF16)
    n2_ref[...] = n2
    acc_ref[...] = hidden + vec_ref[7:8]
    parts, inner = ff_ref.shape[0], ff_ref.shape[2] // 2
    join = max(1, 1536 // inner)
    chunk = inner * join
    for c in range(parts // join):
        cols = slice(chunk * c, chunk * c + chunk)
        blocks = range(join * c, join * c + join)
        w1 = jnp.concatenate([ff_ref[i, :, :inner] for i in blocks], axis=1)
        w2t = jnp.concatenate([ff_ref[i, :, inner:] for i in blocks], axis=1)
        u = mm(n2, w1) + b1_ref[:, cols]
        dact = mm(gb, w2t)
        cdf, pdf = phi_parts(u)
        act = (u * cdf).astype(BF16)
        act_ref[:, cols] = act
        acc_ref[...] += mm_nt(act, w2t)
        dpre32 = dact * (cdf + u * pdf)
        dpre = dpre32.astype(BF16)
        dpre_ref[:, cols] = dpre
        sum1_ref[:, cols] += fold8(dpre32)
        step = mm_nt(dpre, w1)
        if c == 0:
            dn_ref[...] = step
        else:
            dn_ref[...] += step
    out_ref[...] = acc_ref[...].astype(BF16)
    dn = dn_ref[...]
    sums_ref[1] += fold8(dn * unit)
    sums_ref[2] += fold8(dn)
    dh = g + norm_back(dn, unit, inverse, vec_ref[5:6])
    dmix = dh.astype(BF16)
    dmix_ref[...] = dmix
    sums_ref[3] += fold8(dh)
    datt_ref[...] = mm_nt(dmix, wproj_ref[...]).astype(BF16)


def tile_rows(rows):
    return next(t for t in (416, 448, 224) if rows % t == 0)


def feed_forward(g, x, att, wproj, vectors, ff, b1, spare):
    cap = g.shape[0]
    rows = cap * TW
    tile = tile_rows(rows)
    sds = jax.ShapeDtypeStruct

    def tiled(width):
        return pl.BlockSpec((tile, width), lambda i: (i, 0))

    def kept(shape):
        zeros = (0,) * len(shape)
        return pl.BlockSpec(shape, lambda i: zeros, pipeline_mode=pl.Buffered(1))

    out, *rest = pl.pallas_call(
        mlp_kernel,
        grid=(rows // tile,),
        in_specs=[
            tiled(D), tiled(D), tiled(D), kept((D, D)), kept((8, D)), kept(ff.shape), kept((1, FF)),
        ],
        out_specs=[tiled(D), tiled(D), tiled(FF), tiled(FF), tiled(D), tiled(D), kept((4, 8, D)), kept((8, FF))],
        scratch_shapes=[pltpu.VMEM((tile, D), F32), pltpu.VMEM((tile, D), F32)],
        out_shape=[
            sds((rows + spare * TW, D), BF16), sds((rows, D), BF16), sds((rows, FF), BF16), sds((rows, FF), BF16),
            sds((rows, D), BF16), sds((rows, D), BF16), sds((4, 8, D), F32), sds((8, FF), F32),
        ],
        compiler_params=pltpu.CompilerParams(vmem_limit_bytes=VMEM_LIMIT),
        cost_estimate=pl.CostEstimate(flops=60_000_000_000, bytes_accessed=80_000_000, transcendentals=8_000_000),
    )(g.reshape(rows, D), x.reshape(rows, D), att.reshape(rows, D), wproj, vectors, ff, b1)
    return out.reshape(cap + spare, TW, D), rest[0], rest[1], rest[2], *[a.reshape(cap, TW, D) for a in rest[3:5]], *rest[5:]


MESH = pl.DeviceIdType.MESH
SHARD_ROWS = 192
SHARD_COLS = 384


def place():
    img, band = lax.axis_index("img"), lax.axis_index("band")
    return {"zh": img // 4, "zl": img // 2 % 2, "y": img % 2, "x": band // 2, "c": band % 2}


def partner(dim):
    img, band = lax.axis_index("img"), lax.axis_index("band")
    at = place()[dim]
    step = {"zh": 4, "zl": 2, "y": 1, "x": 2, "c": 1}[dim]
    move = step - 2 * step * at
    return (img, band + move) if dim in ("x", "c") else (img + move, band)


def peers():
    img, band = lax.axis_index("img"), lax.axis_index("band")
    return [(img, (band + d) % 4) for d in range(1, 4)], [((img + d) % 8, band) for d in range(1, 8)]


def greet():
    barrier = pltpu.get_barrier_semaphore()
    near_by, far = peers()
    for device in near_by + far:
        pl.semaphore_signal(barrier, inc=1, device_id=device, device_id_type=MESH)
    pl.semaphore_wait(barrier, 10)


class Halving:
    AXES = ("x", "zh", "zl", "y")

    def __init__(self, source, own, got, sems, order, rows):
        self.source, self.own, self.got, self.sems, self.order, self.rows = source, own, got, sems, order, rows
        self.at = place()

    @staticmethod
    def scratch(rows):
        shapes = [(2, 2, 2, 2), (2, 2, 2, 2), (2, 2, 2), (2, 2), (2,), (1,)]
        return [pltpu.VMEM(s + (rows, SHARD_COLS), BF16) for s in shapes] + [pltpu.SemaphoreType.DMA((11,))]

    def first(self):
        c = self.at["c"]
        send, recv, local = self.sems.at[0], self.sems.at[1], self.sems.at[10]
        for x in range(2):
            for img in range(8):
                spot = (x, img // 4, img // 2 % 2, img % 2)
                pltpu.make_async_remote_copy(
                    src_ref=self.source(x, img, 1 - c), dst_ref=self.got[0].at[spot], send_sem=send, recv_sem=recv,
                    device_id=partner("c"), device_id_type=MESH,
                ).start()
                pltpu.make_async_copy(self.source(x, img, c), self.own.at[spot], local).start()

    def first_done(self):
        send, recv, local = self.sems.at[0], self.sems.at[1], self.sems.at[10]
        whole = pltpu.make_async_remote_copy(
            src_ref=self.got[0], dst_ref=self.got[0], send_sem=send, recv_sem=recv,
            device_id=partner("c"), device_id_type=MESH,
        )
        whole.wait_send()
        whole.wait_recv()
        pltpu.make_async_copy(self.got[0], self.own, local).wait()

        def add(i, _):
            spot = (i // 8, i // 4 % 2, i // 2 % 2, i % 2)
            self.own[spot] = (self.own[spot].astype(F32) + self.got[0][spot].astype(F32)).astype(BF16)
            return 0

        lax.fori_loop(0, 16, add, 0)

    def index(self, k, dim=None):
        spot = []
        for axis in self.AXES:
            if axis == dim:
                spot.append(1 - self.at[axis])
            elif axis in self.order[:k]:
                spot.append(self.at[axis])
            else:
                spot.append(slice(None))
        return tuple(spot)

    def copy(self, k):
        dim = self.order[k]
        src = self.own.at[self.index(k, dim)]
        dst = self.got[k + 1].at[0] if k == 3 else self.got[k + 1]
        return pltpu.make_async_remote_copy(
            src_ref=src, dst_ref=dst, send_sem=self.sems.at[2 + 2 * k], recv_sem=self.sems.at[3 + 2 * k],
            device_id=partner(dim), device_id_type=MESH,
        )

    def step(self, k):
        self.copy(k).start()

    def step_done(self, k):
        self.copy(k).wait()
        done = self.order[: k + 1]
        free = [axis for axis in self.AXES if axis not in done]
        count = 2 ** len(free)

        def add(i, _):
            bits = {axis: (i // 2 ** (len(free) - 1 - j)) % 2 for j, axis in enumerate(free)}
            spot = tuple(bits[axis] if axis in bits else self.at[axis] for axis in self.AXES)
            self.own[spot] = (self.own[spot].astype(F32) + self.got[k + 1][tuple(bits[axis] for axis in free)].astype(F32)).astype(BF16)
            return 0

        if k < 3:
            lax.fori_loop(0, count, add, 0)

    def result(self):
        spot = tuple(self.at[axis] for axis in self.AXES)
        return self.own[spot].astype(F32) + self.got[4][0].astype(F32)


ORDERS = (("x", "y", "zh", "zl"), ("y", "x", "zh", "zl"))


def wide_source(ref, part):
    half = SHARD_ROWS // 2

    def source(x, img, c):
        row = pl.multiple_of((2 * x + c) * SHARD_ROWS + part * half, half)
        return ref.at[pl.ds(row, half), pl.ds(img * SHARD_COLS, SHARD_COLS)]

    return source


def each(group, name, *args):
    def body():
        for stream in group:
            getattr(stream, name)(*args)

    return body


def timeline(w, moments):
    for when, bodies in moments.items():
        @pl.when(w == when)
        def _(bodies=bodies):
            for body in bodies:
                body()


NEAR_CORE = 7
NEAR_CROSS = 5
CROSS_ROWS = 160


class Homeward:
    def __init__(self, windows, everything, sems):
        self.windows, self.all, self.sems = windows, everything, sems
        self.cap = everything.shape[0] - NEAR_CORE - NEAR_CROSS
        self.band = lax.axis_index("band")

    def inner(self):
        return (self.band == 1) | (self.band == 2)

    def outer(self):
        return (self.band == 0) | (self.band == 3)

    def keep(self):
        return pltpu.make_async_copy(self.windows, self.all.at[pl.ds(0, self.cap)], self.sems.at[4])

    def to_core(self, first, count):
        return pltpu.make_async_remote_copy(
            src_ref=self.windows.at[pl.ds(first, count)], dst_ref=self.all.at[pl.ds(self.cap, count)],
            send_sem=self.sems.at[0], recv_sem=self.sems.at[1], device_id=partner("c"), device_id_type=MESH,
        )

    def to_cross(self, sending):
        img = lax.axis_index("img")
        skip = (2 - self.band) if sending else (self.band - 1)
        rows = pl.ds(pl.multiple_of(skip * (TW - CROSS_ROWS), TW - CROSS_ROWS), CROSS_ROWS)
        return pltpu.make_async_remote_copy(
            src_ref=self.windows.at[pl.ds(0, NEAR_CROSS), rows],
            dst_ref=self.all.at[pl.ds(self.cap + NEAR_CORE, NEAR_CROSS), rows],
            send_sem=self.sems.at[2], recv_sem=self.sems.at[3], device_id=(img, 3 - self.band), device_id_type=MESH,
        )

    def send_cross(self):
        pl.when(self.inner())(lambda: self.to_cross(True).start())

    def send_core_inner(self):
        pl.when(self.inner())(lambda: self.to_core(NEAR_CROSS, NEAR_CORE).start())

    def send_core_outer(self):
        pl.when(self.outer())(lambda: self.to_core(0, 3).start())

    def finish(self):
        @pl.when(self.inner())
        def _():
            self.to_core(NEAR_CROSS, NEAR_CORE).wait_send()
            self.to_core(0, 3).wait_recv()
            self.to_cross(True).wait_send()
            self.to_cross(False).wait_recv()

        @pl.when(self.outer())
        def _():
            self.to_core(0, 3).wait_send()
            self.to_core(NEAR_CROSS, NEAR_CORE).wait_recv()


class Gather:
    def __init__(self, block, out, sems):
        self.block, self.out, self.sems = block, out, sems
        img, self.band = lax.axis_index("img"), lax.axis_index("band")
        self.z, self.y = img // 2, img % 2
        self.x, self.c = self.band // 2, self.band % 2

    def where(self, dz, fx, fy):
        img = (self.z + 4 - dz) % 4 * 2 + (1 - self.y if fy else self.y)
        return img, (1 - self.x if fx else self.x) * 2 + self.c

    def move(self, k, dz, fx, fy, device):
        img, band = self.where(dz, fx, fy)
        own = (dz, fx, fy) == (0, 0, 0)
        return pltpu.make_async_remote_copy(
            src_ref=self.block if own else self.out.at[img, band], dst_ref=self.out.at[img, band],
            send_sem=self.sems.at[0, k], recv_sem=self.sems.at[1, k], device_id=device, device_id_type=MESH,
        )

    def along_z(self, d):
        return self.move(d - 1, 0, 0, 0, ((self.z + d) % 4 * 2 + self.y, self.band))

    def along_x(self, dz):
        return self.move(3 + dz, dz, 0, 0, partner("x"))

    def along_y(self, fx, dz):
        return self.move(7 + 4 * fx + dz, dz, fx, 0, partner("y"))

    def to_core(self, fy, fx, dz):
        return self.move(15 + 8 * fy + 4 * fx + dz, dz, fx, fy, partner("c"))

    def keep(self):
        img, band = self.where(0, 0, 0)
        return pltpu.make_async_copy(self.block, self.out.at[img, band], self.sems.at[0, 31])

    def pass_on(self, dz):
        self.along_x(dz).start()
        self.along_y(0, dz).start()
        self.to_core(0, 0, dz).start()

    def begin(self):
        self.keep().start()
        for d in range(1, 4):
            self.along_z(d).start()
        self.pass_on(0)

    def run(self, then):
        for dz in range(1, 4):
            self.along_z(dz).wait_recv()
            self.pass_on(dz)
        then()
        for dz in range(4):
            self.along_x(dz).wait_recv()
            self.along_y(1, dz).start()
            self.to_core(0, 1, dz).start()
        for fx in range(2):
            for dz in range(4):
                self.along_y(fx, dz).wait_recv()
                self.to_core(1, fx, dz).start()
        for d in range(1, 4):
            self.along_z(d).wait_send()
        for dz in range(4):
            self.along_x(dz).wait_send()
            for fx in range(2):
                self.along_y(fx, dz).wait_send()
                for fy in range(2):
                    self.to_core(fy, fx, dz).wait()
        self.keep().wait()


CROSS_HALO = 10


class Edges:
    def __init__(self, rows, ext, zero, sems):
        self.rows, self.ext, self.zero, self.sems = rows, ext, zero, sems
        self.band = lax.axis_index("band")
        self.own_rows = rows.shape[1]

    def inner(self):
        return (self.band == 1) | (self.band == 2)

    def keep(self):
        return pltpu.make_async_copy(self.rows, self.ext.at[:, pl.ds(HALO, self.own_rows)], self.sems.at[0])

    def empty(self):
        at = self.band // 3 * (HALO + self.own_rows)
        return [
            pltpu.make_async_copy(self.zero, self.ext.at[m, pl.ds(at, HALO)], self.sems.at[1 + m]) for m in range(2)
        ]

    def core(self, sending):
        odd = self.band % 2
        far = self.own_rows - HALO
        there = (odd if sending else 1 - odd) * (HALO + self.own_rows)
        return pltpu.make_async_remote_copy(
            src_ref=self.rows.at[:, pl.ds((1 - odd) * far, HALO)], dst_ref=self.ext.at[:, pl.ds(there, HALO)],
            send_sem=self.sems.at[3], recv_sem=self.sems.at[4], device_id=partner("c"), device_id_type=MESH,
        )

    def cross(self, sending):
        img = lax.axis_index("img")
        m = 2 - self.band
        far = self.own_rows - CROSS_HALO
        to = m if sending else 1 - m
        there = to * (HALO - CROSS_HALO) + (1 - to) * (HALO + self.own_rows)
        return pltpu.make_async_remote_copy(
            src_ref=self.rows.at[m, pl.ds(m * far, CROSS_HALO)], dst_ref=self.ext.at[to, pl.ds(there, CROSS_HALO)],
            send_sem=self.sems.at[5], recv_sem=self.sems.at[6], device_id=(img, 3 - self.band), device_id_type=MESH,
        )

    def start_cross(self):
        pl.when(self.inner())(lambda: self.cross(True).start())

    def start(self):
        self.core(True).start()
        self.keep().start()

        @pl.when(jnp.logical_not(self.inner()))
        def _():
            for copy in self.empty():
                copy.start()

    def finish(self):
        self.core(True).wait_send()
        self.core(False).wait_recv()
        self.keep().wait()

        @pl.when(self.inner())
        def _():
            self.cross(True).wait_send()
            self.cross(False).wait_recv()

        @pl.when(jnp.logical_not(self.inner()))
        def _():
            for copy in self.empty():
                copy.wait()


def pack_kernel(wqkv_ref, wproj_ref, small_ref, relr_ref, relc_ref, w1_ref, w2t_ref, block_ref, ff_ref):
    rows, wide = wqkv_ref.shape
    block_ref[:rows, :wide] = wqkv_ref[...]
    block_ref[:rows, wide:] = wproj_ref[...]
    parts = [ref[...] for ref in (small_ref, relr_ref, relc_ref)]
    rest = block_ref.shape[1] - sum(part.shape[1] for part in parts)
    block_ref[rows:] = jnp.concatenate(parts + [jnp.zeros((small_ref.shape[0], rest), BF16)], axis=1)
    inner = w1_ref.shape[1]
    ff_ref[:, :inner] = w1_ref[...]
    ff_ref[:, inner:] = w2t_ref[...]


def pack(wqkv, wproj, small, relr, relc, w1, w2t):
    rows = wqkv.shape[0]
    return pl.pallas_call(
        pack_kernel,
        out_shape=[
            jax.ShapeDtypeStruct((rows + small.shape[0], wqkv.shape[1] + wproj.shape[1]), BF16),
            jax.ShapeDtypeStruct((rows, 2 * w1.shape[1]), BF16),
        ],
        cost_estimate=pl.CostEstimate(flops=0, bytes_accessed=1_000_000, transcendentals=0),
    )(wqkv, wproj, small, relr, relc, w1, w2t)


def entry_kernel(
    block_ref, x_ref, g_ref, all_ref, xext_ref, gext_ref, zero_ref, xin_ref, gin_ref, lsems, gsems, xsems, esems,
):
    loads = [pltpu.make_async_copy(x_ref, xin_ref, lsems.at[0]), pltpu.make_async_copy(g_ref, gin_ref, lsems.at[1])]
    for load in loads:
        load.start()
    zero_ref[...] = jnp.zeros_like(zero_ref)
    edges = [Edges(xin_ref, xext_ref, zero_ref, xsems), Edges(gin_ref, gext_ref, zero_ref, esems)]
    greet()
    gather = Gather(block_ref, all_ref, gsems)
    gather.begin()

    def next_edges(n):
        loads[n].wait()
        edges[n].start_cross()
        edges[n].start()

    next_edges(0)
    gather.run(lambda: next_edges(1))
    for item in edges:
        item.finish()


def entry(block, x, g):
    sds = jax.ShapeDtypeStruct
    ext = sds((2, x.shape[1] + 2 * HALO, SIDE, D), BF16)
    inside, anywhere = pl.BlockSpec(memory_space=pltpu.VMEM), pl.BlockSpec(memory_space=pl.ANY)
    return pl.pallas_call(
        entry_kernel,
        in_specs=[inside, anywhere, anywhere],
        out_specs=[anywhere] * 3,
        out_shape=[sds((8, 4) + block.shape, BF16), ext, ext],
        scratch_shapes=[
            pltpu.VMEM((HALO, SIDE, D), BF16), pltpu.VMEM(x.shape, BF16), pltpu.VMEM(x.shape, BF16),
            pltpu.SemaphoreType.DMA((2,)), pltpu.SemaphoreType.DMA((2, 32)), pltpu.SemaphoreType.DMA((7,)),
            pltpu.SemaphoreType.DMA((7,)),
        ],
        compiler_params=pltpu.CompilerParams(vmem_limit_bytes=VMEM_LIMIT, collective_id=3, has_side_effects=True),
    )(block, x, g)


def attn_bwd_kernel(
    meta_ref, qkv_ref, p_ref, inv_ref, att_ref, datt_ref, table_ref, kback_ref, *rest,
):
    w = pl.program_id(0)
    if len(rest) == 3:
        dqkv_ref, rel_ref, bias_ref = rest
        streams = None
    else:
        fc1_ref, fc2_ref, dqkv_ref, rel_ref, bias_ref, part_ref, sum2_ref = rest[:7]
        half = SHARD_ROWS // 2
        streams = []
        for n in range(4):
            own, *got, sems = rest[7 + 7 * n : 14 + 7 * n]
            source = wide_source(fc2_ref if n < 2 else fc1_ref, n % 2)
            streams.append(Halving(source, own, got, sems, ORDERS[n % 2], half))
        ones, twos = streams[:2], streams[2:]
        timeline(
            w,
            {
                0: [greet, each(streams, "first")],
                2: [each(ones, "first_done"), each(ones, "step", 0), each(twos, "first_done")],
                5: [each(ones, "step_done", 0), each(ones, "step", 1), each(twos, "step", 0)],
                7: [each(ones, "step_done", 1), each(ones, "step", 2)],
                10: [each(twos, "step_done", 0), each(twos, "step", 1), each(ones, "step_done", 2), each(ones, "step", 3)],
            },
        )

    @pl.when(w == 0)
    def _():
        rel_ref[...] = jnp.zeros_like(rel_ref)
        bias_ref[...] = jnp.zeros_like(bias_ref)

    lane = iota((TW, LANES), 1)
    low_half = lane < 64
    onehot = kback_ref[...]
    for p in range(PAIRS):
        q = qkv_ref[:, LANES * p : LANES * p + LANES]
        k8 = qkv_ref[:, D + LANES * p : D + LANES * p + LANES]
        v = qkv_ref[:, 2 * D + LANES * p : 2 * D + LANES * p + LANES]
        cols = slice(LANES * p, LANES * p + LANES)
        da = datt_ref[:, cols].astype(F32) * inv_ref[:, cols]
        da_low = da.astype(BF16)
        prod = da_low.astype(F32) * att_ref[:, cols].astype(F32)
        keys = jnp.concatenate([k8, onehot], axis=1)
        da_t = da.T.astype(BF16)
        q_t = q.astype(F32).T.astype(BF16)
        zero = jnp.zeros_like(v)
        dqx, dv_t, dk_t = [], [], []
        for h in range(2):
            mine = low_half if h == 0 else ~low_half
            centre = jnp.sum(jnp.where(mine, prod, 0.0), axis=-1, keepdims=True)
            dp = mm_nt(da_low, jnp.where(mine, v, zero))
            e = p_ref[2 * p + h]
            ds = (e.astype(F32) * (dp - centre)).astype(BF16)
            dqx.append(mm(ds, keys))
            dv_t.append(mm(da_t[64 * h : 64 * h + 64], e))
            dk_t.append(mm(q_t[64 * h : 64 * h + 64], ds))
        dq = jnp.where(low_half, dqx[0][:, :LANES], dqx[1][:, :LANES])
        drc = jnp.where(low_half, dqx[0][:, LANES:], dqx[1][:, LANES:])
        part = lane & 63
        rows = roll_rows(jnp.where(part < 16, drc, 0.0), False)
        cols_part = roll_cols(jnp.where((part >= 16) & (part < 32), drc, 0.0), LANES - 16)
        skew = jnp.concatenate([rows, cols_part], axis=1).astype(BF16)
        dq = dq + mm_nt(skew, table_ref[...])
        rel_ref[...] += mm(q_t, skew)
        dv = jnp.concatenate(dv_t, axis=0).T
        dk = (jnp.concatenate(dk_t, axis=0) * 0.125).T
        dqkv_ref[:, cols] = dq.astype(BF16)
        dqkv_ref[:, D + LANES * p : D + LANES * p + LANES] = dk.astype(BF16)
        dqkv_ref[:, 2 * D + LANES * p : 2 * D + LANES * p + LANES] = dv.astype(BF16)
        bias_ref[0, :, cols] += fold8(dq)
        bias_ref[1, :, cols] += fold8(dv)

    if streams:
        @pl.when(w == pl.num_programs(0) - 1)
        def _():
            each(ones, "step_done", 3)()
            sum2_ref[:half] = ones[0].result()
            sum2_ref[half:] = ones[1].result()
            each(twos, "step_done", 1)()
            for n, stream in enumerate(twos):
                part_ref[n] = stream.own[stream.at["x"], :, :, stream.at["y"]]


def attention_backward(meta, qkv, p, inv, att, datt, table, kback, beside=()):
    cap = meta.shape[0]
    sds = jax.ShapeDtypeStruct
    anywhere = pl.BlockSpec(memory_space=pl.ANY)
    shard = (SHARD_ROWS, SHARD_COLS)
    more_specs, more_outs, scratch, extra = [], [], [], {}
    if beside:
        part = (2, 2, 2, SHARD_ROWS // 2, SHARD_COLS)
        more_specs = [whole(part), whole(shard)]
        more_outs = [sds(part, BF16), sds(shard, F32)]
        scratch = Halving.scratch(SHARD_ROWS // 2) * 4
        extra = dict(collective_id=1, has_side_effects=True)
    return pl.pallas_call(
        attn_bwd_kernel,
        grid_spec=pltpu.PrefetchScalarGridSpec(
            num_scalar_prefetch=1,
            grid=(cap,),
            in_specs=[
                per_window(TW, 3 * D), per_window(HEADS, TW, TW), per_window(TW, D), per_window(TW, D),
                per_window(TW, D), whole((LANES, 256)), whole((TW, LANES)),
            ] + [anywhere] * len(beside),
            out_specs=[per_window(TW, 3 * D), whole((LANES, 256)), whole((2, 8, D))] + more_specs,
            scratch_shapes=scratch,
        ),
        out_shape=[sds((cap, TW, 3 * D), BF16), sds((LANES, 256), F32), sds((2, 8, D), F32)] + more_outs,
        compiler_params=pltpu.CompilerParams(vmem_limit_bytes=VMEM_LIMIT, **extra),
        cost_estimate=pl.CostEstimate(flops=60_000_000_000, bytes_accessed=80_000_000, transcendentals=0),
    )(meta, qkv, p, inv, att, datt, table, kback, *beside)


def rel_from(acc):
    def one(block):
        own = block[:64, :32] + block[64:, 64:96]
        return own[:, :RELS].T

    return one(acc[:, :LANES]), one(acc[:, LANES:])


def put_window(target, y, acc_ref, row0):
    picks = jnp.where(iota((TW, 256), 1) == target, 1.0, 0.0).astype(BF16)
    for q in range(4):
        n = 4 if q < 3 else 2
        t = slice(64 * q, 64 * q + STRIDE * n)
        part = lax.dot_general(
            picks[t, : 64 * n], y[t], (((0,), (0,)), ((), ())), preferred_element_type=F32
        )
        acc_ref[pl.ds(row0 + 4 * q, n)] += part.reshape(n, SIDE, D).astype(acc_ref.dtype)


def scatter_kernel(meta_ref, y_ref, ext_ref, acc_ref):
    w = pl.program_id(0)

    @pl.when(w == 0)
    def _():
        acc_ref[...] = jnp.zeros_like(acc_ref)

    put_window(token_target(meta_ref, w), y_ref[...], acc_ref, meta_ref[w, 0])

    @pl.when(w == pl.num_programs(0) - 1)
    def _():
        def copy(i, _):
            ext_ref[i] = acc_ref[i].astype(BF16)
            return 0
        lax.fori_loop(0, ext_ref.shape[0], copy, 0)


def scatter(meta, y, ext_rows):
    cap = meta.shape[0]
    return pl.pallas_call(
        scatter_kernel,
        grid_spec=pltpu.PrefetchScalarGridSpec(
            num_scalar_prefetch=1,
            grid=(cap,),
            in_specs=[per_window(TW, D)],
            out_specs=whole((ext_rows, SIDE, D)),
            scratch_shapes=[pltpu.VMEM((ext_rows, SIDE, D), F32)],
        ),
        out_shape=jax.ShapeDtypeStruct((ext_rows, SIDE, D), BF16),
        compiler_params=pltpu.CompilerParams(vmem_limit_bytes=VMEM_LIMIT),
        cost_estimate=pl.CostEstimate(flops=5_000_000_000, bytes_accessed=20_000_000, transcendentals=0),
    )(meta, y)


def last_kernel(
    meta_ref, dqkv_ref, wqkv_ref, x_ref, dmix_ref, gain_ref, ext_ref, sums_ref, acc_ref,
):
    w = pl.program_id(0)

    @pl.when(w == 0)
    def _():
        acc_ref[...] = jnp.zeros_like(acc_ref)
        sums_ref[...] = jnp.zeros_like(sums_ref)

    target = token_target(meta_ref, w)
    dn = jnp.zeros((TW, D), F32)
    for c in range(3):
        cols = slice(D * c, D * c + D)
        dn = dn + mm_nt(dqkv_ref[:, cols], wqkv_ref[:, cols])
    dn = jnp.where(target >= 0, dn, 0.0)
    unit, inverse = norm(x_ref[...].astype(F32))
    sums_ref[0] += fold8(dn * unit)
    sums_ref[1] += fold8(dn)
    grad = dmix_ref[...].astype(F32) + norm_back(dn, unit, inverse, gain_ref[0:1])
    put_window(target, grad.astype(BF16), acc_ref, meta_ref[w, 0])

    @pl.when(w == pl.num_programs(0) - 1)
    def _():
        def copy(i, _):
            ext_ref[i] = acc_ref[i].astype(BF16)
            return 0
        lax.fori_loop(0, ext_ref.shape[0], copy, 0)


def last_norm(meta, dqkv, wqkv, x, dmix, gain, ext_rows):
    cap = meta.shape[0]
    sds = jax.ShapeDtypeStruct
    return pl.pallas_call(
        last_kernel,
        grid_spec=pltpu.PrefetchScalarGridSpec(
            num_scalar_prefetch=1,
            grid=(cap,),
            in_specs=[
                per_window(TW, 3 * D), whole((D, 3 * D)), per_window(TW, D), per_window(TW, D), whole((8, D)),
            ],
            out_specs=[whole((ext_rows, SIDE, D)), whole((2, 8, D))],
            scratch_shapes=[pltpu.VMEM((ext_rows, SIDE, D), F32)],
        ),
        out_shape=[sds((ext_rows, SIDE, D), BF16), sds((2, 8, D), F32)],
        compiler_params=pltpu.CompilerParams(vmem_limit_bytes=VMEM_LIMIT),
        cost_estimate=pl.CostEstimate(flops=15_000_000_000, bytes_accessed=30_000_000, transcendentals=0),
    )(meta, dqkv, wqkv, x, dmix, gain)


class SmallSum:
    def __init__(self, mine, got_band, got_img, sems, part):
        self.mine, self.got, self.sems, self.part = mine, (got_band, got_img), sems, part

    @staticmethod
    def scratch(shape, part):
        return [
            pltpu.VMEM(shape, F32), pltpu.VMEM((3,) + shape, F32), pltpu.VMEM((7,) + part, F32),
            pltpu.SemaphoreType.DMA((2, 2, 7)),
        ]

    def copies(self, k):
        return [
            pltpu.make_async_remote_copy(
                src_ref=self.part(device[0]) if k else self.mine, dst_ref=self.got[k].at[d],
                send_sem=self.sems.at[k, 0, d], recv_sem=self.sems.at[k, 1, d], device_id=device, device_id_type=MESH,
            )
            for d, device in enumerate(peers()[k])
        ]

    def send(self, k):
        for copy in self.copies(k):
            copy.start()

    def add(self):
        for copy in self.copies(0):
            copy.wait()
        self.mine[...] = self.mine[...] + self.got[0][0] + self.got[0][1] + self.got[0][2]

    def result(self):
        for copy in self.copies(1):
            copy.wait()
        total = self.part(lax.axis_index("img"))[...]
        for d in range(7):
            total = total + self.got[1][d]
        return total


def deal(rows_ref, parts_ref, rows, wide):
    groups = parts_ref.shape[0]
    share = D // groups
    for i in range(groups):
        parts_ref[i, :rows, :share] = rows_ref[:rows, share * i : share * i + share]
        for k in range(wide):
            at = share * (wide * i + k)
            parts_ref[i, rows + k : rows + k + 1, :share] = rows_ref[rows + at // D : rows + at // D + 1, at % D : at % D + share]


HOME_ROWS = 8


def home_kernel(
    table_ref, own_ref, core_ref, cross_ref, grad_ref, total_ref, ln_ref, rel_ref, q_ref,
    output_ref, input_grad_ref, vec_refs, b1_ref, relr_ref, relc_ref, wq_ref, wp_ref,
    out_ref, sems,
):
    step = pl.program_id(0)
    per_image = pl.num_programs(0) // 2
    m = step // per_image
    top, left = table_ref[m, 25], table_ref[m, 26]
    first = table_ref[m, 27] + (step - m * per_image) * HOME_ROWS

    @pl.when(step == 0)
    def _():
        cap = own_ref.shape[0]
        loads = [
            pltpu.make_async_copy(ref, out_ref.at[pl.ds(at, ref.shape[0])], sems.at[n])
            for n, (ref, at) in enumerate(((own_ref, 0), (core_ref, cap), (cross_ref, cap + NEAR_CORE)))
        ]
        for load in loads:
            load.start()
        share = vec_refs[0].shape[1]
        ln, total = ln_ref[:, :share], total_ref[:, :share]
        for ref, row in zip(vec_refs, (ln[0:1], ln[1:2], total[0:1], total[1:2], total[5:6], total[3:4], total[4:5], total[2:3])):
            ref[...] = row
        b1_ref[...] = jnp.concatenate([total[6 + k : 7 + k] for k in range(4)], axis=1)
        relr_ref[...] = rel_ref[:, :RELS]
        relc_ref[...] = rel_ref[:, LANES : LANES + RELS]
        wq_ref[...] = q_ref[:, : 3 * share]
        wp_ref[...] = q_ref[:, 3 * share :]
        for load in loads:
            load.wait()

    col = iota((SIDE, GRID * STRIDE), 0) + left
    spot = iota((SIDE, GRID * STRIDE), 1)
    picks = jnp.where((spot >> 4) * WIN + (spot & 15) == col, 1.0, 0.0)
    picks = jnp.where((spot & 15) < WIN, picks, 0.0).astype(BF16)
    for i in range(HOME_ROWS):
        at = i + first + top
        r = at // WIN
        a = pl.multiple_of((at - r * WIN) * STRIDE, STRIDE)
        slots = [table_ref[m, r * GRID + c] for c in range(GRID)]
        for source, target in ((out_ref, output_ref), (grad_ref, input_grad_ref)):
            tokens = jnp.concatenate([source[slot, pl.ds(a, STRIDE)] for slot in slots], axis=0)
            target[0, i] = mm(picks, tokens).astype(target.dtype)


def home(table, sources, rows):
    per_image = rows // HOME_ROWS
    sds = jax.ShapeDtypeStruct
    tiled = pl.BlockSpec((1, HOME_ROWS, SIDE, D), lambda w, meta: (w // per_image, w % per_image, 0, 0))
    shapes = [[(1, D // 8)] * 8, (1, FF // 8)] + [(HEAD // 4, RELS)] * 2 + [
        (SHARD_ROWS, 3 * D // 8), (SHARD_ROWS, D // 8),
    ]
    is_shape = lambda shape: isinstance(shape, tuple)
    return pl.pallas_call(
        home_kernel,
        grid_spec=pltpu.PrefetchScalarGridSpec(
            num_scalar_prefetch=1,
            grid=(2 * per_image,),
            in_specs=[pl.BlockSpec(memory_space=pl.ANY)] * 3 + [whole(a.shape) for a in sources[3:]],
            scratch_shapes=[pltpu.VMEM(sources[3].shape, BF16), pltpu.SemaphoreType.DMA((3,))],
            out_specs=[tiled, tiled] + jax.tree.map(whole, shapes, is_leaf=is_shape),
        ),
        out_shape=[sds((2, rows, SIDE, D), BF16), sds((2, rows, SIDE, D), F32)]
        + jax.tree.map(lambda shape: sds(shape, F32), shapes, is_leaf=is_shape),
        compiler_params=pltpu.CompilerParams(vmem_limit_bytes=VMEM_LIMIT),
        cost_estimate=pl.CostEstimate(flops=500_000_000, bytes_accessed=20_000_000, transcendentals=0),
    )(table, *sources)


def home_table(plan, offsets, band, band_rows):
    own = np.full((4, 2, WINDOWS), 0, np.int32)
    for b in range(4):
        for slot, (m, w) in enumerate(plan[b]):
            if w >= 0:
                own[b, m, w] = slot
        odd, cap = b % 2, len(plan[b])
        mate = plan[b ^ 1]
        sent = mate[:3] if (b ^ 1) in (0, 3) else mate[NEAR_CROSS : NEAR_CROSS + NEAR_CORE]
        for slot, (m, w) in enumerate(sent):
            own[b, m, w] = cap + slot
        if b in (1, 2):
            for slot, (m, w) in enumerate(plan[3 - b][:NEAR_CROSS]):
                own[b, m, w] = cap + NEAR_CORE + slot
    rows = jnp.asarray(own)[band]
    first = jnp.full((2, 1), band_rows, jnp.int32) * band
    return jnp.concatenate([rows, offsets.astype(jnp.int32), first, jnp.zeros((2, 4), jnp.int32)], axis=1)


def last_fused_kernel(
    meta_ref, dqkv_ref, wqkv_ref, x_ref, dmix_ref, gain_ref, dwq_ref, dwp_ref, bias_ref, sums_ref, fc1_ref, rel_ref,
    all_ref, shard_ref, total_ref, rels_ref, ln_ref,
    grad_ref, ln_acc, q_ref, *rest,
):
    w = pl.program_id(0)
    end = pl.num_programs(0) - 1
    half = SHARD_ROWS // 2
    streams = []
    for n, order in enumerate(ORDERS):
        own, *got, sems = rest[7 * n : 7 * n + 7]

        def source(x, img, c, n=n):
            row = pl.multiple_of((2 * x + c) * SHARD_ROWS + n * half, half)
            return q_ref.at[img, pl.ds(row, half)]

        streams.append(Halving(source, own, got, sems, order, half))
    rest = rest[14:]
    small_parts, ln_parts = rest[12:14]
    features = HEAD // 4
    own_features = pl.ds(pl.multiple_of(lax.axis_index("band") * features, features), features)
    small = SmallSum(*rest[:4], lambda i: small_parts.at[i])
    rel = SmallSum(*rest[4:8], lambda i: rest[4].at[own_features])
    ln = SmallSum(*rest[8:12], lambda i: ln_parts.at[i])
    back = Homeward(grad_ref, all_ref, rest[14])

    def start():
        groups = q_ref.shape[0]
        wide, share = 3 * D // groups, D // groups
        for i in range(groups):
            q_ref[i] = jnp.concatenate(
                [dwq_ref[:, wide * i : wide * i + wide], dwp_ref[:, share * i : share * i + share]], axis=1
            )
        greet()
        each(streams, "first")()

    def prepare():
        for r in range(2):
            small.mine[r : r + 1] = jnp.sum(bias_ref[r], axis=0, keepdims=True)
        for r in range(4):
            small.mine[2 + r : 3 + r] = jnp.sum(sums_ref[r], axis=0, keepdims=True)
            small.mine[6 + r : 7 + r] = jnp.sum(fc1_ref[:, D * r : D * r + D], axis=0, keepdims=True)
        small.mine[10:] = jnp.zeros((6, D), F32)
        small_parts[...] = jnp.zeros_like(small_parts)
        ln_parts[...] = jnp.zeros_like(ln_parts)
        rel.mine[...] = rel_ref[:64] + pltpu.roll(rel_ref[64:], 192, 1)
        small.send(0)
        rel.send(0)
        ln_acc[...] = jnp.zeros_like(ln_acc)

    def middle():
        small.add()
        rel.add()
        deal(small.mine, small_parts, 6, 4)
        small.send(1)
        rel.send(1)

    def finish():
        total_ref[...] = small.result()
        rels_ref[...] = rel.result()

    timeline(
        w,
        {
            0: [start, prepare],
            2: [each(streams, "first_done"), each(streams, "step", 0)],
            3: [middle, back.send_core_outer],
            6: [each(streams, "step_done", 0), each(streams, "step", 1), finish],
            8: [each(streams, "step_done", 1), each(streams, "step", 2), back.send_cross],
            12: [each(streams, "step_done", 2), each(streams, "step", 3), back.send_core_inner],
        },
    )

    target = token_target(meta_ref, w)
    dn = jnp.zeros((TW, D), F32)
    for c in range(3):
        cols = slice(D * c, D * c + D)
        dn = dn + mm_nt(dqkv_ref[:, cols], wqkv_ref[:, cols])
    dn = jnp.where(target >= 0, dn, 0.0)
    unit, inverse = norm(x_ref[...].astype(F32))
    ln_acc[0] += fold8(dn * unit)
    ln_acc[1] += fold8(dn)
    grad = dmix_ref[...].astype(F32) + norm_back(dn, unit, inverse, gain_ref[0:1])
    grad_ref[w] = grad.astype(BF16)

    @pl.when(w == end)
    def _():
        back.keep().start()
        ln.mine[0:1] = jnp.sum(ln_acc[0], axis=0, keepdims=True)
        ln.mine[1:2] = jnp.sum(ln_acc[1], axis=0, keepdims=True)
        ln.mine[2:] = jnp.zeros((6, D), F32)
        ln.send(0)
        each(streams, "step_done", 3)()
        ln.add()
        deal(ln.mine, ln_parts, 2, 0)
        ln.send(1)
        for n, stream in enumerate(streams):
            shard_ref[half * n : half * n + half] = stream.result()
        back.keep().wait()
        back.finish()
        ln_ref[...] = ln.result()


def last_fused(meta, dqkv, wqkv, x, dmix, gain, dwq, dwp, bias_sums, sums, fc1_sum, rel_acc):
    cap = meta.shape[0]
    sds = jax.ShapeDtypeStruct
    half = SHARD_ROWS // 2
    anywhere = pl.BlockSpec(memory_space=pl.ANY)
    sums_out = [((SHARD_ROWS, SHARD_COLS), F32), ((16, LANES), F32), ((HEAD // 4, 256), F32), ((8, LANES), F32)]
    return pl.pallas_call(
        last_fused_kernel,
        grid_spec=pltpu.PrefetchScalarGridSpec(
            num_scalar_prefetch=1,
            grid=(cap,),
            in_specs=[
                per_window(TW, 3 * D), whole((D, 3 * D)), per_window(TW, D), per_window(TW, D), whole((8, D)),
                whole((D, 3 * D)), whole((D, D)), whole((2, 8, D)), whole((4, 8, D)), whole((8, FF)), whole((LANES, 256)),
            ],
            out_specs=[anywhere] + [whole(shape) for shape, _ in sums_out],
            scratch_shapes=[
                pltpu.VMEM((cap, TW, D), BF16), pltpu.VMEM((2, 8, D), F32), pltpu.VMEM((8, D, SHARD_COLS), BF16)
            ]
            + Halving.scratch(half) * 2
            + SmallSum.scratch((16, D), (16, LANES)) + SmallSum.scratch((HEAD, 256), (HEAD // 4, 256))
            + SmallSum.scratch((8, D), (8, LANES))
            + [pltpu.VMEM((8, 16, LANES), F32), pltpu.VMEM((8, 8, LANES), F32), pltpu.SemaphoreType.DMA((5,))],
        ),
        out_shape=[sds((cap + NEAR_CORE + NEAR_CROSS, TW, D), BF16)] + [sds(shape, dtype) for shape, dtype in sums_out],
        compiler_params=pltpu.CompilerParams(vmem_limit_bytes=VMEM_LIMIT, collective_id=2, has_side_effects=True),
        cost_estimate=pl.CostEstimate(flops=20_000_000_000, bytes_accessed=50_000_000, transcendentals=0),
    )(meta, dqkv, wqkv, x, dmix, gain, dwq, dwp, bias_sums, sums, fc1_sum, rel_acc)


def window_plan(images, bands):
    lists = [[] for _ in range(bands)]
    if images == 2 and bands == 4:
        spans = (
            ((0, 5, 8), (0, 0, 5), (1, 0, 5)),
            ((0, 10, 15), (0, 8, 10), (1, 5, 10)),
            ((1, 10, 15), (1, 15, 17), (0, 15, 20)),
            ((1, 17, 20), (1, 20, 25), (0, 20, 25)),
        )
        lists = [[(m, w) for m, first, last in row for w in range(first, last)] for row in spans]
    else:
        cuts = [
            [(WINDOWS * b + (bands - 1 if m % 2 else 0)) // bands for b in range(bands + 1)] for m in range(images)
        ]
        for m in range(images):
            for b in range(bands):
                lists[b] += [(m, w) for w in range(cuts[m][b], min(cuts[m][b + 1], WINDOWS))]
    cap = max(len(item) for item in lists)
    return np.array([item + [(0, -1)] * (cap - len(item)) for item in lists], np.int32)


HALO = 12


def near(images, bands, band_rows):
    return images == 2 and bands == 4 and band_rows == 16


CORE = [(0, 1), (1, 0), (2, 3), (3, 2)]
CROSS = [(1, 2), (2, 1)]


def extend(rows, band):
    images, band_rows = rows.shape[:2]
    if not near(images, lax.axis_size("band"), band_rows):
        full = lax.all_gather(rows, "band", axis=1, tiled=True)
        return jnp.pad(full, ((0, 0), (6, 6), (0, 0), (0, 0)))
    odd = band % 2 == 1
    top, bottom = rows[:, :HALO], rows[:, -HALO:]
    from_core = lax.ppermute(jnp.where(odd, top, bottom), "band", CORE)
    from_cross = lax.ppermute(jnp.where(odd, bottom[1], top[0]), "band", CROSS)
    zero = jnp.zeros_like(from_cross)
    above = jnp.where(odd, from_core, jnp.stack([zero, from_cross]))
    below = jnp.where(odd, jnp.stack([from_cross, zero]), from_core)
    return jnp.concatenate([above, rows, below], axis=1)


def collect(ext, band, images, band_rows):
    if not near(images, lax.axis_size("band"), band_rows):
        return lax.psum_scatter(ext[:, 6:-6], "band", scatter_dimension=1, tiled=True).astype(F32)
    odd = band % 2 == 1
    above, below = ext[:, :HALO], ext[:, -HALO:]
    from_core = lax.ppermute(jnp.where(odd, above, below), "band", CORE).astype(F32)
    from_cross = lax.ppermute(jnp.where(odd, below[0], above[1]), "band", CROSS).astype(F32)
    zero = jnp.zeros_like(from_cross)
    top = jnp.where(odd, from_core, jnp.stack([from_cross, zero]))
    bottom = jnp.where(odd, jnp.stack([zero, from_cross]), from_core)
    own = ext[:, HALO:-HALO].astype(F32)
    rest = band_rows - HALO
    return own + jnp.pad(top, ((0, 0), (0, rest), (0, 0), (0, 0))) + jnp.pad(bottom, ((0, 0), (rest, 0), (0, 0), (0, 0)))


def shards(
    image_tokens, pad_offsets, ln1_gain, ln1_bias, w_qkv, q_bias, v_bias, rel_rows, rel_cols, w_proj, proj_bias,
    ln2_gain, ln2_bias, w_fc1, fc1_bias, w_fc2, fc2_bias, out_grad,
):
    images, band_rows = image_tokens.shape[:2]
    bands, groups = lax.axis_size("band"), lax.axis_size("img")
    band, group = lax.axis_index("band"), lax.axis_index("img")
    axes = ("img", "band")

    part, wide = w_qkv.shape
    close = near(images, bands, band_rows)
    fused = close and groups == 8
    share = D // groups
    vector_rows = [ln1_gain, ln1_bias, q_bias, v_bias, proj_bias, ln2_gain, ln2_bias, fc2_bias]
    small = jnp.concatenate([v[None] for v in vector_rows] + [fc1_bias.reshape(4, share), jnp.zeros((4, share), BF16)])
    block_cols = wide + w_proj.shape[1]
    small_rows = 16
    if fused:
        block, ff_block = pack(w_qkv, w_proj, small, rel_rows.T, rel_cols.T, w_fc1, w_fc2.T)
        first, ext, gext = entry(block, image_tokens, out_grad)
    else:
        features = rel_rows.shape[1]
        rest = jnp.zeros((small_rows, block_cols - share - 2 * RELS), BF16)
        tables = [jnp.pad(rel.T, ((0, small_rows - features), (0, 0))) for rel in (rel_rows, rel_cols)]
        block = jnp.concatenate(
            [jnp.concatenate([w_qkv, w_proj], axis=1), jnp.concatenate([small, *tables, rest], axis=1)], axis=0
        )
        ff_block = jnp.concatenate([w_fc1, w_fc2.T], axis=1)
        first = lax.all_gather(block, axes, axis=0, tiled=False).reshape(groups, bands, part + small_rows, block_cols)
        ext, gext = extend(image_tokens, band), extend(out_grad, band)
    ff = lax.all_gather(ff_block, axes, axis=0, tiled=False).reshape(groups, bands * part, -1)
    tail = first[:, :, part:]
    vectors = tail[:, 0, :8, :share].transpose(1, 0, 2).reshape(8, D).astype(F32)
    fc1_shift = tail[:, 0, 8:12, :share].reshape(1, FF).astype(F32)
    features = HEAD // bands
    rels = [tail[0, :, :features, at : at + RELS].reshape(HEAD, RELS) for at in (share, share + RELS)]
    plan = jnp.asarray(window_plan(images, bands))[band]
    image, window = plan[:, 0], plan[:, 1]
    ext_per = band_rows + 2 * HALO if close else bands * band_rows + 12
    base = band_rows * band - HALO if close else -6
    live = window >= 0
    spot = jnp.maximum(window, 0)
    offsets = pad_offsets[image]
    row = spot // GRID * WIN - offsets[:, 0]
    col = spot % GRID * WIN - offsets[:, 1]
    meta = jnp.stack(
        [jnp.where(live, image * ext_per + row - base, HALO), col, row, live.astype(jnp.int32)], axis=1
    ).astype(jnp.int32)
    cap = meta.shape[0]
    ext_rows = images * ext_per

    ka, kb, kback = key_constants()
    ext, gext = ext.reshape(ext_rows, SIDE, D), gext.reshape(ext_rows, SIDE, D)
    if not fused:
        weights = first[:, :, :part].transpose(1, 2, 0, 3)
        wqkv, wproj = weights[..., :wide].reshape(D, 3 * D), weights[..., wide:].reshape(D, D)
    x, g, normed1, qkv, probs, inv, att, *weights = attention_forward(
        meta, ext, gext, vectors, first if fused else wqkv, rel_table(rels[0], rels[1], True), ka, kb
    )
    if fused:
        wqkv, wproj = weights
    out_win, normed2, act, d_pre, d_mixed, d_att, sums, sum_fc1 = feed_forward(
        g, x, att, wproj, vectors, ff, fc1_shift, 0
    )

    def flat(a):
        return a.reshape(-1, a.shape[-1])

    def weight_grad(left, right):
        return jnp.einsum("td,te->de", flat(left), flat(right), preferred_element_type=F32).astype(BF16)

    if fused:
        inner = (band == 1) | (band == 2)
        to_core = lax.dynamic_slice_in_dim(out_win, jnp.where(inner, NEAR_CROSS, 0), NEAR_CORE, 0)
        core_out = lax.ppermute(to_core, "band", CORE)
        cross_out = lax.ppermute(out_win[:NEAR_CROSS], "band", CROSS)
    d_fc2 = weight_grad(g, act)
    d_fc1 = weight_grad(normed2, d_pre)
    d_proj = weight_grad(att, d_mixed)
    if fused:
        d_fc1, d_fc2, core_out, cross_out = lax.optimization_barrier((d_fc1, d_fc2, core_out, cross_out))
    d_qkv, rel_acc, bias_sums, *done = attention_backward(
        meta, qkv, probs, inv, att, d_att, rel_table(rels[0], rels[1], False), kback,
        (d_fc1, d_fc2) if fused else (),
    )
    d_wqkv = weight_grad(normed1, d_qkv)

    if fused:
        partial, g_fc2 = done

        def fold(value, axis, bit, step):
            mine = lax.dynamic_index_in_dim(value, bit, axis, keepdims=False)
            other = lax.dynamic_index_in_dim(value, 1 - bit, axis, keepdims=False)
            came = lax.ppermute(other, "img", [(i, i ^ step) for i in range(groups)])
            return mine.astype(F32) + came.astype(F32)

        partial = fold(partial, 1, group // 4, 4).astype(BF16)
        g_fc1 = fold(partial, 1, group // 2 % 2, 2).reshape(part, FF // groups)
        all_grad, q_shard, total, rel_total, ln_total = last_fused(
            meta, d_qkv, wqkv, x, d_mixed, vectors, d_wqkv, d_proj, bias_sums, sums, sum_fc1, rel_acc
        )
        output, input_grad, shares, b1_share, d_rel_rows, d_rel_cols, g_qkv, g_proj = home(
            home_table(window_plan(images, bands), pad_offsets, band, band_rows),
            (out_win, core_out, cross_out, all_grad, total, ln_total, rel_total, q_shard), band_rows,
        )
        ln1g, ln1b, qb, vb, pb, ln2g, ln2b, b2 = [share.reshape(-1) for share in shares]
        return (
            output, input_grad, ln1g, ln1b, g_qkv, qb, vb, d_rel_rows.T, d_rel_cols.T, g_proj, pb, ln2g, ln2b, g_fc1,
            b1_share.reshape(-1), g_fc2.T, b2,
        )
    else:
        out_ext = scatter(meta, out_win, ext_rows).reshape(images, ext_per, SIDE, D)
        output = collect(out_ext, band, images, band_rows).astype(BF16)
        in_ext, sums1 = last_norm(meta, d_qkv, wqkv, x, d_mixed, vectors, ext_rows)
        input_grad = collect(in_ext.reshape(images, ext_per, SIDE, D), band, images, band_rows)

        def reduce(grad):
            grad = lax.psum_scatter(grad, "img", scatter_dimension=1, tiled=True)
            return lax.psum_scatter(grad, "band", scatter_dimension=0, tiled=True).astype(F32)

        g_fc1, g_fc2, g_qkv, g_proj = reduce(d_fc1), reduce(d_fc2), reduce(d_wqkv), reduce(d_proj)
        ln_total, bias_total, sum_total, fc1_total, d_rel_rows, d_rel_cols = lax.psum(
            (jnp.sum(sums1, 1), jnp.sum(bias_sums, 1), jnp.sum(sums, 1), jnp.sum(sum_fc1, 0)) + rel_from(rel_acc), axes
        )

    def img_share(vector):
        n = vector.shape[0] // groups
        return lax.dynamic_slice_in_dim(vector, group * n, n, 0)

    def band_share(table):
        n = table.shape[1] // bands
        return lax.dynamic_slice_in_dim(table, band * n, n, 1)

    return (
        output,
        input_grad,
        img_share(ln_total[0]),
        img_share(ln_total[1]),
        g_qkv,
        img_share(bias_total[0]),
        img_share(bias_total[1]),
        band_share(d_rel_rows),
        band_share(d_rel_cols),
        g_proj,
        img_share(sum_total[3]),
        img_share(sum_total[1]),
        img_share(sum_total[2]),
        g_fc1,
        img_share(fc1_total),
        g_fc2.T,
        img_share(sum_total[0]),
    )


def solution(mesh):
    tokens, vector, matrix = P("img", "band", None, None), P("img"), P("band", "img")
    table, wide = P(None, "band"), P("img", "band")
    return jax.shard_map(
        shards,
        mesh=mesh,
        in_specs=(
            tokens, P("img", None), vector, vector, matrix, vector, vector, table, table, matrix, vector, vector,
            vector, matrix, vector, wide, vector, tokens,
        ),
        out_specs=(
            tokens, tokens, vector, vector, matrix, vector, vector, table, table, matrix, vector, vector, vector,
            matrix, vector, wide, vector,
        ),
        check_vma=False,
    )
```

```python
import functools
import numpy as np
import jax
import jax.numpy as jnp
from jax import lax
from jax.sharding import PartitionSpec as P
from jax.experimental import pallas as pl
from jax.experimental.pallas import tpu as pltpu

D = 768
HEADS = 12
HEAD = 64
FF = 3072
WIN = 14
SIDE = 64
GRID = 5
WINDOWS = 25
RELS = 27
STRIDE = 16
TW = WIN * STRIDE
PAIRS = HEADS // 2
LANES = 128
EPSILON = 1e-06
F32 = jnp.float32
BF16 = jnp.bfloat16
VMEM_LIMIT = 60 * 1024 * 1024
NT = (((1,), (1,)), ((), ()))


def mm(a, b):
    return jnp.dot(a, b, preferred_element_type=F32)


def mm_nt(a, b):
    return lax.dot_general(a, b, NT, preferred_element_type=F32)


def iota(shape, dim):
    return lax.broadcasted_iota(jnp.int32, shape, dim)


def token_target(meta_ref, w):
    t = iota((TW, 1), 0)
    a, b = t >> 4, t & 15
    col = meta_ref[w, 1] + b
    row = meta_ref[w, 2] + a
    ok = (b < WIN) & (col >= 0) & (col < SIDE) & (row >= 0) & (row < SIDE) & (meta_ref[w, 3] > 0)
    return jnp.where(ok, ((a & 3) << 6) + col, -1)


def take_window(target, rows_ref):
    picks = jnp.where(iota((TW, 256), 1) == target, 1.0, 0.0).astype(BF16)
    parts = []
    for q in range(3):
        src = rows_ref[4 * q : 4 * q + 4].reshape(256, D)
        parts.append(mm(picks[64 * q : 64 * q + 64], src))
    src = rows_ref[12:14].reshape(128, D)
    parts.append(mm(picks[192:224, :128], src))
    return jnp.concatenate(parts, axis=0)


def norm(values):
    mean = jnp.sum(values, axis=-1, keepdims=True) * (1.0 / D)
    centred = values - mean
    inverse = lax.rsqrt(jnp.sum(centred * centred, axis=-1, keepdims=True) * (1.0 / D) + EPSILON)
    return centred * inverse, inverse


def norm_back(grad, unit, inverse, gain):
    s = grad * gain
    m1 = jnp.sum(s, axis=-1, keepdims=True) * (1.0 / D)
    m2 = jnp.sum(s * unit, axis=-1, keepdims=True) * (1.0 / D)
    return inverse * (s - m1 - unit * m2)


def fold8(x):
    return jnp.sum(x.reshape(x.shape[0] // 8, 8, x.shape[1]), axis=0)


def roll_rows(x, forward):
    out = []
    for a in range(WIN):
        piece = x[STRIDE * a : STRIDE * a + STRIDE]
        by = (a - 13) % LANES if forward else a
        out.append(pltpu.roll(piece, by, 1) if by else piece)
    return jnp.concatenate(out, axis=0)


def roll_cols(x, first):
    out = []
    for a in range(WIN):
        piece = x[STRIDE * a : STRIDE * a + STRIDE]
        out.append(pltpu.roll(piece, first, 1, stride=1, stride_axis=0))
    return jnp.concatenate(out, axis=0)


def attn_fwd_pair(q, k8, v, table, keys_a, keys_b, p_ref, p):
    lane = iota((TW, LANES), 1)
    low_half = lane < 64
    rc = mm(q, table)
    both = jnp.where((lane & 31) < 16, roll_rows(rc[:, :LANES], True), roll_cols(rc[:, LANES:], 3))
    high = both.astype(BF16)
    rest = (both - high.astype(F32)).astype(BF16)
    extra = jnp.where((lane & 63) < 32, high, rest)
    extra = jnp.where((lane & 63) == 14, jnp.ones_like(extra), extra)
    left = jnp.concatenate([q, extra], axis=1)
    zero = jnp.zeros_like(k8)
    wide_v = jnp.concatenate([v, jnp.ones_like(v)], axis=1)
    outs, invs = [], []
    for h in range(2):
        keys = jnp.concatenate(
            [jnp.where(low_half if h == 0 else ~low_half, k8, zero), (keys_a, keys_b)[h]], axis=1
        )
        s = mm_nt(left, keys)
        e = jnp.exp(s - jnp.max(s, axis=-1, keepdims=True)).astype(BF16)
        p_ref[2 * p + h] = e
        o = mm(e, wide_v)
        inv = 1.0 / o[:, LANES:]
        outs.append(o[:, :LANES] * inv)
        invs.append(inv)
    att = jnp.where(low_half, outs[0], outs[1]).astype(BF16)
    inv = jnp.where(low_half, invs[0], invs[1])
    return att, inv


def fwd_kernel(
    meta_ref, rows_ref, grows_ref, vec_ref, wqkv_ref, table_ref, ka_ref, kb_ref,
    x_ref, g_ref, n_ref, qkv_ref, p_ref, inv_ref, att_ref, *weights,
):
    w = pl.program_id(0)
    if weights:
        blocks_ref, (wqkv_ref, wproj_ref) = wqkv_ref, weights

        @pl.when(w == 0)
        def _():
            share = D // blocks_ref.shape[0]
            for b in range(blocks_ref.shape[1]):
                rows = slice(SHARD_ROWS * b, SHARD_ROWS * b + SHARD_ROWS)
                parts = [blocks_ref[i, b, :SHARD_ROWS] for i in range(blocks_ref.shape[0])]
                wqkv_ref[rows] = jnp.concatenate([part[:, : 3 * share] for part in parts], axis=1)
                wproj_ref[rows] = jnp.concatenate([part[:, 3 * share :] for part in parts], axis=1)

    target = token_target(meta_ref, w)
    x = take_window(target, rows_ref)
    x_ref[...] = x.astype(BF16)
    g_ref[...] = take_window(target, grows_ref).astype(BF16)
    unit, _ = norm(x)
    normed = jnp.where(target >= 0, unit * vec_ref[0:1] + vec_ref[1:2], 0.0).astype(BF16)
    n_ref[...] = normed
    for c in range(9):
        cols = slice(256 * c, 256 * c + 256)
        y = mm(normed, wqkv_ref[:, cols])
        if c < 3:
            y = y + vec_ref[2:3, cols]
        elif c >= 6:
            y = y + vec_ref[3:4, 256 * (c - 6) : 256 * (c - 6) + 256]
        else:
            y = y.astype(BF16).astype(F32) * 0.125
        qkv_ref[:, cols] = y.astype(BF16)

    for p in range(PAIRS):
        a = slice(LANES * p, LANES * p + LANES)
        q = qkv_ref[:, LANES * p : LANES * p + LANES]
        k8 = qkv_ref[:, D + LANES * p : D + LANES * p + LANES]
        v = qkv_ref[:, 2 * D + LANES * p : 2 * D + LANES * p + LANES]
        att, inv = attn_fwd_pair(q, k8, v, table_ref[...], ka_ref[...], kb_ref[...], p_ref, p)
        att_ref[:, a] = att
        inv_ref[:, a] = inv


def rows_spec(rows):
    return pl.BlockSpec(
        (pl.Element(rows), pl.Element(SIDE), pl.Element(D)), lambda w, meta: (meta[w, 0], 0, 0)
    )


def whole(shape, buffers=1):
    zeros = (0,) * len(shape)
    return pl.BlockSpec(shape, lambda w, meta: zeros, pipeline_mode=pl.Buffered(buffers))


def per_window(*tail):
    zeros = (0,) * len(tail)
    return pl.BlockSpec((None,) + tail, lambda w, meta: (w,) + zeros)


def key_constants():
    t = np.arange(TW)
    kr, kc = t >> 4, t & 15
    real = kc < WIN
    base = np.zeros((TW, 64), np.float32)
    for off in (0, 32):
        base[t[real], off + kr[real]] = 1.0
        base[t[real], off + 16 + kc[real]] = 1.0
    back = np.zeros_like(base)
    back[t[real], 13 - kr[real]] = 1.0
    back[t[real], 16 + 13 - kc[real]] = 1.0
    base[~real, 14] = -1e30
    none = np.zeros_like(base)
    ka = np.concatenate([base, none], 1)
    kb = np.concatenate([none, base], 1)
    back = np.concatenate([back, back], 1)
    return jnp.asarray(ka, BF16), jnp.asarray(kb, BF16), jnp.asarray(back, BF16)


def rel_table(rel_rows, rel_cols, forward):
    def wide(rel):
        turned = jnp.pad(rel, ((0, 0), (0, 32 - RELS)))
        twice = jnp.concatenate([turned, turned], axis=1)
        none = jnp.zeros_like(twice)
        return jnp.concatenate(
            [jnp.concatenate([twice, none], 1), jnp.concatenate([none, twice], 1)], 0
        )

    turn = (lambda rel: rel[:, ::-1]) if forward else (lambda rel: rel)
    return jnp.concatenate([wide(turn(rel_rows)), wide(turn(rel_cols))], axis=1)


def attention_forward(meta, ext, gext, vectors, wqkv, table, ka, kb):
    cap = meta.shape[0]
    weights = [(D, 3 * D), (D, D)] if wqkv.ndim == 4 else []
    sds = jax.ShapeDtypeStruct
    return pl.pallas_call(
        fwd_kernel,
        grid_spec=pltpu.PrefetchScalarGridSpec(
            num_scalar_prefetch=1,
            grid=(cap,),
            in_specs=[
                rows_spec(WIN), rows_spec(WIN), whole((8, D)), whole(wqkv.shape),
                whole((LANES, 256)), whole((TW, LANES)), whole((TW, LANES)),
            ],
            out_specs=[
                per_window(TW, D), per_window(TW, D), per_window(TW, D), per_window(TW, 3 * D),
                per_window(HEADS, TW, TW), per_window(TW, D), per_window(TW, D),
            ] + [whole(shape) for shape in weights],
        ),
        out_shape=[
            sds((cap, TW, D), BF16), sds((cap, TW, D), BF16), sds((cap, TW, D), BF16), sds((cap, TW, 3 * D), BF16),
            sds((cap, HEADS, TW, TW), BF16), sds((cap, TW, D), F32), sds((cap, TW, D), BF16),
        ] + [sds(shape, BF16) for shape in weights],
        compiler_params=pltpu.CompilerParams(vmem_limit_bytes=VMEM_LIMIT),
        cost_estimate=pl.CostEstimate(flops=40_000_000_000, bytes_accessed=80_000_000, transcendentals=8_000_000),
    )(meta, ext, gext, vectors, wqkv, table, ka, kb)


def phi_parts(u):
    e = jnp.exp(u * u * -0.5)
    t = 1.0 / (1.0 + (0.3275911 * 0.7071067811865476) * jnp.abs(u))
    poly = t * (0.254829592 + t * (-0.284496736 + t * (1.421413741 + t * (-1.453152027 + t * 1.061405429))))
    tail = 0.5 * poly * e
    return jnp.where(u >= 0, 1.0 - tail, tail), e * 0.3989422804014327


def mlp_kernel(
    g_ref, x_ref, att_ref, wproj_ref, vec_ref, ff_ref, b1_ref,
    out_ref, n2_ref, act_ref, dpre_ref, dmix_ref, datt_ref, sums_ref, sum1_ref,
    acc_ref, dn_ref,
):
    @pl.when(pl.program_id(0) == 0)
    def _():
        sums_ref[...] = jnp.zeros_like(sums_ref)
        sum1_ref[...] = jnp.zeros_like(sum1_ref)

    gb = g_ref[...]
    g = gb.astype(F32)
    sums_ref[0] += fold8(g)
    hidden = x_ref[...].astype(F32) + mm(att_ref[...], wproj_ref[...]) + vec_ref[4:5]
    unit, inverse = norm(hidden)
    n2 = (unit * vec_ref[5:6] + vec_ref[6:7]).astype(BF16)
    n2_ref[...] = n2
    acc_ref[...] = hidden + vec_ref[7:8]
    parts, inner = ff_ref.shape[0], ff_ref.shape[2] // 2
    join = max(1, 1536 // inner)
    chunk = inner * join
    for c in range(parts // join):
        cols = slice(chunk * c, chunk * c + chunk)
        blocks = range(join * c, join * c + join)
        w1 = jnp.concatenate([ff_ref[i, :, :inner] for i in blocks], axis=1)
        w2t = jnp.concatenate([ff_ref[i, :, inner:] for i in blocks], axis=1)
        u = mm(n2, w1) + b1_ref[:, cols]
        dact = mm(gb, w2t)
        cdf, pdf = phi_parts(u)
        act = (u * cdf).astype(BF16)
        act_ref[:, cols] = act
        acc_ref[...] += mm_nt(act, w2t)
        dpre32 = dact * (cdf + u * pdf)
        dpre = dpre32.astype(BF16)
        dpre_ref[:, cols] = dpre
        sum1_ref[:, cols] += fold8(dpre32)
        step = mm_nt(dpre, w1)
        if c == 0:
            dn_ref[...] = step
        else:
            dn_ref[...] += step
    out_ref[...] = acc_ref[...].astype(BF16)
    dn = dn_ref[...]
    sums_ref[1] += fold8(dn * unit)
    sums_ref[2] += fold8(dn)
    dh = g + norm_back(dn, unit, inverse, vec_ref[5:6])
    dmix = dh.astype(BF16)
    dmix_ref[...] = dmix
    sums_ref[3] += fold8(dh)
    datt_ref[...] = mm_nt(dmix, wproj_ref[...]).astype(BF16)


def tile_rows(rows):
    return next(t for t in (416, 448, 224) if rows % t == 0)


def feed_forward(g, x, att, wproj, vectors, ff, b1, spare):
    cap = g.shape[0]
    rows = cap * TW
    tile = tile_rows(rows)
    sds = jax.ShapeDtypeStruct

    def tiled(width):
        return pl.BlockSpec((tile, width), lambda i: (i, 0))

    def kept(shape):
        zeros = (0,) * len(shape)
        return pl.BlockSpec(shape, lambda i: zeros, pipeline_mode=pl.Buffered(1))

    out, *rest = pl.pallas_call(
        mlp_kernel,
        grid=(rows // tile,),
        in_specs=[
            tiled(D), tiled(D), tiled(D), kept((D, D)), kept((8, D)), kept(ff.shape), kept((1, FF)),
        ],
        out_specs=[tiled(D), tiled(D), tiled(FF), tiled(FF), tiled(D), tiled(D), kept((4, 8, D)), kept((8, FF))],
        scratch_shapes=[pltpu.VMEM((tile, D), F32), pltpu.VMEM((tile, D), F32)],
        out_shape=[
            sds((rows + spare * TW, D), BF16), sds((rows, D), BF16), sds((rows, FF), BF16), sds((rows, FF), BF16),
            sds((rows, D), BF16), sds((rows, D), BF16), sds((4, 8, D), F32), sds((8, FF), F32),
        ],
        compiler_params=pltpu.CompilerParams(vmem_limit_bytes=VMEM_LIMIT),
        cost_estimate=pl.CostEstimate(flops=60_000_000_000, bytes_accessed=80_000_000, transcendentals=8_000_000),
    )(g.reshape(rows, D), x.reshape(rows, D), att.reshape(rows, D), wproj, vectors, ff, b1)
    return out.reshape(cap + spare, TW, D), rest[0], rest[1], rest[2], *[a.reshape(cap, TW, D) for a in rest[3:5]], *rest[5:]


MESH = pl.DeviceIdType.MESH
SHARD_ROWS = 192
SHARD_COLS = 384


def place():
    img, band = lax.axis_index("img"), lax.axis_index("band")
    return {"zh": img // 4, "zl": img // 2 % 2, "y": img % 2, "x": band // 2, "c": band % 2}


def partner(dim):
    img, band = lax.axis_index("img"), lax.axis_index("band")
    at = place()[dim]
    step = {"zh": 4, "zl": 2, "y": 1, "x": 2, "c": 1}[dim]
    move = step - 2 * step * at
    return (img, band + move) if dim in ("x", "c") else (img + move, band)


def peers():
    img, band = lax.axis_index("img"), lax.axis_index("band")
    return [(img, (band + d) % 4) for d in range(1, 4)], [((img + d) % 8, band) for d in range(1, 8)]


def greet():
    barrier = pltpu.get_barrier_semaphore()
    near_by, far = peers()
    for device in near_by + far:
        pl.semaphore_signal(barrier, inc=1, device_id=device, device_id_type=MESH)
    pl.semaphore_wait(barrier, 10)


class Halving:
    AXES = ("x", "zh", "zl", "y")

    def __init__(self, source, own, got, sems, order, rows):
        self.source, self.own, self.got, self.sems, self.order, self.rows = source, own, got, sems, order, rows
        self.at = place()

    @staticmethod
    def scratch(rows):
        shapes = [(2, 2, 2, 2), (2, 2, 2, 2), (2, 2, 2), (2, 2), (2,), (1,)]
        return [pltpu.VMEM(s + (rows, SHARD_COLS), BF16) for s in shapes] + [pltpu.SemaphoreType.DMA((11,))]

    def first(self):
        c = self.at["c"]
        send, recv, local = self.sems.at[0], self.sems.at[1], self.sems.at[10]
        for x in range(2):
            for img in range(8):
                spot = (x, img // 4, img // 2 % 2, img % 2)
                pltpu.make_async_remote_copy(
                    src_ref=self.source(x, img, 1 - c), dst_ref=self.got[0].at[spot], send_sem=send, recv_sem=recv,
                    device_id=partner("c"), device_id_type=MESH,
                ).start()
                pltpu.make_async_copy(self.source(x, img, c), self.own.at[spot], local).start()

    def first_done(self):
        send, recv, local = self.sems.at[0], self.sems.at[1], self.sems.at[10]
        whole = pltpu.make_async_remote_copy(
            src_ref=self.got[0], dst_ref=self.got[0], send_sem=send, recv_sem=recv,
            device_id=partner("c"), device_id_type=MESH,
        )
        whole.wait_send()
        whole.wait_recv()
        pltpu.make_async_copy(self.got[0], self.own, local).wait()

        def add(i, _):
            spot = (i // 8, i // 4 % 2, i // 2 % 2, i % 2)
            self.own[spot] = self.own[spot] + self.got[0][spot]
            return 0

        lax.fori_loop(0, 16, add, 0)

    def index(self, k, dim=None):
        spot = []
        for axis in self.AXES:
            if axis == dim:
                spot.append(1 - self.at[axis])
            elif axis in self.order[:k]:
                spot.append(self.at[axis])
            else:
                spot.append(slice(None))
        return tuple(spot)

    def copy(self, k):
        dim = self.order[k]
        src = self.own.at[self.index(k, dim)]
        dst = self.got[k + 1].at[0] if k == 3 else self.got[k + 1]
        return pltpu.make_async_remote_copy(
            src_ref=src, dst_ref=dst, send_sem=self.sems.at[2 + 2 * k], recv_sem=self.sems.at[3 + 2 * k],
            device_id=partner(dim), device_id_type=MESH,
        )

    def step(self, k):
        self.copy(k).start()

    def step_done(self, k):
        self.copy(k).wait()
        done = self.order[: k + 1]
        free = [axis for axis in self.AXES if axis not in done]
        count = 2 ** len(free)

        def add(i, _):
            bits = {axis: (i // 2 ** (len(free) - 1 - j)) % 2 for j, axis in enumerate(free)}
            spot = tuple(bits[axis] if axis in bits else self.at[axis] for axis in self.AXES)
            self.own[spot] = self.own[spot] + self.got[k + 1][tuple(bits[axis] for axis in free)]
            return 0

        if k < 3:
            lax.fori_loop(0, count, add, 0)

    def result(self):
        spot = tuple(self.at[axis] for axis in self.AXES)
        return self.own[spot].astype(F32) + self.got[4][0].astype(F32)


ORDERS = (("x", "y", "zh", "zl"), ("y", "x", "zh", "zl"))


def wide_source(ref, part):
    half = SHARD_ROWS // 2

    def source(x, img, c):
        row = pl.multiple_of((2 * x + c) * SHARD_ROWS + part * half, half)
        return ref.at[pl.ds(row, half), pl.ds(img * SHARD_COLS, SHARD_COLS)]

    return source


def each(group, name, *args):
    def body():
        for stream in group:
            getattr(stream, name)(*args)

    return body


def timeline(w, moments):
    for when, bodies in moments.items():
        @pl.when(w == when)
        def _(bodies=bodies):
            for body in bodies:
                body()


NEAR_CORE = 7
NEAR_CROSS = 5
CROSS_ROWS = 160


class Homeward:
    def __init__(self, windows, everything, sems):
        self.windows, self.all, self.sems = windows, everything, sems
        self.cap = everything.shape[0] - NEAR_CORE - NEAR_CROSS
        self.band = lax.axis_index("band")

    def inner(self):
        return (self.band == 1) | (self.band == 2)

    def outer(self):
        return (self.band == 0) | (self.band == 3)

    def keep(self):
        return pltpu.make_async_copy(self.windows, self.all.at[pl.ds(0, self.cap)], self.sems.at[4])

    def to_core(self, first, count):
        return pltpu.make_async_remote_copy(
            src_ref=self.windows.at[pl.ds(first, count)], dst_ref=self.all.at[pl.ds(self.cap, count)],
            send_sem=self.sems.at[0], recv_sem=self.sems.at[1], device_id=partner("c"), device_id_type=MESH,
        )

    def to_cross(self, sending):
        img = lax.axis_index("img")
        skip = (2 - self.band) if sending else (self.band - 1)
        rows = pl.ds(pl.multiple_of(skip * (TW - CROSS_ROWS), TW - CROSS_ROWS), CROSS_ROWS)
        return pltpu.make_async_remote_copy(
            src_ref=self.windows.at[pl.ds(0, NEAR_CROSS), rows],
            dst_ref=self.all.at[pl.ds(self.cap + NEAR_CORE, NEAR_CROSS), rows],
            send_sem=self.sems.at[2], recv_sem=self.sems.at[3], device_id=(img, 3 - self.band), device_id_type=MESH,
        )

    def send_cross(self):
        pl.when(self.inner())(lambda: self.to_cross(True).start())

    def send_core_inner(self):
        pl.when(self.inner())(lambda: self.to_core(NEAR_CROSS, NEAR_CORE).start())

    def send_core_outer(self):
        pl.when(self.outer())(lambda: self.to_core(0, 3).start())

    def finish(self):
        @pl.when(self.inner())
        def _():
            self.to_core(NEAR_CROSS, NEAR_CORE).wait_send()
            self.to_core(0, 3).wait_recv()
            self.to_cross(True).wait_send()
            self.to_cross(False).wait_recv()

        @pl.when(self.outer())
        def _():
            self.to_core(0, 3).wait_send()
            self.to_core(NEAR_CROSS, NEAR_CORE).wait_recv()


class Gather:
    def __init__(self, block, out, sems):
        self.block, self.out, self.sems = block, out, sems
        img, self.band = lax.axis_index("img"), lax.axis_index("band")
        self.z, self.y = img // 2, img % 2
        self.x, self.c = self.band // 2, self.band % 2

    def where(self, dz, fx, fy):
        img = (self.z + 4 - dz) % 4 * 2 + (1 - self.y if fy else self.y)
        return img, (1 - self.x if fx else self.x) * 2 + self.c

    def move(self, k, dz, fx, fy, device):
        img, band = self.where(dz, fx, fy)
        own = (dz, fx, fy) == (0, 0, 0)
        return pltpu.make_async_remote_copy(
            src_ref=self.block if own else self.out.at[img, band], dst_ref=self.out.at[img, band],
            send_sem=self.sems.at[0, k], recv_sem=self.sems.at[1, k], device_id=device, device_id_type=MESH,
        )

    def along_z(self, d):
        return self.move(d - 1, 0, 0, 0, ((self.z + d) % 4 * 2 + self.y, self.band))

    def along_x(self, dz):
        return self.move(3 + dz, dz, 0, 0, partner("x"))

    def along_y(self, fx, dz):
        return self.move(7 + 4 * fx + dz, dz, fx, 0, partner("y"))

    def to_core(self, fy, fx, dz):
        return self.move(15 + 8 * fy + 4 * fx + dz, dz, fx, fy, partner("c"))

    def keep(self):
        img, band = self.where(0, 0, 0)
        return pltpu.make_async_copy(self.block, self.out.at[img, band], self.sems.at[0, 31])

    def pass_on(self, dz):
        self.along_x(dz).start()
        self.along_y(0, dz).start()
        self.to_core(0, 0, dz).start()

    def begin(self):
        self.keep().start()
        for d in range(1, 4):
            self.along_z(d).start()
        self.pass_on(0)

    def run(self, then):
        for dz in range(1, 4):
            self.along_z(dz).wait_recv()
            self.pass_on(dz)
        then()
        for dz in range(4):
            self.along_x(dz).wait_recv()
            self.along_y(1, dz).start()
            self.to_core(0, 1, dz).start()
        for fx in range(2):
            for dz in range(4):
                self.along_y(fx, dz).wait_recv()
                self.to_core(1, fx, dz).start()
        for d in range(1, 4):
            self.along_z(d).wait_send()
        for dz in range(4):
            self.along_x(dz).wait_send()
            for fx in range(2):
                self.along_y(fx, dz).wait_send()
                for fy in range(2):
                    self.to_core(fy, fx, dz).wait()
        self.keep().wait()


CROSS_HALO = 10


class Edges:
    def __init__(self, rows, ext, zero, sems):
        self.rows, self.ext, self.zero, self.sems = rows, ext, zero, sems
        self.band = lax.axis_index("band")
        self.own_rows = rows.shape[1]

    def inner(self):
        return (self.band == 1) | (self.band == 2)

    def keep(self):
        return pltpu.make_async_copy(self.rows, self.ext.at[:, pl.ds(HALO, self.own_rows)], self.sems.at[0])

    def empty(self):
        at = self.band // 3 * (HALO + self.own_rows)
        return [
            pltpu.make_async_copy(self.zero, self.ext.at[m, pl.ds(at, HALO)], self.sems.at[1 + m]) for m in range(2)
        ]

    def core(self, sending):
        odd = self.band % 2
        far = self.own_rows - HALO
        there = (odd if sending else 1 - odd) * (HALO + self.own_rows)
        return pltpu.make_async_remote_copy(
            src_ref=self.rows.at[:, pl.ds((1 - odd) * far, HALO)], dst_ref=self.ext.at[:, pl.ds(there, HALO)],
            send_sem=self.sems.at[3], recv_sem=self.sems.at[4], device_id=partner("c"), device_id_type=MESH,
        )

    def cross(self, sending):
        img = lax.axis_index("img")
        m = 2 - self.band
        far = self.own_rows - CROSS_HALO
        to = m if sending else 1 - m
        there = to * (HALO - CROSS_HALO) + (1 - to) * (HALO + self.own_rows)
        return pltpu.make_async_remote_copy(
            src_ref=self.rows.at[m, pl.ds(m * far, CROSS_HALO)], dst_ref=self.ext.at[to, pl.ds(there, CROSS_HALO)],
            send_sem=self.sems.at[5], recv_sem=self.sems.at[6], device_id=(img, 3 - self.band), device_id_type=MESH,
        )

    def start_cross(self):
        pl.when(self.inner())(lambda: self.cross(True).start())

    def start(self):
        self.core(True).start()
        self.keep().start()

        @pl.when(jnp.logical_not(self.inner()))
        def _():
            for copy in self.empty():
                copy.start()

    def finish(self):
        self.core(True).wait_send()
        self.core(False).wait_recv()
        self.keep().wait()

        @pl.when(self.inner())
        def _():
            self.cross(True).wait_send()
            self.cross(False).wait_recv()

        @pl.when(jnp.logical_not(self.inner()))
        def _():
            for copy in self.empty():
                copy.wait()


def pack_kernel(wqkv_ref, wproj_ref, small_ref, relr_ref, relc_ref, w1_ref, w2t_ref, block_ref, ff_ref):
    rows, wide = wqkv_ref.shape
    block_ref[:rows, :wide] = wqkv_ref[...]
    block_ref[:rows, wide:] = wproj_ref[...]
    parts = [ref[...] for ref in (small_ref, relr_ref, relc_ref)]
    rest = block_ref.shape[1] - sum(part.shape[1] for part in parts)
    block_ref[rows:] = jnp.concatenate(parts + [jnp.zeros((small_ref.shape[0], rest), BF16)], axis=1)
    inner = w1_ref.shape[1]
    ff_ref[:, :inner] = w1_ref[...]
    ff_ref[:, inner:] = w2t_ref[...]


def pack(wqkv, wproj, small, relr, relc, w1, w2t):
    rows = wqkv.shape[0]
    return pl.pallas_call(
        pack_kernel,
        out_shape=[
            jax.ShapeDtypeStruct((rows + small.shape[0], wqkv.shape[1] + wproj.shape[1]), BF16),
            jax.ShapeDtypeStruct((rows, 2 * w1.shape[1]), BF16),
        ],
        cost_estimate=pl.CostEstimate(flops=0, bytes_accessed=1_000_000, transcendentals=0),
    )(wqkv, wproj, small, relr, relc, w1, w2t)


def entry_kernel(
    block_ref, x_ref, g_ref, all_ref, xext_ref, gext_ref, zero_ref, xin_ref, gin_ref, lsems, gsems, xsems, esems,
):
    loads = [pltpu.make_async_copy(x_ref, xin_ref, lsems.at[0]), pltpu.make_async_copy(g_ref, gin_ref, lsems.at[1])]
    for load in loads:
        load.start()
    zero_ref[...] = jnp.zeros_like(zero_ref)
    edges = [Edges(xin_ref, xext_ref, zero_ref, xsems), Edges(gin_ref, gext_ref, zero_ref, esems)]
    greet()
    gather = Gather(block_ref, all_ref, gsems)
    gather.begin()

    def next_edges(n):
        loads[n].wait()
        edges[n].start_cross()
        edges[n].start()

    next_edges(0)
    gather.run(lambda: next_edges(1))
    for item in edges:
        item.finish()


def entry(block, x, g):
    sds = jax.ShapeDtypeStruct
    ext = sds((2, x.shape[1] + 2 * HALO, SIDE, D), BF16)
    inside, anywhere = pl.BlockSpec(memory_space=pltpu.VMEM), pl.BlockSpec(memory_space=pl.ANY)
    return pl.pallas_call(
        entry_kernel,
        in_specs=[inside, anywhere, anywhere],
        out_specs=[anywhere] * 3,
        out_shape=[sds((8, 4) + block.shape, BF16), ext, ext],
        scratch_shapes=[
            pltpu.VMEM((HALO, SIDE, D), BF16), pltpu.VMEM(x.shape, BF16), pltpu.VMEM(x.shape, BF16),
            pltpu.SemaphoreType.DMA((2,)), pltpu.SemaphoreType.DMA((2, 32)), pltpu.SemaphoreType.DMA((7,)),
            pltpu.SemaphoreType.DMA((7,)),
        ],
        compiler_params=pltpu.CompilerParams(vmem_limit_bytes=VMEM_LIMIT, collective_id=3, has_side_effects=True),
    )(block, x, g)


def attn_bwd_kernel(
    meta_ref, qkv_ref, p_ref, inv_ref, att_ref, datt_ref, table_ref, kback_ref, *rest,
):
    w = pl.program_id(0)
    if len(rest) == 3:
        dqkv_ref, rel_ref, bias_ref = rest
        streams = None
    else:
        fc1_ref, fc2_ref, dqkv_ref, rel_ref, bias_ref, part_ref, sum2_ref = rest[:7]
        half = SHARD_ROWS // 2
        streams = []
        for n in range(4):
            own, *got, sems = rest[7 + 7 * n : 14 + 7 * n]
            source = wide_source(fc2_ref if n < 2 else fc1_ref, n % 2)
            streams.append(Halving(source, own, got, sems, ORDERS[n % 2], half))
        ones, twos = streams[:2], streams[2:]
        timeline(
            w,
            {
                0: [greet, each(streams, "first")],
                2: [each(ones, "first_done"), each(ones, "step", 0), each(twos, "first_done")],
                5: [each(ones, "step_done", 0), each(ones, "step", 1), each(twos, "step", 0)],
                7: [each(ones, "step_done", 1), each(ones, "step", 2)],
                10: [each(twos, "step_done", 0), each(twos, "step", 1), each(ones, "step_done", 2), each(ones, "step", 3)],
            },
        )

    @pl.when(w == 0)
    def _():
        rel_ref[...] = jnp.zeros_like(rel_ref)
        bias_ref[...] = jnp.zeros_like(bias_ref)

    lane = iota((TW, LANES), 1)
    low_half = lane < 64
    onehot = kback_ref[...]
    for p in range(PAIRS):
        q = qkv_ref[:, LANES * p : LANES * p + LANES]
        k8 = qkv_ref[:, D + LANES * p : D + LANES * p + LANES]
        v = qkv_ref[:, 2 * D + LANES * p : 2 * D + LANES * p + LANES]
        cols = slice(LANES * p, LANES * p + LANES)
        da = datt_ref[:, cols].astype(F32) * inv_ref[:, cols]
        da_low = da.astype(BF16)
        prod = da_low.astype(F32) * att_ref[:, cols].astype(F32)
        keys = jnp.concatenate([k8, onehot], axis=1)
        da_t = da.T.astype(BF16)
        q_t = q.astype(F32).T.astype(BF16)
        zero = jnp.zeros_like(v)
        dqx, dv_t, dk_t = [], [], []
        dps, dss = [], []
        for h in range(2):
            mine = low_half if h == 0 else ~low_half
            dps.append(mm_nt(da_low, jnp.where(mine, v, zero)))
        for h in range(2):
            mine = low_half if h == 0 else ~low_half
            centre = jnp.sum(jnp.where(mine, prod, 0.0), axis=-1, keepdims=True)
            e = p_ref[2 * p + h]
            dss.append((e.astype(F32) * (dps[h] - centre)).astype(BF16))
        for h in range(2):
            dqx.append(mm(dss[h], keys))
            dv_t.append(mm(da_t[64 * h : 64 * h + 64], p_ref[2 * p + h]))
            dk_t.append(mm(q_t[64 * h : 64 * h + 64], dss[h]))
        dq = jnp.where(low_half, dqx[0][:, :LANES], dqx[1][:, :LANES])
        drc = jnp.where(low_half, dqx[0][:, LANES:], dqx[1][:, LANES:])
        part = lane & 63
        rows = roll_rows(jnp.where(part < 16, drc, 0.0), False)
        cols_part = roll_cols(jnp.where((part >= 16) & (part < 32), drc, 0.0), LANES - 16)
        skew = jnp.concatenate([rows, cols_part], axis=1).astype(BF16)
        dq = dq + mm_nt(skew, table_ref[...])
        rel_ref[...] += mm(q_t, skew)
        dv = jnp.concatenate(dv_t, axis=0).T
        dk = (jnp.concatenate(dk_t, axis=0) * 0.125).T
        dqkv_ref[:, cols] = dq.astype(BF16)
        dqkv_ref[:, D + LANES * p : D + LANES * p + LANES] = dk.astype(BF16)
        dqkv_ref[:, 2 * D + LANES * p : 2 * D + LANES * p + LANES] = dv.astype(BF16)
        bias_ref[0, :, cols] += fold8(dq)
        bias_ref[1, :, cols] += fold8(dv)

    if streams:
        @pl.when(w == pl.num_programs(0) - 1)
        def _():
            each(ones, "step_done", 3)()
            sum2_ref[:half] = ones[0].result()
            sum2_ref[half:] = ones[1].result()
            each(twos, "step_done", 1)()
            for n, stream in enumerate(twos):
                part_ref[n] = stream.own[stream.at["x"], :, :, stream.at["y"]]


def attention_backward(meta, qkv, p, inv, att, datt, table, kback, beside=()):
    cap = meta.shape[0]
    sds = jax.ShapeDtypeStruct
    anywhere = pl.BlockSpec(memory_space=pl.ANY)
    shard = (SHARD_ROWS, SHARD_COLS)
    more_specs, more_outs, scratch, extra = [], [], [], {}
    if beside:
        part = (2, 2, 2, SHARD_ROWS // 2, SHARD_COLS)
        more_specs = [whole(part), whole(shard)]
        more_outs = [sds(part, BF16), sds(shard, F32)]
        scratch = Halving.scratch(SHARD_ROWS // 2) * 4
        extra = dict(collective_id=1, has_side_effects=True)
    return pl.pallas_call(
        attn_bwd_kernel,
        grid_spec=pltpu.PrefetchScalarGridSpec(
            num_scalar_prefetch=1,
            grid=(cap,),
            in_specs=[
                per_window(TW, 3 * D), per_window(HEADS, TW, TW), per_window(TW, D), per_window(TW, D),
                per_window(TW, D), whole((LANES, 256)), whole((TW, LANES)),
            ] + [anywhere] * len(beside),
            out_specs=[per_window(TW, 3 * D), whole((LANES, 256)), whole((2, 8, D))] + more_specs,
            scratch_shapes=scratch,
        ),
        out_shape=[sds((cap, TW, 3 * D), BF16), sds((LANES, 256), F32), sds((2, 8, D), F32)] + more_outs,
        compiler_params=pltpu.CompilerParams(vmem_limit_bytes=VMEM_LIMIT, **extra),
        cost_estimate=pl.CostEstimate(flops=60_000_000_000, bytes_accessed=80_000_000, transcendentals=0),
    )(meta, qkv, p, inv, att, datt, table, kback, *beside)


def rel_from(acc):
    def one(block):
        own = block[:64, :32] + block[64:, 64:96]
        return own[:, :RELS].T

    return one(acc[:, :LANES]), one(acc[:, LANES:])


def put_window(target, y, acc_ref, row0):
    picks = jnp.where(iota((TW, 256), 1) == target, 1.0, 0.0).astype(BF16)
    for q in range(4):
        n = 4 if q < 3 else 2
        t = slice(64 * q, 64 * q + STRIDE * n)
        part = lax.dot_general(
            picks[t, : 64 * n], y[t], (((0,), (0,)), ((), ())), preferred_element_type=F32
        )
        acc_ref[pl.ds(row0 + 4 * q, n)] += part.reshape(n, SIDE, D).astype(acc_ref.dtype)


def scatter_kernel(meta_ref, y_ref, ext_ref, acc_ref):
    w = pl.program_id(0)

    @pl.when(w == 0)
    def _():
        acc_ref[...] = jnp.zeros_like(acc_ref)

    put_window(token_target(meta_ref, w), y_ref[...], acc_ref, meta_ref[w, 0])

    @pl.when(w == pl.num_programs(0) - 1)
    def _():
        def copy(i, _):
            ext_ref[i] = acc_ref[i].astype(BF16)
            return 0
        lax.fori_loop(0, ext_ref.shape[0], copy, 0)


def scatter(meta, y, ext_rows):
    cap = meta.shape[0]
    return pl.pallas_call(
        scatter_kernel,
        grid_spec=pltpu.PrefetchScalarGridSpec(
            num_scalar_prefetch=1,
            grid=(cap,),
            in_specs=[per_window(TW, D)],
            out_specs=whole((ext_rows, SIDE, D)),
            scratch_shapes=[pltpu.VMEM((ext_rows, SIDE, D), F32)],
        ),
        out_shape=jax.ShapeDtypeStruct((ext_rows, SIDE, D), BF16),
        compiler_params=pltpu.CompilerParams(vmem_limit_bytes=VMEM_LIMIT),
        cost_estimate=pl.CostEstimate(flops=5_000_000_000, bytes_accessed=20_000_000, transcendentals=0),
    )(meta, y)


def last_kernel(
    meta_ref, dqkv_ref, wqkv_ref, x_ref, dmix_ref, gain_ref, ext_ref, sums_ref, acc_ref,
):
    w = pl.program_id(0)

    @pl.when(w == 0)
    def _():
        acc_ref[...] = jnp.zeros_like(acc_ref)
        sums_ref[...] = jnp.zeros_like(sums_ref)

    target = token_target(meta_ref, w)
    dn = jnp.zeros((TW, D), F32)
    for c in range(3):
        cols = slice(D * c, D * c + D)
        dn = dn + mm_nt(dqkv_ref[:, cols], wqkv_ref[:, cols])
    dn = jnp.where(target >= 0, dn, 0.0)
    unit, inverse = norm(x_ref[...].astype(F32))
    sums_ref[0] += fold8(dn * unit)
    sums_ref[1] += fold8(dn)
    grad = dmix_ref[...].astype(F32) + norm_back(dn, unit, inverse, gain_ref[0:1])
    put_window(target, grad.astype(BF16), acc_ref, meta_ref[w, 0])

    @pl.when(w == pl.num_programs(0) - 1)
    def _():
        def copy(i, _):
            ext_ref[i] = acc_ref[i].astype(BF16)
            return 0
        lax.fori_loop(0, ext_ref.shape[0], copy, 0)


def last_norm(meta, dqkv, wqkv, x, dmix, gain, ext_rows):
    cap = meta.shape[0]
    sds = jax.ShapeDtypeStruct
    return pl.pallas_call(
        last_kernel,
        grid_spec=pltpu.PrefetchScalarGridSpec(
            num_scalar_prefetch=1,
            grid=(cap,),
            in_specs=[
                per_window(TW, 3 * D), whole((D, 3 * D)), per_window(TW, D), per_window(TW, D), whole((8, D)),
            ],
            out_specs=[whole((ext_rows, SIDE, D)), whole((2, 8, D))],
            scratch_shapes=[pltpu.VMEM((ext_rows, SIDE, D), F32)],
        ),
        out_shape=[sds((ext_rows, SIDE, D), BF16), sds((2, 8, D), F32)],
        compiler_params=pltpu.CompilerParams(vmem_limit_bytes=VMEM_LIMIT),
        cost_estimate=pl.CostEstimate(flops=15_000_000_000, bytes_accessed=30_000_000, transcendentals=0),
    )(meta, dqkv, wqkv, x, dmix, gain)


class SmallSum:
    def __init__(self, mine, got_band, got_img, sems, part):
        self.mine, self.got, self.sems, self.part = mine, (got_band, got_img), sems, part

    @staticmethod
    def scratch(shape, part):
        return [
            pltpu.VMEM(shape, F32), pltpu.VMEM((3,) + shape, F32), pltpu.VMEM((7,) + part, F32),
            pltpu.SemaphoreType.DMA((2, 2, 7)),
        ]

    def copies(self, k):
        return [
            pltpu.make_async_remote_copy(
                src_ref=self.part(device[0]) if k else self.mine, dst_ref=self.got[k].at[d],
                send_sem=self.sems.at[k, 0, d], recv_sem=self.sems.at[k, 1, d], device_id=device, device_id_type=MESH,
            )
            for d, device in enumerate(peers()[k])
        ]

    def send(self, k):
        for copy in self.copies(k):
            copy.start()

    def add(self):
        for copy in self.copies(0):
            copy.wait()
        self.mine[...] = self.mine[...] + self.got[0][0] + self.got[0][1] + self.got[0][2]

    def result(self):
        for copy in self.copies(1):
            copy.wait()
        total = self.part(lax.axis_index("img"))[...]
        for d in range(7):
            total = total + self.got[1][d]
        return total


def deal(rows_ref, parts_ref, rows, wide):
    groups = parts_ref.shape[0]
    share = D // groups
    for i in range(groups):
        parts_ref[i, :rows, :share] = rows_ref[:rows, share * i : share * i + share]
        for k in range(wide):
            at = share * (wide * i + k)
            parts_ref[i, rows + k : rows + k + 1, :share] = rows_ref[rows + at // D : rows + at // D + 1, at % D : at % D + share]


HOME_ROWS = 8


def home_kernel(
    table_ref, own_ref, core_ref, cross_ref, grad_ref, total_ref, ln_ref, rel_ref, q_ref,
    output_ref, input_grad_ref, vec_refs, b1_ref, relr_ref, relc_ref, wq_ref, wp_ref,
    out_ref, sems,
):
    step = pl.program_id(0)
    per_image = pl.num_programs(0) // 2
    m = step // per_image
    top, left = table_ref[m, 25], table_ref[m, 26]
    first = table_ref[m, 27] + (step - m * per_image) * HOME_ROWS

    @pl.when(step == 0)
    def _():
        cap = own_ref.shape[0]
        loads = [
            pltpu.make_async_copy(ref, out_ref.at[pl.ds(at, ref.shape[0])], sems.at[n])
            for n, (ref, at) in enumerate(((own_ref, 0), (core_ref, cap), (cross_ref, cap + NEAR_CORE)))
        ]
        for load in loads:
            load.start()
        share = vec_refs[0].shape[1]
        ln, total = ln_ref[:, :share], total_ref[:, :share]
        for ref, row in zip(vec_refs, (ln[0:1], ln[1:2], total[0:1], total[1:2], total[5:6], total[3:4], total[4:5], total[2:3])):
            ref[...] = row
        b1_ref[...] = jnp.concatenate([total[6 + k : 7 + k] for k in range(4)], axis=1)
        relr_ref[...] = rel_ref[:, :RELS]
        relc_ref[...] = rel_ref[:, LANES : LANES + RELS]
        wq_ref[...] = q_ref[:, : 3 * share]
        wp_ref[...] = q_ref[:, 3 * share :]
        for load in loads:
            load.wait()

    col = iota((SIDE, GRID * STRIDE), 0) + left
    spot = iota((SIDE, GRID * STRIDE), 1)
    picks = jnp.where((spot >> 4) * WIN + (spot & 15) == col, 1.0, 0.0)
    picks = jnp.where((spot & 15) < WIN, picks, 0.0).astype(BF16)
    for i in range(HOME_ROWS):
        at = i + first + top
        r = at // WIN
        a = pl.multiple_of((at - r * WIN) * STRIDE, STRIDE)
        slots = [table_ref[m, r * GRID + c] for c in range(GRID)]
        for source, target in ((out_ref, output_ref), (grad_ref, input_grad_ref)):
            tokens = jnp.concatenate([source[slot, pl.ds(a, STRIDE)] for slot in slots], axis=0)
            target[0, i] = mm(picks, tokens).astype(target.dtype)


def home(table, sources, rows):
    per_image = rows // HOME_ROWS
    sds = jax.ShapeDtypeStruct
    tiled = pl.BlockSpec((1, HOME_ROWS, SIDE, D), lambda w, meta: (w // per_image, w % per_image, 0, 0))
    shapes = [[(1, D // 8)] * 8, (1, FF // 8)] + [(HEAD // 4, RELS)] * 2 + [
        (SHARD_ROWS, 3 * D // 8), (SHARD_ROWS, D // 8),
    ]
    is_shape = lambda shape: isinstance(shape, tuple)
    return pl.pallas_call(
        home_kernel,
        grid_spec=pltpu.PrefetchScalarGridSpec(
            num_scalar_prefetch=1,
            grid=(2 * per_image,),
            in_specs=[pl.BlockSpec(memory_space=pl.ANY)] * 3 + [whole(a.shape) for a in sources[3:]],
            scratch_shapes=[pltpu.VMEM(sources[3].shape, BF16), pltpu.SemaphoreType.DMA((3,))],
            out_specs=[tiled, tiled] + jax.tree.map(whole, shapes, is_leaf=is_shape),
        ),
        out_shape=[sds((2, rows, SIDE, D), BF16), sds((2, rows, SIDE, D), F32)]
        + jax.tree.map(lambda shape: sds(shape, F32), shapes, is_leaf=is_shape),
        compiler_params=pltpu.CompilerParams(vmem_limit_bytes=VMEM_LIMIT),
        cost_estimate=pl.CostEstimate(flops=500_000_000, bytes_accessed=20_000_000, transcendentals=0),
    )(table, *sources)


def home_table(plan, offsets, band, band_rows):
    own = np.full((4, 2, WINDOWS), 0, np.int32)
    for b in range(4):
        for slot, (m, w) in enumerate(plan[b]):
            if w >= 0:
                own[b, m, w] = slot
        odd, cap = b % 2, len(plan[b])
        mate = plan[b ^ 1]
        sent = mate[:3] if (b ^ 1) in (0, 3) else mate[NEAR_CROSS : NEAR_CROSS + NEAR_CORE]
        for slot, (m, w) in enumerate(sent):
            own[b, m, w] = cap + slot
        if b in (1, 2):
            for slot, (m, w) in enumerate(plan[3 - b][:NEAR_CROSS]):
                own[b, m, w] = cap + NEAR_CORE + slot
    rows = jnp.asarray(own)[band]
    first = jnp.full((2, 1), band_rows, jnp.int32) * band
    return jnp.concatenate([rows, offsets.astype(jnp.int32), first, jnp.zeros((2, 4), jnp.int32)], axis=1)


def last_fused_kernel(
    meta_ref, dqkv_ref, wqkv_ref, x_ref, dmix_ref, gain_ref, dwq_ref, dwp_ref, bias_ref, sums_ref, fc1_ref, rel_ref,
    all_ref, shard_ref, total_ref, rels_ref, ln_ref,
    grad_ref, ln_acc, q_ref, *rest,
):
    w = pl.program_id(0)
    end = pl.num_programs(0) - 1
    half = SHARD_ROWS // 2
    streams = []
    for n, order in enumerate(ORDERS):
        own, *got, sems = rest[7 * n : 7 * n + 7]

        def source(x, img, c, n=n):
            row = pl.multiple_of((2 * x + c) * SHARD_ROWS + n * half, half)
            return q_ref.at[img, pl.ds(row, half)]

        streams.append(Halving(source, own, got, sems, order, half))
    rest = rest[14:]
    small_parts, ln_parts = rest[12:14]
    features = HEAD // 4
    own_features = pl.ds(pl.multiple_of(lax.axis_index("band") * features, features), features)
    small = SmallSum(*rest[:4], lambda i: small_parts.at[i])
    rel = SmallSum(*rest[4:8], lambda i: rest[4].at[own_features])
    ln = SmallSum(*rest[8:12], lambda i: ln_parts.at[i])
    back = Homeward(grad_ref, all_ref, rest[14])

    def start():
        groups = q_ref.shape[0]
        wide, share = 3 * D // groups, D // groups
        for i in range(groups):
            q_ref[i] = jnp.concatenate(
                [dwq_ref[:, wide * i : wide * i + wide], dwp_ref[:, share * i : share * i + share]], axis=1
            )
        greet()
        each(streams, "first")()

    def prepare():
        for r in range(2):
            small.mine[r : r + 1] = jnp.sum(bias_ref[r], axis=0, keepdims=True)
        for r in range(4):
            small.mine[2 + r : 3 + r] = jnp.sum(sums_ref[r], axis=0, keepdims=True)
            small.mine[6 + r : 7 + r] = jnp.sum(fc1_ref[:, D * r : D * r + D], axis=0, keepdims=True)
        small.mine[10:] = jnp.zeros((6, D), F32)
        small_parts[...] = jnp.zeros_like(small_parts)
        ln_parts[...] = jnp.zeros_like(ln_parts)
        rel.mine[...] = rel_ref[:64] + pltpu.roll(rel_ref[64:], 192, 1)
        small.send(0)
        rel.send(0)
        ln_acc[...] = jnp.zeros_like(ln_acc)

    def middle():
        small.add()
        rel.add()
        deal(small.mine, small_parts, 6, 4)
        small.send(1)
        rel.send(1)

    def finish():
        total_ref[...] = small.result()
        rels_ref[...] = rel.result()

    timeline(
        w,
        {
            0: [start, prepare],
            2: [each(streams, "first_done"), each(streams, "step", 0)],
            3: [middle, back.send_core_outer],
            6: [each(streams, "step_done", 0), each(streams, "step", 1), finish],
            8: [each(streams, "step_done", 1), each(streams, "step", 2), back.send_cross],
            12: [each(streams, "step_done", 2), each(streams, "step", 3), back.send_core_inner],
        },
    )

    target = token_target(meta_ref, w)
    dn = jnp.zeros((TW, D), F32)
    for c in range(3):
        cols = slice(D * c, D * c + D)
        dn = dn + mm_nt(dqkv_ref[:, cols], wqkv_ref[:, cols])
    dn = jnp.where(target >= 0, dn, 0.0)
    unit, inverse = norm(x_ref[...].astype(F32))
    ln_acc[0] += fold8(dn * unit)
    ln_acc[1] += fold8(dn)
    grad = dmix_ref[...].astype(F32) + norm_back(dn, unit, inverse, gain_ref[0:1])
    grad_ref[w] = grad.astype(BF16)

    @pl.when(w == end)
    def _():
        back.keep().start()
        ln.mine[0:1] = jnp.sum(ln_acc[0], axis=0, keepdims=True)
        ln.mine[1:2] = jnp.sum(ln_acc[1], axis=0, keepdims=True)
        ln.mine[2:] = jnp.zeros((6, D), F32)
        ln.send(0)
        each(streams, "step_done", 3)()
        ln.add()
        deal(ln.mine, ln_parts, 2, 0)
        ln.send(1)
        for n, stream in enumerate(streams):
            shard_ref[half * n : half * n + half] = stream.result()
        back.keep().wait()
        back.finish()
        ln_ref[...] = ln.result()


def last_fused(meta, dqkv, wqkv, x, dmix, gain, dwq, dwp, bias_sums, sums, fc1_sum, rel_acc):
    cap = meta.shape[0]
    sds = jax.ShapeDtypeStruct
    half = SHARD_ROWS // 2
    anywhere = pl.BlockSpec(memory_space=pl.ANY)
    sums_out = [((SHARD_ROWS, SHARD_COLS), F32), ((16, LANES), F32), ((HEAD // 4, 256), F32), ((8, LANES), F32)]
    return pl.pallas_call(
        last_fused_kernel,
        grid_spec=pltpu.PrefetchScalarGridSpec(
            num_scalar_prefetch=1,
            grid=(cap,),
            in_specs=[
                per_window(TW, 3 * D), whole((D, 3 * D)), per_window(TW, D), per_window(TW, D), whole((8, D)),
                whole((D, 3 * D)), whole((D, D)), whole((2, 8, D)), whole((4, 8, D)), whole((8, FF)), whole((LANES, 256)),
            ],
            out_specs=[anywhere] + [whole(shape) for shape, _ in sums_out],
            scratch_shapes=[
                pltpu.VMEM((cap, TW, D), BF16), pltpu.VMEM((2, 8, D), F32), pltpu.VMEM((8, D, SHARD_COLS), BF16)
            ]
            + Halving.scratch(half) * 2
            + SmallSum.scratch((16, D), (16, LANES)) + SmallSum.scratch((HEAD, 256), (HEAD // 4, 256))
            + SmallSum.scratch((8, D), (8, LANES))
            + [pltpu.VMEM((8, 16, LANES), F32), pltpu.VMEM((8, 8, LANES), F32), pltpu.SemaphoreType.DMA((5,))],
        ),
        out_shape=[sds((cap + NEAR_CORE + NEAR_CROSS, TW, D), BF16)] + [sds(shape, dtype) for shape, dtype in sums_out],
        compiler_params=pltpu.CompilerParams(vmem_limit_bytes=VMEM_LIMIT, collective_id=2, has_side_effects=True),
        cost_estimate=pl.CostEstimate(flops=20_000_000_000, bytes_accessed=50_000_000, transcendentals=0),
    )(meta, dqkv, wqkv, x, dmix, gain, dwq, dwp, bias_sums, sums, fc1_sum, rel_acc)


def window_plan(images, bands):
    lists = [[] for _ in range(bands)]
    if images == 2 and bands == 4:
        spans = (
            ((0, 5, 8), (0, 0, 5), (1, 0, 5)),
            ((0, 10, 15), (0, 8, 10), (1, 5, 10)),
            ((1, 10, 15), (1, 15, 17), (0, 15, 20)),
            ((1, 17, 20), (1, 20, 25), (0, 20, 25)),
        )
        lists = [[(m, w) for m, first, last in row for w in range(first, last)] for row in spans]
    else:
        cuts = [
            [(WINDOWS * b + (bands - 1 if m % 2 else 0)) // bands for b in range(bands + 1)] for m in range(images)
        ]
        for m in range(images):
            for b in range(bands):
                lists[b] += [(m, w) for w in range(cuts[m][b], min(cuts[m][b + 1], WINDOWS))]
    cap = max(len(item) for item in lists)
    return np.array([item + [(0, -1)] * (cap - len(item)) for item in lists], np.int32)


HALO = 12


def near(images, bands, band_rows):
    return images == 2 and bands == 4 and band_rows == 16


CORE = [(0, 1), (1, 0), (2, 3), (3, 2)]
CROSS = [(1, 2), (2, 1)]


def extend(rows, band):
    images, band_rows = rows.shape[:2]
    if not near(images, lax.axis_size("band"), band_rows):
        full = lax.all_gather(rows, "band", axis=1, tiled=True)
        return jnp.pad(full, ((0, 0), (6, 6), (0, 0), (0, 0)))
    odd = band % 2 == 1
    top, bottom = rows[:, :HALO], rows[:, -HALO:]
    from_core = lax.ppermute(jnp.where(odd, top, bottom), "band", CORE)
    from_cross = lax.ppermute(jnp.where(odd, bottom[1], top[0]), "band", CROSS)
    zero = jnp.zeros_like(from_cross)
    above = jnp.where(odd, from_core, jnp.stack([zero, from_cross]))
    below = jnp.where(odd, jnp.stack([from_cross, zero]), from_core)
    return jnp.concatenate([above, rows, below], axis=1)


def collect(ext, band, images, band_rows):
    if not near(images, lax.axis_size("band"), band_rows):
        return lax.psum_scatter(ext[:, 6:-6], "band", scatter_dimension=1, tiled=True).astype(F32)
    odd = band % 2 == 1
    above, below = ext[:, :HALO], ext[:, -HALO:]
    from_core = lax.ppermute(jnp.where(odd, above, below), "band", CORE).astype(F32)
    from_cross = lax.ppermute(jnp.where(odd, below[0], above[1]), "band", CROSS).astype(F32)
    zero = jnp.zeros_like(from_cross)
    top = jnp.where(odd, from_core, jnp.stack([from_cross, zero]))
    bottom = jnp.where(odd, jnp.stack([zero, from_cross]), from_core)
    own = ext[:, HALO:-HALO].astype(F32)
    rest = band_rows - HALO
    return own + jnp.pad(top, ((0, 0), (0, rest), (0, 0), (0, 0))) + jnp.pad(bottom, ((0, 0), (rest, 0), (0, 0), (0, 0)))


def shards(
    image_tokens, pad_offsets, ln1_gain, ln1_bias, w_qkv, q_bias, v_bias, rel_rows, rel_cols, w_proj, proj_bias,
    ln2_gain, ln2_bias, w_fc1, fc1_bias, w_fc2, fc2_bias, out_grad,
):
    images, band_rows = image_tokens.shape[:2]
    bands, groups = lax.axis_size("band"), lax.axis_size("img")
    band, group = lax.axis_index("band"), lax.axis_index("img")
    axes = ("img", "band")

    part, wide = w_qkv.shape
    close = near(images, bands, band_rows)
    fused = close and groups == 8
    share = D // groups
    vector_rows = [ln1_gain, ln1_bias, q_bias, v_bias, proj_bias, ln2_gain, ln2_bias, fc2_bias]
    small = jnp.concatenate([v[None] for v in vector_rows] + [fc1_bias.reshape(4, share), jnp.zeros((4, share), BF16)])
    block_cols = wide + w_proj.shape[1]
    small_rows = 16
    if fused:
        block, ff_block = pack(w_qkv, w_proj, small, rel_rows.T, rel_cols.T, w_fc1, w_fc2.T)
        first, ext, gext = entry(block, image_tokens, out_grad)
    else:
        features = rel_rows.shape[1]
        rest = jnp.zeros((small_rows, block_cols - share - 2 * RELS), BF16)
        tables = [jnp.pad(rel.T, ((0, small_rows - features), (0, 0))) for rel in (rel_rows, rel_cols)]
        block = jnp.concatenate(
            [jnp.concatenate([w_qkv, w_proj], axis=1), jnp.concatenate([small, *tables, rest], axis=1)], axis=0
        )
        ff_block = jnp.concatenate([w_fc1, w_fc2.T], axis=1)
        first = lax.all_gather(block, axes, axis=0, tiled=False).reshape(groups, bands, part + small_rows, block_cols)
        ext, gext = extend(image_tokens, band), extend(out_grad, band)
    ff = lax.all_gather(ff_block, axes, axis=0, tiled=False).reshape(groups, bands * part, -1)
    tail = first[:, :, part:]
    vectors = tail[:, 0, :8, :share].transpose(1, 0, 2).reshape(8, D).astype(F32)
    fc1_shift = tail[:, 0, 8:12, :share].reshape(1, FF).astype(F32)
    features = HEAD // bands
    rels = [tail[0, :, :features, at : at + RELS].reshape(HEAD, RELS) for at in (share, share + RELS)]
    plan = jnp.asarray(window_plan(images, bands))[band]
    image, window = plan[:, 0], plan[:, 1]
    ext_per = band_rows + 2 * HALO if close else bands * band_rows + 12
    base = band_rows * band - HALO if close else -6
    live = window >= 0
    spot = jnp.maximum(window, 0)
    offsets = pad_offsets[image]
    row = spot // GRID * WIN - offsets[:, 0]
    col = spot % GRID * WIN - offsets[:, 1]
    meta = jnp.stack(
        [jnp.where(live, image * ext_per + row - base, HALO), col, row, live.astype(jnp.int32)], axis=1
    ).astype(jnp.int32)
    cap = meta.shape[0]
    ext_rows = images * ext_per

    ka, kb, kback = key_constants()
    ext, gext = ext.reshape(ext_rows, SIDE, D), gext.reshape(ext_rows, SIDE, D)
    if not fused:
        weights = first[:, :, :part].transpose(1, 2, 0, 3)
        wqkv, wproj = weights[..., :wide].reshape(D, 3 * D), weights[..., wide:].reshape(D, D)
    x, g, normed1, qkv, probs, inv, att, *weights = attention_forward(
        meta, ext, gext, vectors, first if fused else wqkv, rel_table(rels[0], rels[1], True), ka, kb
    )
    if fused:
        wqkv, wproj = weights
    out_win, normed2, act, d_pre, d_mixed, d_att, sums, sum_fc1 = feed_forward(
        g, x, att, wproj, vectors, ff, fc1_shift, 0
    )

    def flat(a):
        return a.reshape(-1, a.shape[-1])

    def weight_grad(left, right):
        return jnp.einsum("td,te->de", flat(left), flat(right), preferred_element_type=F32).astype(BF16)

    if fused:
        inner = (band == 1) | (band == 2)
        to_core = lax.dynamic_slice_in_dim(out_win, jnp.where(inner, NEAR_CROSS, 0), NEAR_CORE, 0)
        core_out = lax.ppermute(to_core, "band", CORE)
        cross_out = lax.ppermute(out_win[:NEAR_CROSS], "band", CROSS)
    d_fc2 = weight_grad(g, act)
    d_fc1 = weight_grad(normed2, d_pre)
    d_proj = weight_grad(att, d_mixed)
    if fused:
        d_fc1, d_fc2, core_out, cross_out = lax.optimization_barrier((d_fc1, d_fc2, core_out, cross_out))
    d_qkv, rel_acc, bias_sums, *done = attention_backward(
        meta, qkv, probs, inv, att, d_att, rel_table(rels[0], rels[1], False), kback,
        (d_fc1, d_fc2) if fused else (),
    )
    d_wqkv = weight_grad(normed1, d_qkv)

    if fused:
        partial, g_fc2 = done

        def fold(value, axis, bit, step):
            mine = lax.dynamic_index_in_dim(value, bit, axis, keepdims=False)
            other = lax.dynamic_index_in_dim(value, 1 - bit, axis, keepdims=False)
            came = lax.ppermute(other, "img", [(i, i ^ step) for i in range(groups)])
            return mine.astype(F32) + came.astype(F32)

        partial = fold(partial, 1, group // 4, 4).astype(BF16)
        g_fc1 = fold(partial, 1, group // 2 % 2, 2).reshape(part, FF // groups)
        all_grad, q_shard, total, rel_total, ln_total = last_fused(
            meta, d_qkv, wqkv, x, d_mixed, vectors, d_wqkv, d_proj, bias_sums, sums, sum_fc1, rel_acc
        )
        output, input_grad, shares, b1_share, d_rel_rows, d_rel_cols, g_qkv, g_proj = home(
            home_table(window_plan(images, bands), pad_offsets, band, band_rows),
            (out_win, core_out, cross_out, all_grad, total, ln_total, rel_total, q_shard), band_rows,
        )
        ln1g, ln1b, qb, vb, pb, ln2g, ln2b, b2 = [share.reshape(-1) for share in shares]
        return (
            output, input_grad, ln1g, ln1b, g_qkv, qb, vb, d_rel_rows.T, d_rel_cols.T, g_proj, pb, ln2g, ln2b, g_fc1,
            b1_share.reshape(-1), g_fc2.T, b2,
        )
    else:
        out_ext = scatter(meta, out_win, ext_rows).reshape(images, ext_per, SIDE, D)
        output = collect(out_ext, band, images, band_rows).astype(BF16)
        in_ext, sums1 = last_norm(meta, d_qkv, wqkv, x, d_mixed, vectors, ext_rows)
        input_grad = collect(in_ext.reshape(images, ext_per, SIDE, D), band, images, band_rows)

        def reduce(grad):
            grad = lax.psum_scatter(grad, "img", scatter_dimension=1, tiled=True)
            return lax.psum_scatter(grad, "band", scatter_dimension=0, tiled=True).astype(F32)

        g_fc1, g_fc2, g_qkv, g_proj = reduce(d_fc1), reduce(d_fc2), reduce(d_wqkv), reduce(d_proj)
        ln_total, bias_total, sum_total, fc1_total, d_rel_rows, d_rel_cols = lax.psum(
            (jnp.sum(sums1, 1), jnp.sum(bias_sums, 1), jnp.sum(sums, 1), jnp.sum(sum_fc1, 0)) + rel_from(rel_acc), axes
        )

    def img_share(vector):
        n = vector.shape[0] // groups
        return lax.dynamic_slice_in_dim(vector, group * n, n, 0)

    def band_share(table):
        n = table.shape[1] // bands
        return lax.dynamic_slice_in_dim(table, band * n, n, 1)

    return (
        output,
        input_grad,
        img_share(ln_total[0]),
        img_share(ln_total[1]),
        g_qkv,
        img_share(bias_total[0]),
        img_share(bias_total[1]),
        band_share(d_rel_rows),
        band_share(d_rel_cols),
        g_proj,
        img_share(sum_total[3]),
        img_share(sum_total[1]),
        img_share(sum_total[2]),
        g_fc1,
        img_share(fc1_total),
        g_fc2.T,
        img_share(sum_total[0]),
    )


def solution(mesh):
    tokens, vector, matrix = P("img", "band", None, None), P("img"), P("band", "img")
    table, wide = P(None, "band"), P("img", "band")
    return jax.shard_map(
        shards,
        mesh=mesh,
        in_specs=(
            tokens, P("img", None), vector, vector, matrix, vector, vector, table, table, matrix, vector, vector,
            vector, matrix, vector, wide, vector, tokens,
        ),
        out_specs=(
            tokens, tokens, vector, vector, matrix, vector, vector, table, table, matrix, vector, vector, vector,
            matrix, vector, wide, vector,
        ),
        check_vma=False,
    )
```

```python
import functools
import numpy as np
import jax
import jax.numpy as jnp
from jax import lax
from jax.sharding import PartitionSpec as P
from jax.experimental import pallas as pl
from jax.experimental.pallas import tpu as pltpu

D = 768
HEADS = 12
HEAD = 64
FF = 3072
WIN = 14
SIDE = 64
GRID = 5
WINDOWS = 25
RELS = 27
STRIDE = 16
TW = WIN * STRIDE
PAIRS = HEADS // 2
LANES = 128
EPSILON = 1e-06
F32 = jnp.float32
BF16 = jnp.bfloat16
VMEM_LIMIT = 60 * 1024 * 1024
NT = (((1,), (1,)), ((), ()))


def mm(a, b):
    return jnp.dot(a, b, preferred_element_type=F32)


def mm_nt(a, b):
    return lax.dot_general(a, b, NT, preferred_element_type=F32)


def iota(shape, dim):
    return lax.broadcasted_iota(jnp.int32, shape, dim)


def token_target(meta_ref, w):
    t = iota((TW, 1), 0)
    a, b = t >> 4, t & 15
    col = meta_ref[w, 1] + b
    row = meta_ref[w, 2] + a
    ok = (b < WIN) & (col >= 0) & (col < SIDE) & (row >= 0) & (row < SIDE) & (meta_ref[w, 3] > 0)
    return jnp.where(ok, ((a & 3) << 6) + col, -1)


def take_window(target, rows_ref):
    picks = jnp.where(iota((TW, 256), 1) == target, 1.0, 0.0).astype(BF16)
    parts = []
    for q in range(3):
        src = rows_ref[4 * q : 4 * q + 4].reshape(256, D)
        parts.append(mm(picks[64 * q : 64 * q + 64], src))
    src = rows_ref[12:14].reshape(128, D)
    parts.append(mm(picks[192:224, :128], src))
    return jnp.concatenate(parts, axis=0)


def norm(values):
    mean = jnp.sum(values, axis=-1, keepdims=True) * (1.0 / D)
    centred = values - mean
    inverse = lax.rsqrt(jnp.sum(centred * centred, axis=-1, keepdims=True) * (1.0 / D) + EPSILON)
    return centred * inverse, inverse


def norm_back(grad, unit, inverse, gain):
    s = grad * gain
    m1 = jnp.sum(s, axis=-1, keepdims=True) * (1.0 / D)
    m2 = jnp.sum(s * unit, axis=-1, keepdims=True) * (1.0 / D)
    return inverse * (s - m1 - unit * m2)


def fold8(x):
    return jnp.sum(x.reshape(x.shape[0] // 8, 8, x.shape[1]), axis=0)


def roll_rows(x, forward):
    out = []
    for a in range(WIN):
        piece = x[STRIDE * a : STRIDE * a + STRIDE]
        by = (a - 13) % LANES if forward else a
        out.append(pltpu.roll(piece, by, 1) if by else piece)
    return jnp.concatenate(out, axis=0)


def roll_cols(x, first):
    out = []
    for a in range(WIN):
        piece = x[STRIDE * a : STRIDE * a + STRIDE]
        out.append(pltpu.roll(piece, first, 1, stride=1, stride_axis=0))
    return jnp.concatenate(out, axis=0)


def attn_fwd_pair(q, k8, v, table, keys_a, keys_b, p_ref, p):
    lane = iota((TW, LANES), 1)
    low_half = lane < 64
    rc = mm(q, table)
    both = jnp.where((lane & 31) < 16, roll_rows(rc[:, :LANES], True), roll_cols(rc[:, LANES:], 3))
    high = both.astype(BF16)
    rest = (both - high.astype(F32)).astype(BF16)
    extra = jnp.where((lane & 63) < 32, high, rest)
    extra = jnp.where((lane & 63) == 14, jnp.ones_like(extra), extra)
    left = jnp.concatenate([q, extra], axis=1)
    zero = jnp.zeros_like(k8)
    wide_v = jnp.concatenate([v, jnp.ones_like(v)], axis=1)
    outs, invs = [], []
    for h in range(2):
        keys = jnp.concatenate(
            [jnp.where(low_half if h == 0 else ~low_half, k8, zero), (keys_a, keys_b)[h]], axis=1
        )
        s = mm_nt(left, keys)
        e = jnp.exp(s - jnp.max(s, axis=-1, keepdims=True)).astype(BF16)
        p_ref[2 * p + h] = e
        o = mm(e, wide_v)
        inv = 1.0 / o[:, LANES:]
        outs.append(o[:, :LANES] * inv)
        invs.append(inv)
    att = jnp.where(low_half, outs[0], outs[1]).astype(BF16)
    inv = jnp.where(low_half, invs[0], invs[1])
    return att, inv


def fwd_kernel(
    meta_ref, rows_ref, grows_ref, vec_ref, wqkv_ref, table_ref, ka_ref, kb_ref,
    x_ref, g_ref, n_ref, qkv_ref, p_ref, inv_ref, att_ref, *weights,
):
    w = pl.program_id(0)
    if weights:
        blocks_ref, (wqkv_ref, wproj_ref) = wqkv_ref, weights

        @pl.when(w == 0)
        def _():
            share = D // blocks_ref.shape[0]
            for b in range(blocks_ref.shape[1]):
                rows = slice(SHARD_ROWS * b, SHARD_ROWS * b + SHARD_ROWS)
                parts = [blocks_ref[i, b, :SHARD_ROWS] for i in range(blocks_ref.shape[0])]
                wqkv_ref[rows] = jnp.concatenate([part[:, : 3 * share] for part in parts], axis=1)
                wproj_ref[rows] = jnp.concatenate([part[:, 3 * share :] for part in parts], axis=1)

    target = token_target(meta_ref, w)
    x = take_window(target, rows_ref)
    x_ref[...] = x.astype(BF16)
    g_ref[...] = take_window(target, grows_ref).astype(BF16)
    unit, _ = norm(x)
    normed = jnp.where(target >= 0, unit * vec_ref[0:1] + vec_ref[1:2], 0.0).astype(BF16)
    n_ref[...] = normed
    for c in range(9):
        cols = slice(256 * c, 256 * c + 256)
        y = mm(normed, wqkv_ref[:, cols])
        if c < 3:
            y = y + vec_ref[2:3, cols]
        elif c >= 6:
            y = y + vec_ref[3:4, 256 * (c - 6) : 256 * (c - 6) + 256]
        else:
            y = y.astype(BF16).astype(F32) * 0.125
        qkv_ref[:, cols] = y.astype(BF16)

    for p in range(PAIRS):
        a = slice(LANES * p, LANES * p + LANES)
        q = qkv_ref[:, LANES * p : LANES * p + LANES]
        k8 = qkv_ref[:, D + LANES * p : D + LANES * p + LANES]
        v = qkv_ref[:, 2 * D + LANES * p : 2 * D + LANES * p + LANES]
        att, inv = attn_fwd_pair(q, k8, v, table_ref[...], ka_ref[...], kb_ref[...], p_ref, p)
        att_ref[:, a] = att
        inv_ref[:, a] = inv


def rows_spec(rows):
    return pl.BlockSpec(
        (pl.Element(rows), pl.Element(SIDE), pl.Element(D)), lambda w, meta: (meta[w, 0], 0, 0)
    )


def whole(shape, buffers=1):
    zeros = (0,) * len(shape)
    return pl.BlockSpec(shape, lambda w, meta: zeros, pipeline_mode=pl.Buffered(buffers))


def per_window(*tail):
    zeros = (0,) * len(tail)
    return pl.BlockSpec((None,) + tail, lambda w, meta: (w,) + zeros)


def key_constants():
    t = np.arange(TW)
    kr, kc = t >> 4, t & 15
    real = kc < WIN
    base = np.zeros((TW, 64), np.float32)
    for off in (0, 32):
        base[t[real], off + kr[real]] = 1.0
        base[t[real], off + 16 + kc[real]] = 1.0
    back = np.zeros_like(base)
    back[t[real], 13 - kr[real]] = 1.0
    back[t[real], 16 + 13 - kc[real]] = 1.0
    base[~real, 14] = -1e30
    none = np.zeros_like(base)
    ka = np.concatenate([base, none], 1)
    kb = np.concatenate([none, base], 1)
    back = np.concatenate([back, back], 1)
    return jnp.asarray(ka, BF16), jnp.asarray(kb, BF16), jnp.asarray(back, BF16)


def rel_table(rel_rows, rel_cols, forward):
    def wide(rel):
        turned = jnp.pad(rel, ((0, 0), (0, 32 - RELS)))
        twice = jnp.concatenate([turned, turned], axis=1)
        none = jnp.zeros_like(twice)
        return jnp.concatenate(
            [jnp.concatenate([twice, none], 1), jnp.concatenate([none, twice], 1)], 0
        )

    turn = (lambda rel: rel[:, ::-1]) if forward else (lambda rel: rel)
    return jnp.concatenate([wide(turn(rel_rows)), wide(turn(rel_cols))], axis=1)


def attention_forward(meta, ext, gext, vectors, wqkv, table, ka, kb):
    cap = meta.shape[0]
    weights = [(D, 3 * D), (D, D)] if wqkv.ndim == 4 else []
    sds = jax.ShapeDtypeStruct
    return pl.pallas_call(
        fwd_kernel,
        grid_spec=pltpu.PrefetchScalarGridSpec(
            num_scalar_prefetch=1,
            grid=(cap,),
            in_specs=[
                rows_spec(WIN), rows_spec(WIN), whole((8, D)), whole(wqkv.shape),
                whole((LANES, 256)), whole((TW, LANES)), whole((TW, LANES)),
            ],
            out_specs=[
                per_window(TW, D), per_window(TW, D), per_window(TW, D), per_window(TW, 3 * D),
                per_window(HEADS, TW, TW), per_window(TW, D), per_window(TW, D),
            ] + [whole(shape) for shape in weights],
        ),
        out_shape=[
            sds((cap, TW, D), BF16), sds((cap, TW, D), BF16), sds((cap, TW, D), BF16), sds((cap, TW, 3 * D), BF16),
            sds((cap, HEADS, TW, TW), BF16), sds((cap, TW, D), F32), sds((cap, TW, D), BF16),
        ] + [sds(shape, BF16) for shape in weights],
        compiler_params=pltpu.CompilerParams(vmem_limit_bytes=VMEM_LIMIT),
        cost_estimate=pl.CostEstimate(flops=40_000_000_000, bytes_accessed=80_000_000, transcendentals=8_000_000),
    )(meta, ext, gext, vectors, wqkv, table, ka, kb)


def phi_parts(u):
    e = jnp.exp(u * u * -0.5)
    t = 1.0 / (1.0 + (0.3275911 * 0.7071067811865476) * jnp.abs(u))
    poly = t * (0.254829592 + t * (-0.284496736 + t * (1.421413741 + t * (-1.453152027 + t * 1.061405429))))
    tail = 0.5 * poly * e
    return jnp.where(u >= 0, 1.0 - tail, tail), e * 0.3989422804014327


def mlp_kernel(
    g_ref, x_ref, att_ref, wproj_ref, vec_ref, ff_ref, b1_ref,
    out_ref, n2_ref, act_ref, dpre_ref, dmix_ref, datt_ref, sums_ref, sum1_ref,
    acc_ref, dn_ref,
):
    @pl.when(pl.program_id(0) == 0)
    def _():
        sums_ref[...] = jnp.zeros_like(sums_ref)
        sum1_ref[...] = jnp.zeros_like(sum1_ref)

    gb = g_ref[...]
    g = gb.astype(F32)
    sums_ref[0] += fold8(g)
    hidden = x_ref[...].astype(F32) + mm(att_ref[...], wproj_ref[...]) + vec_ref[4:5]
    unit, inverse = norm(hidden)
    n2 = (unit * vec_ref[5:6] + vec_ref[6:7]).astype(BF16)
    n2_ref[...] = n2
    acc_ref[...] = hidden + vec_ref[7:8]
    parts, inner = ff_ref.shape[0], ff_ref.shape[2] // 2
    join = max(1, 1536 // inner)
    chunk = inner * join
    for c in range(parts // join):
        cols = slice(chunk * c, chunk * c + chunk)
        blocks = range(join * c, join * c + join)
        w1 = jnp.concatenate([ff_ref[i, :, :inner] for i in blocks], axis=1)
        w2t = jnp.concatenate([ff_ref[i, :, inner:] for i in blocks], axis=1)
        u = mm(n2, w1) + b1_ref[:, cols]
        dact = mm(gb, w2t)
        cdf, pdf = phi_parts(u)
        act = (u * cdf).astype(BF16)
        act_ref[:, cols] = act
        acc_ref[...] += mm_nt(act, w2t)
        dpre32 = dact * (cdf + u * pdf)
        dpre = dpre32.astype(BF16)
        dpre_ref[:, cols] = dpre
        sum1_ref[:, cols] += fold8(dpre32)
        step = mm_nt(dpre, w1)
        if c == 0:
            dn_ref[...] = step
        else:
            dn_ref[...] += step
    out_ref[...] = acc_ref[...].astype(BF16)
    dn = dn_ref[...]
    sums_ref[1] += fold8(dn * unit)
    sums_ref[2] += fold8(dn)
    dh = g + norm_back(dn, unit, inverse, vec_ref[5:6])
    dmix = dh.astype(BF16)
    dmix_ref[...] = dmix
    sums_ref[3] += fold8(dh)
    datt_ref[...] = mm_nt(dmix, wproj_ref[...]).astype(BF16)


def tile_rows(rows):
    return next(t for t in (416, 448, 224) if rows % t == 0)


def feed_forward(g, x, att, wproj, vectors, ff, b1, spare):
    cap = g.shape[0]
    rows = cap * TW
    tile = tile_rows(rows)
    sds = jax.ShapeDtypeStruct

    def tiled(width):
        return pl.BlockSpec((tile, width), lambda i: (i, 0))

    def kept(shape):
        zeros = (0,) * len(shape)
        return pl.BlockSpec(shape, lambda i: zeros, pipeline_mode=pl.Buffered(1))

    out, *rest = pl.pallas_call(
        mlp_kernel,
        grid=(rows // tile,),
        in_specs=[
            tiled(D), tiled(D), tiled(D), kept((D, D)), kept((8, D)), kept(ff.shape), kept((1, FF)),
        ],
        out_specs=[tiled(D), tiled(D), tiled(FF), tiled(FF), tiled(D), tiled(D), kept((4, 8, D)), kept((8, FF))],
        scratch_shapes=[pltpu.VMEM((tile, D), F32), pltpu.VMEM((tile, D), F32)],
        out_shape=[
            sds((rows + spare * TW, D), BF16), sds((rows, D), BF16), sds((rows, FF), BF16), sds((rows, FF), BF16),
            sds((rows, D), BF16), sds((rows, D), BF16), sds((4, 8, D), F32), sds((8, FF), F32),
        ],
        compiler_params=pltpu.CompilerParams(vmem_limit_bytes=VMEM_LIMIT),
        cost_estimate=pl.CostEstimate(flops=60_000_000_000, bytes_accessed=80_000_000, transcendentals=8_000_000),
    )(g.reshape(rows, D), x.reshape(rows, D), att.reshape(rows, D), wproj, vectors, ff, b1)
    return out.reshape(cap + spare, TW, D), rest[0], rest[1], rest[2], *[a.reshape(cap, TW, D) for a in rest[3:5]], *rest[5:]


MESH = pl.DeviceIdType.MESH
SHARD_ROWS = 192
SHARD_COLS = 384


def place():
    img, band = lax.axis_index("img"), lax.axis_index("band")
    return {"zh": img // 4, "zl": img // 2 % 2, "y": img % 2, "x": band // 2, "c": band % 2}


def partner(dim):
    img, band = lax.axis_index("img"), lax.axis_index("band")
    at = place()[dim]
    step = {"zh": 4, "zl": 2, "y": 1, "x": 2, "c": 1}[dim]
    move = step - 2 * step * at
    return (img, band + move) if dim in ("x", "c") else (img + move, band)


def peers():
    img, band = lax.axis_index("img"), lax.axis_index("band")
    return [(img, (band + d) % 4) for d in range(1, 4)], [((img + d) % 8, band) for d in range(1, 8)]


def greet():
    barrier = pltpu.get_barrier_semaphore()
    near_by, far = peers()
    for device in near_by + far:
        pl.semaphore_signal(barrier, inc=1, device_id=device, device_id_type=MESH)
    pl.semaphore_wait(barrier, 10)


class Halving:
    AXES = ("x", "zh", "zl", "y")

    def __init__(self, source, own, got, sems, order, rows):
        self.source, self.own, self.got, self.sems, self.order, self.rows = source, own, got, sems, order, rows
        self.at = place()

    @staticmethod
    def scratch(rows):
        shapes = [(2, 2, 2, 2), (2, 2, 2, 2), (2, 2, 2), (2, 2), (2,), (1,)]
        return [pltpu.VMEM(s + (rows, SHARD_COLS), BF16) for s in shapes] + [pltpu.SemaphoreType.DMA((11,))]

    def first(self):
        c = self.at["c"]
        send, recv, local = self.sems.at[0], self.sems.at[1], self.sems.at[10]
        for x in range(2):
            for img in range(8):
                spot = (x, img // 4, img // 2 % 2, img % 2)
                pltpu.make_async_remote_copy(
                    src_ref=self.source(x, img, 1 - c), dst_ref=self.got[0].at[spot], send_sem=send, recv_sem=recv,
                    device_id=partner("c"), device_id_type=MESH,
                ).start()
                pltpu.make_async_copy(self.source(x, img, c), self.own.at[spot], local).start()

    def first_done(self):
        send, recv, local = self.sems.at[0], self.sems.at[1], self.sems.at[10]
        whole = pltpu.make_async_remote_copy(
            src_ref=self.got[0], dst_ref=self.got[0], send_sem=send, recv_sem=recv,
            device_id=partner("c"), device_id_type=MESH,
        )
        whole.wait_send()
        whole.wait_recv()
        pltpu.make_async_copy(self.got[0], self.own, local).wait()

        def add(i, _):
            spot = (i // 8, i // 4 % 2, i // 2 % 2, i % 2)
            self.own[spot] = self.own[spot] + self.got[0][spot]
            return 0

        lax.fori_loop(0, 16, add, 0)

    def index(self, k, dim=None):
        spot = []
        for axis in self.AXES:
            if axis == dim:
                spot.append(1 - self.at[axis])
            elif axis in self.order[:k]:
                spot.append(self.at[axis])
            else:
                spot.append(slice(None))
        return tuple(spot)

    def copy(self, k):
        dim = self.order[k]
        src = self.own.at[self.index(k, dim)]
        dst = self.got[k + 1].at[0] if k == 3 else self.got[k + 1]
        return pltpu.make_async_remote_copy(
            src_ref=src, dst_ref=dst, send_sem=self.sems.at[2 + 2 * k], recv_sem=self.sems.at[3 + 2 * k],
            device_id=partner(dim), device_id_type=MESH,
        )

    def step(self, k):
        self.copy(k).start()

    def step_done(self, k):
        self.copy(k).wait()
        done = self.order[: k + 1]
        free = [axis for axis in self.AXES if axis not in done]
        count = 2 ** len(free)

        def add(i, _):
            bits = {axis: (i // 2 ** (len(free) - 1 - j)) % 2 for j, axis in enumerate(free)}
            spot = tuple(bits[axis] if axis in bits else self.at[axis] for axis in self.AXES)
            self.own[spot] = self.own[spot] + self.got[k + 1][tuple(bits[axis] for axis in free)]
            return 0

        if k < 3:
            lax.fori_loop(0, count, add, 0)

    def result(self):
        spot = tuple(self.at[axis] for axis in self.AXES)
        return self.own[spot].astype(F32) + self.got[4][0].astype(F32)


ORDERS = (("x", "y", "zh", "zl"), ("y", "x", "zh", "zl"))


def wide_source(ref, part):
    half = SHARD_ROWS // 2

    def source(x, img, c):
        row = pl.multiple_of((2 * x + c) * SHARD_ROWS + part * half, half)
        return ref.at[pl.ds(row, half), pl.ds(img * SHARD_COLS, SHARD_COLS)]

    return source


def each(group, name, *args):
    def body():
        for stream in group:
            getattr(stream, name)(*args)

    return body


def timeline(w, moments):
    for when, bodies in moments.items():
        @pl.when(w == when)
        def _(bodies=bodies):
            for body in bodies:
                body()


NEAR_CORE = 7
NEAR_CROSS = 5
CROSS_ROWS = 160


class Homeward:
    def __init__(self, windows, everything, sems):
        self.windows, self.all, self.sems = windows, everything, sems
        self.cap = everything.shape[0] - NEAR_CORE - NEAR_CROSS
        self.band = lax.axis_index("band")

    def inner(self):
        return (self.band == 1) | (self.band == 2)

    def outer(self):
        return (self.band == 0) | (self.band == 3)

    def keep(self):
        return pltpu.make_async_copy(self.windows, self.all.at[pl.ds(0, self.cap)], self.sems.at[4])

    def to_core(self, first, count):
        return pltpu.make_async_remote_copy(
            src_ref=self.windows.at[pl.ds(first, count)], dst_ref=self.all.at[pl.ds(self.cap, count)],
            send_sem=self.sems.at[0], recv_sem=self.sems.at[1], device_id=partner("c"), device_id_type=MESH,
        )

    def to_cross(self, sending):
        img = lax.axis_index("img")
        skip = (2 - self.band) if sending else (self.band - 1)
        rows = pl.ds(pl.multiple_of(skip * (TW - CROSS_ROWS), TW - CROSS_ROWS), CROSS_ROWS)
        return pltpu.make_async_remote_copy(
            src_ref=self.windows.at[pl.ds(0, NEAR_CROSS), rows],
            dst_ref=self.all.at[pl.ds(self.cap + NEAR_CORE, NEAR_CROSS), rows],
            send_sem=self.sems.at[2], recv_sem=self.sems.at[3], device_id=(img, 3 - self.band), device_id_type=MESH,
        )

    def send_cross(self):
        pl.when(self.inner())(lambda: self.to_cross(True).start())

    def send_core_inner(self):
        pl.when(self.inner())(lambda: self.to_core(NEAR_CROSS, NEAR_CORE).start())

    def send_core_outer(self):
        pl.when(self.outer())(lambda: self.to_core(0, 3).start())

    def finish(self):
        @pl.when(self.inner())
        def _():
            self.to_core(NEAR_CROSS, NEAR_CORE).wait_send()
            self.to_core(0, 3).wait_recv()
            self.to_cross(True).wait_send()
            self.to_cross(False).wait_recv()

        @pl.when(self.outer())
        def _():
            self.to_core(0, 3).wait_send()
            self.to_core(NEAR_CROSS, NEAR_CORE).wait_recv()


class Gather:
    def __init__(self, block, out, sems):
        self.block, self.out, self.sems = block, out, sems
        img, self.band = lax.axis_index("img"), lax.axis_index("band")
        self.z, self.y = img // 2, img % 2
        self.x, self.c = self.band // 2, self.band % 2

    def where(self, dz, fx, fy):
        img = (self.z + 4 - dz) % 4 * 2 + (1 - self.y if fy else self.y)
        return img, (1 - self.x if fx else self.x) * 2 + self.c

    def move(self, k, dz, fx, fy, device):
        img, band = self.where(dz, fx, fy)
        own = (dz, fx, fy) == (0, 0, 0)
        return pltpu.make_async_remote_copy(
            src_ref=self.block if own else self.out.at[img, band], dst_ref=self.out.at[img, band],
            send_sem=self.sems.at[0, k], recv_sem=self.sems.at[1, k], device_id=device, device_id_type=MESH,
        )

    def along_z(self, d):
        return self.move(d - 1, 0, 0, 0, ((self.z + d) % 4 * 2 + self.y, self.band))

    def along_x(self, dz):
        return self.move(3 + dz, dz, 0, 0, partner("x"))

    def along_y(self, fx, dz):
        return self.move(7 + 4 * fx + dz, dz, fx, 0, partner("y"))

    def to_core(self, fy, fx, dz):
        return self.move(15 + 8 * fy + 4 * fx + dz, dz, fx, fy, partner("c"))

    def keep(self):
        img, band = self.where(0, 0, 0)
        return pltpu.make_async_copy(self.block, self.out.at[img, band], self.sems.at[0, 31])

    def pass_on(self, dz):
        self.along_x(dz).start()
        self.along_y(0, dz).start()
        self.to_core(0, 0, dz).start()

    def begin(self):
        self.keep().start()
        for d in range(1, 4):
            self.along_z(d).start()
        self.pass_on(0)

    def run(self, then):
        for dz in range(1, 4):
            self.along_z(dz).wait_recv()
            self.pass_on(dz)
        then()
        for dz in range(4):
            self.along_x(dz).wait_recv()
            self.along_y(1, dz).start()
            self.to_core(0, 1, dz).start()
        for fx in range(2):
            for dz in range(4):
                self.along_y(fx, dz).wait_recv()
                self.to_core(1, fx, dz).start()
        for d in range(1, 4):
            self.along_z(d).wait_send()
        for dz in range(4):
            self.along_x(dz).wait_send()
            for fx in range(2):
                self.along_y(fx, dz).wait_send()
                for fy in range(2):
                    self.to_core(fy, fx, dz).wait()
        self.keep().wait()


CROSS_HALO = 10


class Edges:
    def __init__(self, rows, ext, zero, sems):
        self.rows, self.ext, self.zero, self.sems = rows, ext, zero, sems
        self.band = lax.axis_index("band")
        self.own_rows = rows.shape[1]

    def inner(self):
        return (self.band == 1) | (self.band == 2)

    def keep(self):
        return pltpu.make_async_copy(self.rows, self.ext.at[:, pl.ds(HALO, self.own_rows)], self.sems.at[0])

    def empty(self):
        at = self.band // 3 * (HALO + self.own_rows)
        return [
            pltpu.make_async_copy(self.zero, self.ext.at[m, pl.ds(at, HALO)], self.sems.at[1 + m]) for m in range(2)
        ]

    def core(self, sending):
        odd = self.band % 2
        far = self.own_rows - HALO
        there = (odd if sending else 1 - odd) * (HALO + self.own_rows)
        return pltpu.make_async_remote_copy(
            src_ref=self.rows.at[:, pl.ds((1 - odd) * far, HALO)], dst_ref=self.ext.at[:, pl.ds(there, HALO)],
            send_sem=self.sems.at[3], recv_sem=self.sems.at[4], device_id=partner("c"), device_id_type=MESH,
        )

    def cross(self, sending):
        img = lax.axis_index("img")
        m = 2 - self.band
        far = self.own_rows - CROSS_HALO
        to = m if sending else 1 - m
        there = to * (HALO - CROSS_HALO) + (1 - to) * (HALO + self.own_rows)
        return pltpu.make_async_remote_copy(
            src_ref=self.rows.at[m, pl.ds(m * far, CROSS_HALO)], dst_ref=self.ext.at[to, pl.ds(there, CROSS_HALO)],
            send_sem=self.sems.at[5], recv_sem=self.sems.at[6], device_id=(img, 3 - self.band), device_id_type=MESH,
        )

    def start_cross(self):
        pl.when(self.inner())(lambda: self.cross(True).start())

    def start(self):
        self.core(True).start()
        self.keep().start()

        @pl.when(jnp.logical_not(self.inner()))
        def _():
            for copy in self.empty():
                copy.start()

    def finish(self):
        self.core(True).wait_send()
        self.core(False).wait_recv()
        self.keep().wait()

        @pl.when(self.inner())
        def _():
            self.cross(True).wait_send()
            self.cross(False).wait_recv()

        @pl.when(jnp.logical_not(self.inner()))
        def _():
            for copy in self.empty():
                copy.wait()


def pack_kernel(wqkv_ref, wproj_ref, small_ref, relr_ref, relc_ref, w1_ref, w2t_ref, block_ref, ff_ref):
    rows, wide = wqkv_ref.shape
    block_ref[:rows, :wide] = wqkv_ref[...]
    block_ref[:rows, wide:] = wproj_ref[...]
    parts = [ref[...] for ref in (small_ref, relr_ref, relc_ref)]
    rest = block_ref.shape[1] - sum(part.shape[1] for part in parts)
    block_ref[rows:] = jnp.concatenate(parts + [jnp.zeros((small_ref.shape[0], rest), BF16)], axis=1)
    inner = w1_ref.shape[1]
    ff_ref[:, :inner] = w1_ref[...]
    ff_ref[:, inner:] = w2t_ref[...]


def pack(wqkv, wproj, small, relr, relc, w1, w2t):
    rows = wqkv.shape[0]
    return pl.pallas_call(
        pack_kernel,
        out_shape=[
            jax.ShapeDtypeStruct((rows + small.shape[0], wqkv.shape[1] + wproj.shape[1]), BF16),
            jax.ShapeDtypeStruct((rows, 2 * w1.shape[1]), BF16),
        ],
        cost_estimate=pl.CostEstimate(flops=0, bytes_accessed=1_000_000, transcendentals=0),
    )(wqkv, wproj, small, relr, relc, w1, w2t)


def entry_kernel(
    block_ref, x_ref, g_ref, all_ref, xext_ref, gext_ref, zero_ref, xin_ref, gin_ref, lsems, gsems, xsems, esems,
):
    loads = [pltpu.make_async_copy(x_ref, xin_ref, lsems.at[0]), pltpu.make_async_copy(g_ref, gin_ref, lsems.at[1])]
    for load in loads:
        load.start()
    zero_ref[...] = jnp.zeros_like(zero_ref)
    edges = [Edges(xin_ref, xext_ref, zero_ref, xsems), Edges(gin_ref, gext_ref, zero_ref, esems)]
    greet()
    gather = Gather(block_ref, all_ref, gsems)
    gather.begin()

    def next_edges(n):
        loads[n].wait()
        edges[n].start_cross()
        edges[n].start()

    next_edges(0)
    gather.run(lambda: next_edges(1))
    for item in edges:
        item.finish()


def entry(block, x, g):
    sds = jax.ShapeDtypeStruct
    ext = sds((2, x.shape[1] + 2 * HALO, SIDE, D), BF16)
    inside, anywhere = pl.BlockSpec(memory_space=pltpu.VMEM), pl.BlockSpec(memory_space=pl.ANY)
    return pl.pallas_call(
        entry_kernel,
        in_specs=[inside, anywhere, anywhere],
        out_specs=[anywhere] * 3,
        out_shape=[sds((8, 4) + block.shape, BF16), ext, ext],
        scratch_shapes=[
            pltpu.VMEM((HALO, SIDE, D), BF16), pltpu.VMEM(x.shape, BF16), pltpu.VMEM(x.shape, BF16),
            pltpu.SemaphoreType.DMA((2,)), pltpu.SemaphoreType.DMA((2, 32)), pltpu.SemaphoreType.DMA((7,)),
            pltpu.SemaphoreType.DMA((7,)),
        ],
        compiler_params=pltpu.CompilerParams(vmem_limit_bytes=VMEM_LIMIT, collective_id=3, has_side_effects=True),
    )(block, x, g)


def attn_bwd_kernel(
    meta_ref, qkv_ref, p_ref, inv_ref, att_ref, datt_ref, table_ref, kback_ref, *rest,
):
    w = pl.program_id(0)
    if len(rest) == 3:
        dqkv_ref, rel_ref, bias_ref = rest
        streams = None
    else:
        fc1_ref, fc2_ref, dqkv_ref, rel_ref, bias_ref, part_ref, sum2_ref = rest[:7]
        half = SHARD_ROWS // 2
        streams = []
        for n in range(4):
            own, *got, sems = rest[7 + 7 * n : 14 + 7 * n]
            source = wide_source(fc2_ref if n < 2 else fc1_ref, n % 2)
            streams.append(Halving(source, own, got, sems, ORDERS[n % 2], half))
        ones, twos = streams[:2], streams[2:]
        timeline(
            w,
            {
                0: [greet, each(streams, "first")],
                2: [each(ones, "first_done"), each(ones, "step", 0), each(twos, "first_done")],
                5: [each(ones, "step_done", 0), each(ones, "step", 1), each(twos, "step", 0)],
                7: [each(ones, "step_done", 1), each(ones, "step", 2)],
                11: [each(twos, "step_done", 0), each(twos, "step", 1), each(ones, "step_done", 2), each(ones, "step", 3)],
            },
        )

    @pl.when(w == 0)
    def _():
        rel_ref[...] = jnp.zeros_like(rel_ref)
        bias_ref[...] = jnp.zeros_like(bias_ref)

    lane = iota((TW, LANES), 1)
    low_half = lane < 64
    onehot = kback_ref[...]
    for p in range(PAIRS):
        q = qkv_ref[:, LANES * p : LANES * p + LANES]
        k8 = qkv_ref[:, D + LANES * p : D + LANES * p + LANES]
        v = qkv_ref[:, 2 * D + LANES * p : 2 * D + LANES * p + LANES]
        cols = slice(LANES * p, LANES * p + LANES)
        da = datt_ref[:, cols].astype(F32) * inv_ref[:, cols]
        da_low = da.astype(BF16)
        prod = da_low.astype(F32) * att_ref[:, cols].astype(F32)
        keys = jnp.concatenate([k8, onehot], axis=1)
        da_t = da.T.astype(BF16)
        q_t = q.astype(F32).T.astype(BF16)
        zero = jnp.zeros_like(v)
        dqx, dv_t, dk_t = [], [], []
        dps, dss = [], []
        for h in range(2):
            mine = low_half if h == 0 else ~low_half
            dps.append(mm_nt(da_low, jnp.where(mine, v, zero)))
        for h in range(2):
            mine = low_half if h == 0 else ~low_half
            centre = jnp.sum(jnp.where(mine, prod, 0.0), axis=-1, keepdims=True)
            e = p_ref[2 * p + h]
            dss.append((e.astype(F32) * (dps[h] - centre)).astype(BF16))
        for h in range(2):
            dqx.append(mm(dss[h], keys))
            dv_t.append(mm(da_t[64 * h : 64 * h + 64], p_ref[2 * p + h]))
            dk_t.append(mm(q_t[64 * h : 64 * h + 64], dss[h]))
        dq = jnp.where(low_half, dqx[0][:, :LANES], dqx[1][:, :LANES])
        drc = jnp.where(low_half, dqx[0][:, LANES:], dqx[1][:, LANES:])
        part = lane & 63
        rows = roll_rows(jnp.where(part < 16, drc, 0.0), False)
        cols_part = roll_cols(jnp.where((part >= 16) & (part < 32), drc, 0.0), LANES - 16)
        skew = jnp.concatenate([rows, cols_part], axis=1).astype(BF16)
        dq = dq + mm_nt(skew, table_ref[...])
        rel_ref[...] += mm(q_t, skew)
        dv = jnp.concatenate(dv_t, axis=0).T
        dk = (jnp.concatenate(dk_t, axis=0) * 0.125).T
        dqkv_ref[:, cols] = dq.astype(BF16)
        dqkv_ref[:, D + LANES * p : D + LANES * p + LANES] = dk.astype(BF16)
        dqkv_ref[:, 2 * D + LANES * p : 2 * D + LANES * p + LANES] = dv.astype(BF16)
        bias_ref[0, :, cols] += fold8(dq)
        bias_ref[1, :, cols] += fold8(dv)

    if streams:
        @pl.when(w == pl.num_programs(0) - 1)
        def _():
            each(ones, "step_done", 3)()
            sum2_ref[:half] = ones[0].result()
            sum2_ref[half:] = ones[1].result()
            each(twos, "step_done", 1)()
            for n, stream in enumerate(twos):
                part_ref[n] = stream.own[stream.at["x"], :, :, stream.at["y"]]


def attention_backward(meta, qkv, p, inv, att, datt, table, kback, beside=()):
    cap = meta.shape[0]
    sds = jax.ShapeDtypeStruct
    anywhere = pl.BlockSpec(memory_space=pl.ANY)
    shard = (SHARD_ROWS, SHARD_COLS)
    more_specs, more_outs, scratch, extra = [], [], [], {}
    if beside:
        part = (2, 2, 2, SHARD_ROWS // 2, SHARD_COLS)
        more_specs = [whole(part), whole(shard)]
        more_outs = [sds(part, BF16), sds(shard, F32)]
        scratch = Halving.scratch(SHARD_ROWS // 2) * 4
        extra = dict(collective_id=1, has_side_effects=True)
    return pl.pallas_call(
        attn_bwd_kernel,
        grid_spec=pltpu.PrefetchScalarGridSpec(
            num_scalar_prefetch=1,
            grid=(cap,),
            in_specs=[
                per_window(TW, 3 * D), per_window(HEADS, TW, TW), per_window(TW, D), per_window(TW, D),
                per_window(TW, D), whole((LANES, 256)), whole((TW, LANES)),
            ] + [anywhere] * len(beside),
            out_specs=[per_window(TW, 3 * D), whole((LANES, 256)), whole((2, 8, D))] + more_specs,
            scratch_shapes=scratch,
        ),
        out_shape=[sds((cap, TW, 3 * D), BF16), sds((LANES, 256), F32), sds((2, 8, D), F32)] + more_outs,
        compiler_params=pltpu.CompilerParams(vmem_limit_bytes=VMEM_LIMIT, **extra),
        cost_estimate=pl.CostEstimate(flops=60_000_000_000, bytes_accessed=80_000_000, transcendentals=0),
    )(meta, qkv, p, inv, att, datt, table, kback, *beside)


def rel_from(acc):
    def one(block):
        own = block[:64, :32] + block[64:, 64:96]
        return own[:, :RELS].T

    return one(acc[:, :LANES]), one(acc[:, LANES:])


def put_window(target, y, acc_ref, row0):
    picks = jnp.where(iota((TW, 256), 1) == target, 1.0, 0.0).astype(BF16)
    for q in range(4):
        n = 4 if q < 3 else 2
        t = slice(64 * q, 64 * q + STRIDE * n)
        part = lax.dot_general(
            picks[t, : 64 * n], y[t], (((0,), (0,)), ((), ())), preferred_element_type=F32
        )
        acc_ref[pl.ds(row0 + 4 * q, n)] += part.reshape(n, SIDE, D).astype(acc_ref.dtype)


def scatter_kernel(meta_ref, y_ref, ext_ref, acc_ref):
    w = pl.program_id(0)

    @pl.when(w == 0)
    def _():
        acc_ref[...] = jnp.zeros_like(acc_ref)

    put_window(token_target(meta_ref, w), y_ref[...], acc_ref, meta_ref[w, 0])

    @pl.when(w == pl.num_programs(0) - 1)
    def _():
        def copy(i, _):
            ext_ref[i] = acc_ref[i].astype(BF16)
            return 0
        lax.fori_loop(0, ext_ref.shape[0], copy, 0)


def scatter(meta, y, ext_rows):
    cap = meta.shape[0]
    return pl.pallas_call(
        scatter_kernel,
        grid_spec=pltpu.PrefetchScalarGridSpec(
            num_scalar_prefetch=1,
            grid=(cap,),
            in_specs=[per_window(TW, D)],
            out_specs=whole((ext_rows, SIDE, D)),
            scratch_shapes=[pltpu.VMEM((ext_rows, SIDE, D), F32)],
        ),
        out_shape=jax.ShapeDtypeStruct((ext_rows, SIDE, D), BF16),
        compiler_params=pltpu.CompilerParams(vmem_limit_bytes=VMEM_LIMIT),
        cost_estimate=pl.CostEstimate(flops=5_000_000_000, bytes_accessed=20_000_000, transcendentals=0),
    )(meta, y)


def last_kernel(
    meta_ref, dqkv_ref, wqkv_ref, x_ref, dmix_ref, gain_ref, ext_ref, sums_ref, acc_ref,
):
    w = pl.program_id(0)

    @pl.when(w == 0)
    def _():
        acc_ref[...] = jnp.zeros_like(acc_ref)
        sums_ref[...] = jnp.zeros_like(sums_ref)

    target = token_target(meta_ref, w)
    dn = jnp.zeros((TW, D), F32)
    for c in range(3):
        cols = slice(D * c, D * c + D)
        dn = dn + mm_nt(dqkv_ref[:, cols], wqkv_ref[:, cols])
    dn = jnp.where(target >= 0, dn, 0.0)
    unit, inverse = norm(x_ref[...].astype(F32))
    sums_ref[0] += fold8(dn * unit)
    sums_ref[1] += fold8(dn)
    grad = dmix_ref[...].astype(F32) + norm_back(dn, unit, inverse, gain_ref[0:1])
    put_window(target, grad.astype(BF16), acc_ref, meta_ref[w, 0])

    @pl.when(w == pl.num_programs(0) - 1)
    def _():
        def copy(i, _):
            ext_ref[i] = acc_ref[i].astype(BF16)
            return 0
        lax.fori_loop(0, ext_ref.shape[0], copy, 0)


def last_norm(meta, dqkv, wqkv, x, dmix, gain, ext_rows):
    cap = meta.shape[0]
    sds = jax.ShapeDtypeStruct
    return pl.pallas_call(
        last_kernel,
        grid_spec=pltpu.PrefetchScalarGridSpec(
            num_scalar_prefetch=1,
            grid=(cap,),
            in_specs=[
                per_window(TW, 3 * D), whole((D, 3 * D)), per_window(TW, D), per_window(TW, D), whole((8, D)),
            ],
            out_specs=[whole((ext_rows, SIDE, D)), whole((2, 8, D))],
            scratch_shapes=[pltpu.VMEM((ext_rows, SIDE, D), F32)],
        ),
        out_shape=[sds((ext_rows, SIDE, D), BF16), sds((2, 8, D), F32)],
        compiler_params=pltpu.CompilerParams(vmem_limit_bytes=VMEM_LIMIT),
        cost_estimate=pl.CostEstimate(flops=15_000_000_000, bytes_accessed=30_000_000, transcendentals=0),
    )(meta, dqkv, wqkv, x, dmix, gain)


class SmallSum:
    def __init__(self, mine, got_band, got_img, sems, part):
        self.mine, self.got, self.sems, self.part = mine, (got_band, got_img), sems, part

    @staticmethod
    def scratch(shape, part):
        return [
            pltpu.VMEM(shape, F32), pltpu.VMEM((3,) + shape, F32), pltpu.VMEM((7,) + part, F32),
            pltpu.SemaphoreType.DMA((2, 2, 7)),
        ]

    def copies(self, k):
        return [
            pltpu.make_async_remote_copy(
                src_ref=self.part(device[0]) if k else self.mine, dst_ref=self.got[k].at[d],
                send_sem=self.sems.at[k, 0, d], recv_sem=self.sems.at[k, 1, d], device_id=device, device_id_type=MESH,
            )
            for d, device in enumerate(peers()[k])
        ]

    def send(self, k):
        for copy in self.copies(k):
            copy.start()

    def add(self):
        for copy in self.copies(0):
            copy.wait()
        self.mine[...] = self.mine[...] + self.got[0][0] + self.got[0][1] + self.got[0][2]

    def result(self):
        for copy in self.copies(1):
            copy.wait()
        total = self.part(lax.axis_index("img"))[...]
        for d in range(7):
            total = total + self.got[1][d]
        return total


def deal(rows_ref, parts_ref, rows, wide):
    groups = parts_ref.shape[0]
    share = D // groups
    for i in range(groups):
        parts_ref[i, :rows, :share] = rows_ref[:rows, share * i : share * i + share]
        for k in range(wide):
            at = share * (wide * i + k)
            parts_ref[i, rows + k : rows + k + 1, :share] = rows_ref[rows + at // D : rows + at // D + 1, at % D : at % D + share]


HOME_ROWS = 8


def home_kernel(
    table_ref, own_ref, core_ref, cross_ref, grad_ref, total_ref, ln_ref, rel_ref, q_ref,
    output_ref, input_grad_ref, vec_refs, b1_ref, relr_ref, relc_ref, wq_ref, wp_ref,
    out_ref, sems,
):
    step = pl.program_id(0)
    per_image = pl.num_programs(0) // 2
    m = step // per_image
    top, left = table_ref[m, 25], table_ref[m, 26]
    first = table_ref[m, 27] + (step - m * per_image) * HOME_ROWS

    @pl.when(step == 0)
    def _():
        cap = own_ref.shape[0]
        loads = [
            pltpu.make_async_copy(ref, out_ref.at[pl.ds(at, ref.shape[0])], sems.at[n])
            for n, (ref, at) in enumerate(((own_ref, 0), (core_ref, cap), (cross_ref, cap + NEAR_CORE)))
        ]
        for load in loads:
            load.start()
        share = vec_refs[0].shape[1]
        ln, total = ln_ref[:, :share], total_ref[:, :share]
        for ref, row in zip(vec_refs, (ln[0:1], ln[1:2], total[0:1], total[1:2], total[5:6], total[3:4], total[4:5], total[2:3])):
            ref[...] = row
        b1_ref[...] = jnp.concatenate([total[6 + k : 7 + k] for k in range(4)], axis=1)
        relr_ref[...] = rel_ref[:, :RELS]
        relc_ref[...] = rel_ref[:, LANES : LANES + RELS]
        wq_ref[...] = q_ref[:, : 3 * share]
        wp_ref[...] = q_ref[:, 3 * share :]
        for load in loads:
            load.wait()

    col = iota((SIDE, GRID * STRIDE), 0) + left
    spot = iota((SIDE, GRID * STRIDE), 1)
    picks = jnp.where((spot >> 4) * WIN + (spot & 15) == col, 1.0, 0.0)
    picks = jnp.where((spot & 15) < WIN, picks, 0.0).astype(BF16)
    for i in range(HOME_ROWS):
        at = i + first + top
        r = at // WIN
        a = pl.multiple_of((at - r * WIN) * STRIDE, STRIDE)
        slots = [table_ref[m, r * GRID + c] for c in range(GRID)]
        for source, target in ((out_ref, output_ref), (grad_ref, input_grad_ref)):
            tokens = jnp.concatenate([source[slot, pl.ds(a, STRIDE)] for slot in slots], axis=0)
            target[0, i] = mm(picks, tokens).astype(target.dtype)


def home(table, sources, rows):
    per_image = rows // HOME_ROWS
    sds = jax.ShapeDtypeStruct
    tiled = pl.BlockSpec((1, HOME_ROWS, SIDE, D), lambda w, meta: (w // per_image, w % per_image, 0, 0))
    shapes = [[(1, D // 8)] * 8, (1, FF // 8)] + [(HEAD // 4, RELS)] * 2 + [
        (SHARD_ROWS, 3 * D // 8), (SHARD_ROWS, D // 8),
    ]
    is_shape = lambda shape: isinstance(shape, tuple)
    return pl.pallas_call(
        home_kernel,
        grid_spec=pltpu.PrefetchScalarGridSpec(
            num_scalar_prefetch=1,
            grid=(2 * per_image,),
            in_specs=[pl.BlockSpec(memory_space=pl.ANY)] * 3 + [whole(a.shape) for a in sources[3:]],
            scratch_shapes=[pltpu.VMEM(sources[3].shape, BF16), pltpu.SemaphoreType.DMA((3,))],
            out_specs=[tiled, tiled] + jax.tree.map(whole, shapes, is_leaf=is_shape),
        ),
        out_shape=[sds((2, rows, SIDE, D), BF16), sds((2, rows, SIDE, D), F32)]
        + jax.tree.map(lambda shape: sds(shape, F32), shapes, is_leaf=is_shape),
        compiler_params=pltpu.CompilerParams(vmem_limit_bytes=VMEM_LIMIT),
        cost_estimate=pl.CostEstimate(flops=500_000_000, bytes_accessed=20_000_000, transcendentals=0),
    )(table, *sources)


def home_table(plan, offsets, band, band_rows):
    own = np.full((4, 2, WINDOWS), 0, np.int32)
    for b in range(4):
        for slot, (m, w) in enumerate(plan[b]):
            if w >= 0:
                own[b, m, w] = slot
        odd, cap = b % 2, len(plan[b])
        mate = plan[b ^ 1]
        sent = mate[:3] if (b ^ 1) in (0, 3) else mate[NEAR_CROSS : NEAR_CROSS + NEAR_CORE]
        for slot, (m, w) in enumerate(sent):
            own[b, m, w] = cap + slot
        if b in (1, 2):
            for slot, (m, w) in enumerate(plan[3 - b][:NEAR_CROSS]):
                own[b, m, w] = cap + NEAR_CORE + slot
    rows = jnp.asarray(own)[band]
    first = jnp.full((2, 1), band_rows, jnp.int32) * band
    return jnp.concatenate([rows, offsets.astype(jnp.int32), first, jnp.zeros((2, 4), jnp.int32)], axis=1)


def last_fused_kernel(
    meta_ref, dqkv_ref, wqkv_ref, x_ref, dmix_ref, gain_ref, dwq_ref, dwp_ref, bias_ref, sums_ref, fc1_ref, rel_ref,
    all_ref, shard_ref, total_ref, rels_ref, ln_ref,
    grad_ref, ln_acc, q_ref, *rest,
):
    w = pl.program_id(0)
    end = pl.num_programs(0) - 1
    half = SHARD_ROWS // 2
    streams = []
    for n, order in enumerate(ORDERS):
        own, *got, sems = rest[7 * n : 7 * n + 7]

        def source(x, img, c, n=n):
            row = pl.multiple_of((2 * x + c) * SHARD_ROWS + n * half, half)
            return q_ref.at[img, pl.ds(row, half)]

        streams.append(Halving(source, own, got, sems, order, half))
    rest = rest[14:]
    small_parts, ln_parts = rest[12:14]
    features = HEAD // 4
    own_features = pl.ds(pl.multiple_of(lax.axis_index("band") * features, features), features)
    small = SmallSum(*rest[:4], lambda i: small_parts.at[i])
    rel = SmallSum(*rest[4:8], lambda i: rest[4].at[own_features])
    ln = SmallSum(*rest[8:12], lambda i: ln_parts.at[i])
    back = Homeward(grad_ref, all_ref, rest[14])

    def start():
        groups = q_ref.shape[0]
        wide, share = 3 * D // groups, D // groups
        for i in range(groups):
            q_ref[i] = jnp.concatenate(
                [dwq_ref[:, wide * i : wide * i + wide], dwp_ref[:, share * i : share * i + share]], axis=1
            )
        greet()
        each(streams, "first")()

    def prepare():
        for r in range(2):
            small.mine[r : r + 1] = jnp.sum(bias_ref[r], axis=0, keepdims=True)
        for r in range(4):
            small.mine[2 + r : 3 + r] = jnp.sum(sums_ref[r], axis=0, keepdims=True)
            small.mine[6 + r : 7 + r] = jnp.sum(fc1_ref[:, D * r : D * r + D], axis=0, keepdims=True)
        small.mine[10:] = jnp.zeros((6, D), F32)
        small_parts[...] = jnp.zeros_like(small_parts)
        ln_parts[...] = jnp.zeros_like(ln_parts)
        rel.mine[...] = rel_ref[:64] + pltpu.roll(rel_ref[64:], 192, 1)
        small.send(0)
        rel.send(0)
        ln_acc[...] = jnp.zeros_like(ln_acc)

    def middle():
        small.add()
        rel.add()
        deal(small.mine, small_parts, 6, 4)
        small.send(1)
        rel.send(1)

    def finish():
        total_ref[...] = small.result()
        rels_ref[...] = rel.result()

    timeline(
        w,
        {
            0: [start, prepare],
            2: [each(streams, "first_done"), each(streams, "step", 0)],
            3: [middle, back.send_core_outer],
            6: [each(streams, "step_done", 0), each(streams, "step", 1), finish],
            8: [each(streams, "step_done", 1), each(streams, "step", 2), back.send_cross],
            12: [each(streams, "step_done", 2), each(streams, "step", 3), back.send_core_inner],
        },
    )

    target = token_target(meta_ref, w)
    dn = jnp.zeros((TW, D), F32)
    for c in range(3):
        cols = slice(D * c, D * c + D)
        dn = dn + mm_nt(dqkv_ref[:, cols], wqkv_ref[:, cols])
    dn = jnp.where(target >= 0, dn, 0.0)
    unit, inverse = norm(x_ref[...].astype(F32))
    ln_acc[0] += fold8(dn * unit)
    ln_acc[1] += fold8(dn)
    grad = dmix_ref[...].astype(F32) + norm_back(dn, unit, inverse, gain_ref[0:1])
    grad_ref[w] = grad.astype(BF16)

    @pl.when(w == end)
    def _():
        back.keep().start()
        ln.mine[0:1] = jnp.sum(ln_acc[0], axis=0, keepdims=True)
        ln.mine[1:2] = jnp.sum(ln_acc[1], axis=0, keepdims=True)
        ln.mine[2:] = jnp.zeros((6, D), F32)
        ln.send(0)
        each(streams, "step_done", 3)()
        ln.add()
        deal(ln.mine, ln_parts, 2, 0)
        ln.send(1)
        for n, stream in enumerate(streams):
            shard_ref[half * n : half * n + half] = stream.result()
        back.keep().wait()
        back.finish()
        ln_ref[...] = ln.result()


def last_fused(meta, dqkv, wqkv, x, dmix, gain, dwq, dwp, bias_sums, sums, fc1_sum, rel_acc):
    cap = meta.shape[0]
    sds = jax.ShapeDtypeStruct
    half = SHARD_ROWS // 2
    anywhere = pl.BlockSpec(memory_space=pl.ANY)
    sums_out = [((SHARD_ROWS, SHARD_COLS), F32), ((16, LANES), F32), ((HEAD // 4, 256), F32), ((8, LANES), F32)]
    return pl.pallas_call(
        last_fused_kernel,
        grid_spec=pltpu.PrefetchScalarGridSpec(
            num_scalar_prefetch=1,
            grid=(cap,),
            in_specs=[
                per_window(TW, 3 * D), whole((D, 3 * D)), per_window(TW, D), per_window(TW, D), whole((8, D)),
                whole((D, 3 * D)), whole((D, D)), whole((2, 8, D)), whole((4, 8, D)), whole((8, FF)), whole((LANES, 256)),
            ],
            out_specs=[anywhere] + [whole(shape) for shape, _ in sums_out],
            scratch_shapes=[
                pltpu.VMEM((cap, TW, D), BF16), pltpu.VMEM((2, 8, D), F32), pltpu.VMEM((8, D, SHARD_COLS), BF16)
            ]
            + Halving.scratch(half) * 2
            + SmallSum.scratch((16, D), (16, LANES)) + SmallSum.scratch((HEAD, 256), (HEAD // 4, 256))
            + SmallSum.scratch((8, D), (8, LANES))
            + [pltpu.VMEM((8, 16, LANES), F32), pltpu.VMEM((8, 8, LANES), F32), pltpu.SemaphoreType.DMA((5,))],
        ),
        out_shape=[sds((cap + NEAR_CORE + NEAR_CROSS, TW, D), BF16)] + [sds(shape, dtype) for shape, dtype in sums_out],
        compiler_params=pltpu.CompilerParams(vmem_limit_bytes=VMEM_LIMIT, collective_id=2, has_side_effects=True),
        cost_estimate=pl.CostEstimate(flops=20_000_000_000, bytes_accessed=50_000_000, transcendentals=0),
    )(meta, dqkv, wqkv, x, dmix, gain, dwq, dwp, bias_sums, sums, fc1_sum, rel_acc)


def window_plan(images, bands):
    lists = [[] for _ in range(bands)]
    if images == 2 and bands == 4:
        spans = (
            ((0, 5, 8), (0, 0, 5), (1, 0, 5)),
            ((0, 10, 15), (0, 8, 10), (1, 5, 10)),
            ((1, 10, 15), (1, 15, 17), (0, 15, 20)),
            ((1, 17, 20), (1, 20, 25), (0, 20, 25)),
        )
        lists = [[(m, w) for m, first, last in row for w in range(first, last)] for row in spans]
    else:
        cuts = [
            [(WINDOWS * b + (bands - 1 if m % 2 else 0)) // bands for b in range(bands + 1)] for m in range(images)
        ]
        for m in range(images):
            for b in range(bands):
                lists[b] += [(m, w) for w in range(cuts[m][b], min(cuts[m][b + 1], WINDOWS))]
    cap = max(len(item) for item in lists)
    return np.array([item + [(0, -1)] * (cap - len(item)) for item in lists], np.int32)


HALO = 12


def near(images, bands, band_rows):
    return images == 2 and bands == 4 and band_rows == 16


CORE = [(0, 1), (1, 0), (2, 3), (3, 2)]
CROSS = [(1, 2), (2, 1)]


def extend(rows, band):
    images, band_rows = rows.shape[:2]
    if not near(images, lax.axis_size("band"), band_rows):
        full = lax.all_gather(rows, "band", axis=1, tiled=True)
        return jnp.pad(full, ((0, 0), (6, 6), (0, 0), (0, 0)))
    odd = band % 2 == 1
    top, bottom = rows[:, :HALO], rows[:, -HALO:]
    from_core = lax.ppermute(jnp.where(odd, top, bottom), "band", CORE)
    from_cross = lax.ppermute(jnp.where(odd, bottom[1], top[0]), "band", CROSS)
    zero = jnp.zeros_like(from_cross)
    above = jnp.where(odd, from_core, jnp.stack([zero, from_cross]))
    below = jnp.where(odd, jnp.stack([from_cross, zero]), from_core)
    return jnp.concatenate([above, rows, below], axis=1)


def collect(ext, band, images, band_rows):
    if not near(images, lax.axis_size("band"), band_rows):
        return lax.psum_scatter(ext[:, 6:-6], "band", scatter_dimension=1, tiled=True).astype(F32)
    odd = band % 2 == 1
    above, below = ext[:, :HALO], ext[:, -HALO:]
    from_core = lax.ppermute(jnp.where(odd, above, below), "band", CORE).astype(F32)
    from_cross = lax.ppermute(jnp.where(odd, below[0], above[1]), "band", CROSS).astype(F32)
    zero = jnp.zeros_like(from_cross)
    top = jnp.where(odd, from_core, jnp.stack([from_cross, zero]))
    bottom = jnp.where(odd, jnp.stack([zero, from_cross]), from_core)
    own = ext[:, HALO:-HALO].astype(F32)
    rest = band_rows - HALO
    return own + jnp.pad(top, ((0, 0), (0, rest), (0, 0), (0, 0))) + jnp.pad(bottom, ((0, 0), (rest, 0), (0, 0), (0, 0)))


def shards(
    image_tokens, pad_offsets, ln1_gain, ln1_bias, w_qkv, q_bias, v_bias, rel_rows, rel_cols, w_proj, proj_bias,
    ln2_gain, ln2_bias, w_fc1, fc1_bias, w_fc2, fc2_bias, out_grad,
):
    images, band_rows = image_tokens.shape[:2]
    bands, groups = lax.axis_size("band"), lax.axis_size("img")
    band, group = lax.axis_index("band"), lax.axis_index("img")
    axes = ("img", "band")

    part, wide = w_qkv.shape
    close = near(images, bands, band_rows)
    fused = close and groups == 8
    share = D // groups
    vector_rows = [ln1_gain, ln1_bias, q_bias, v_bias, proj_bias, ln2_gain, ln2_bias, fc2_bias]
    small = jnp.concatenate([v[None] for v in vector_rows] + [fc1_bias.reshape(4, share), jnp.zeros((4, share), BF16)])
    block_cols = wide + w_proj.shape[1]
    small_rows = 16
    if fused:
        block, ff_block = pack(w_qkv, w_proj, small, rel_rows.T, rel_cols.T, w_fc1, w_fc2.T)
        first, ext, gext = entry(block, image_tokens, out_grad)
    else:
        features = rel_rows.shape[1]
        rest = jnp.zeros((small_rows, block_cols - share - 2 * RELS), BF16)
        tables = [jnp.pad(rel.T, ((0, small_rows - features), (0, 0))) for rel in (rel_rows, rel_cols)]
        block = jnp.concatenate(
            [jnp.concatenate([w_qkv, w_proj], axis=1), jnp.concatenate([small, *tables, rest], axis=1)], axis=0
        )
        ff_block = jnp.concatenate([w_fc1, w_fc2.T], axis=1)
        first = lax.all_gather(block, axes, axis=0, tiled=False).reshape(groups, bands, part + small_rows, block_cols)
        ext, gext = extend(image_tokens, band), extend(out_grad, band)
    ff = lax.all_gather(ff_block, axes, axis=0, tiled=False).reshape(groups, bands * part, -1)
    tail = first[:, :, part:]
    vectors = tail[:, 0, :8, :share].transpose(1, 0, 2).reshape(8, D).astype(F32)
    fc1_shift = tail[:, 0, 8:12, :share].reshape(1, FF).astype(F32)
    features = HEAD // bands
    rels = [tail[0, :, :features, at : at + RELS].reshape(HEAD, RELS) for at in (share, share + RELS)]
    plan = jnp.asarray(window_plan(images, bands))[band]
    image, window = plan[:, 0], plan[:, 1]
    ext_per = band_rows + 2 * HALO if close else bands * band_rows + 12
    base = band_rows * band - HALO if close else -6
    live = window >= 0
    spot = jnp.maximum(window, 0)
    offsets = pad_offsets[image]
    row = spot // GRID * WIN - offsets[:, 0]
    col = spot % GRID * WIN - offsets[:, 1]
    meta = jnp.stack(
        [jnp.where(live, image * ext_per + row - base, HALO), col, row, live.astype(jnp.int32)], axis=1
    ).astype(jnp.int32)
    cap = meta.shape[0]
    ext_rows = images * ext_per

    ka, kb, kback = key_constants()
    ext, gext = ext.reshape(ext_rows, SIDE, D), gext.reshape(ext_rows, SIDE, D)
    if not fused:
        weights = first[:, :, :part].transpose(1, 2, 0, 3)
        wqkv, wproj = weights[..., :wide].reshape(D, 3 * D), weights[..., wide:].reshape(D, D)
    x, g, normed1, qkv, probs, inv, att, *weights = attention_forward(
        meta, ext, gext, vectors, first if fused else wqkv, rel_table(rels[0], rels[1], True), ka, kb
    )
    if fused:
        wqkv, wproj = weights
    out_win, normed2, act, d_pre, d_mixed, d_att, sums, sum_fc1 = feed_forward(
        g, x, att, wproj, vectors, ff, fc1_shift, 0
    )

    def flat(a):
        return a.reshape(-1, a.shape[-1])

    def weight_grad(left, right):
        return jnp.einsum("td,te->de", flat(left), flat(right), preferred_element_type=F32).astype(BF16)

    if fused:
        inner = (band == 1) | (band == 2)
        to_core = lax.dynamic_slice_in_dim(out_win, jnp.where(inner, NEAR_CROSS, 0), NEAR_CORE, 0)
        core_out = lax.ppermute(to_core, "band", CORE)
        cross_out = lax.ppermute(out_win[:NEAR_CROSS], "band", CROSS)
    d_fc2 = weight_grad(g, act)
    d_fc1 = weight_grad(normed2, d_pre)
    d_proj = weight_grad(att, d_mixed)
    if fused:
        d_fc1, d_fc2, core_out, cross_out = lax.optimization_barrier((d_fc1, d_fc2, core_out, cross_out))
    d_qkv, rel_acc, bias_sums, *done = attention_backward(
        meta, qkv, probs, inv, att, d_att, rel_table(rels[0], rels[1], False), kback,
        (d_fc1, d_fc2) if fused else (),
    )
    d_wqkv = weight_grad(normed1, d_qkv)

    if fused:
        partial, g_fc2 = done

        def fold(value, axis, bit, step):
            mine = lax.dynamic_index_in_dim(value, bit, axis, keepdims=False)
            other = lax.dynamic_index_in_dim(value, 1 - bit, axis, keepdims=False)
            came = lax.ppermute(other, "img", [(i, i ^ step) for i in range(groups)])
            return mine.astype(F32) + came.astype(F32)

        partial = fold(partial, 1, group // 4, 4).astype(BF16)
        g_fc1 = fold(partial, 1, group // 2 % 2, 2).reshape(part, FF // groups)
        all_grad, q_shard, total, rel_total, ln_total = last_fused(
            meta, d_qkv, wqkv, x, d_mixed, vectors, d_wqkv, d_proj, bias_sums, sums, sum_fc1, rel_acc
        )
        output, input_grad, shares, b1_share, d_rel_rows, d_rel_cols, g_qkv, g_proj = home(
            home_table(window_plan(images, bands), pad_offsets, band, band_rows),
            (out_win, core_out, cross_out, all_grad, total, ln_total, rel_total, q_shard), band_rows,
        )
        ln1g, ln1b, qb, vb, pb, ln2g, ln2b, b2 = [share.reshape(-1) for share in shares]
        return (
            output, input_grad, ln1g, ln1b, g_qkv, qb, vb, d_rel_rows.T, d_rel_cols.T, g_proj, pb, ln2g, ln2b, g_fc1,
            b1_share.reshape(-1), g_fc2.T, b2,
        )
    else:
        out_ext = scatter(meta, out_win, ext_rows).reshape(images, ext_per, SIDE, D)
        output = collect(out_ext, band, images, band_rows).astype(BF16)
        in_ext, sums1 = last_norm(meta, d_qkv, wqkv, x, d_mixed, vectors, ext_rows)
        input_grad = collect(in_ext.reshape(images, ext_per, SIDE, D), band, images, band_rows)

        def reduce(grad):
            grad = lax.psum_scatter(grad, "img", scatter_dimension=1, tiled=True)
            return lax.psum_scatter(grad, "band", scatter_dimension=0, tiled=True).astype(F32)

        g_fc1, g_fc2, g_qkv, g_proj = reduce(d_fc1), reduce(d_fc2), reduce(d_wqkv), reduce(d_proj)
        ln_total, bias_total, sum_total, fc1_total, d_rel_rows, d_rel_cols = lax.psum(
            (jnp.sum(sums1, 1), jnp.sum(bias_sums, 1), jnp.sum(sums, 1), jnp.sum(sum_fc1, 0)) + rel_from(rel_acc), axes
        )

    def img_share(vector):
        n = vector.shape[0] // groups
        return lax.dynamic_slice_in_dim(vector, group * n, n, 0)

    def band_share(table):
        n = table.shape[1] // bands
        return lax.dynamic_slice_in_dim(table, band * n, n, 1)

    return (
        output,
        input_grad,
        img_share(ln_total[0]),
        img_share(ln_total[1]),
        g_qkv,
        img_share(bias_total[0]),
        img_share(bias_total[1]),
        band_share(d_rel_rows),
        band_share(d_rel_cols),
        g_proj,
        img_share(sum_total[3]),
        img_share(sum_total[1]),
        img_share(sum_total[2]),
        g_fc1,
        img_share(fc1_total),
        g_fc2.T,
        img_share(sum_total[0]),
    )


def solution(mesh):
    tokens, vector, matrix = P("img", "band", None, None), P("img"), P("band", "img")
    table, wide = P(None, "band"), P("img", "band")
    return jax.shard_map(
        shards,
        mesh=mesh,
        in_specs=(
            tokens, P("img", None), vector, vector, matrix, vector, vector, table, table, matrix, vector, vector,
            vector, matrix, vector, wide, vector, tokens,
        ),
        out_specs=(
            tokens, tokens, vector, vector, matrix, vector, vector, table, table, matrix, vector, vector, vector,
            matrix, vector, wide, vector,
        ),
        check_vma=False,
    )
```
